32 devices in a mesh: dp: 8 (over z, y), seq: 4 (over x, core).
Axes of the slice: x: 2, y: 2, z: 4, core: 2. Of those that a mesh axis runs over, the one named last changes fastest.
Arguments:
- tokens: bfloat16 [6144, 1024], P(('dp', 'seq')), may hold values from -6 to 6
- doc_start: int32 [8, 768], P('dp'), may hold values from 0 to 767, as said below
- lexical_ids: int32 [6144], P(('dp', 'seq')), may hold values from 0 to 250001, as said below
- queries: bfloat16 [8, 32, 1024], P('dp'), may hold values from -0.5 to 0.5
- match_index: int32 [8, 32], P('dp'), may hold values from 0 to 767
- query_weight: bfloat16 [2, 1024, 1024], P(None, ('dp', 'seq')), may hold values from -0.25 to 0.25
- query_bias: bfloat16 [2, 1024], P(None, ('dp', 'seq')), may hold values from -3 to 3
- key_weight: bfloat16 [2, 1024, 1024], P(None, ('dp', 'seq')), may hold values from -0.25 to 0.25
- value_weight: bfloat16 [2, 1024, 1024], P(None, ('dp', 'seq')), may hold values from -0.1875 to 0.1875
- value_bias: bfloat16 [2, 1024], P(None, ('dp', 'seq')), may hold values from -3 to 3
- out_weight: bfloat16 [2, 1024, 1024], P(None, ('dp', 'seq')), may hold values from -0.75 to 0.75
- out_bias: bfloat16 [2, 1024], P(None, ('dp', 'seq')), may hold values from -3 to 3
- norm_gain: bfloat16 [2, 1024], P(None, ('dp', 'seq')), may hold values from 0.25 to 1.75
- norm_bias: bfloat16 [2, 1024], P(None, ('dp', 'seq')), may hold values from -3 to 3
- expand_weight: bfloat16 [2, 1024, 4096], P(None, ('dp', 'seq')), may hold values from -0.1875 to 0.1875
- expand_bias: bfloat16 [2, 4096], P(None, ('dp', 'seq')), may hold values from -3 to 3
- shrink_weight: bfloat16 [2, 4096, 1024], P(None, ('dp', 'seq')), may hold values from -0.09375 to 0.09375
- shrink_bias: bfloat16 [2, 1024], P(None, ('dp', 'seq')), may hold values from -3 to 3
- final_gain: bfloat16 [2, 1024], P(None, ('dp', 'seq')), may hold values from 0.25 to 1.75
- final_bias: bfloat16 [2, 1024], P(None, ('dp', 'seq')), may hold values from -3 to 3
- lexical_weight: bfloat16 [1024], replicated, may hold values from -0.1875 to 0.1875
- lexical_bias: bfloat16 [1], replicated, may hold values from -3 to 3
- score_cot: float32 [8, 32], P('dp'), may hold values from -96 to 96
- encoded_cot: bfloat16 [6144, 1024], P(('dp', 'seq')), may hold values from -6 to 6
Outputs:
- encoded: bfloat16 [6144, 1024], P(('dp', 'seq'))
- scores: float32 [8, 32], P('dp')
- lexical_stats: float32 [2], replicated
- tokens_grad: bfloat16 [6144, 1024], P(('dp', 'seq'))
- query_weight_grad: float32 [2, 1024, 1024], P(None, ('dp', 'seq'))
- query_bias_grad: float32 [2, 1024], P(None, ('dp', 'seq'))
- key_weight_grad: float32 [2, 1024, 1024], P(None, ('dp', 'seq'))
- value_weight_grad: float32 [2, 1024, 1024], P(None, ('dp', 'seq'))
- value_bias_grad: float32 [2, 1024], P(None, ('dp', 'seq'))
- out_weight_grad: float32 [2, 1024, 1024], P(None, ('dp', 'seq'))
- out_bias_grad: float32 [2, 1024], P(None, ('dp', 'seq'))
- norm_gain_grad: float32 [2, 1024], P(None, ('dp', 'seq'))
- norm_bias_grad: float32 [2, 1024], P(None, ('dp', 'seq'))
- expand_weight_grad: float32 [2, 1024, 4096], P(None, ('dp', 'seq'))
- expand_bias_grad: float32 [2, 4096], P(None, ('dp', 'seq'))
- shrink_weight_grad: float32 [2, 4096, 1024], P(None, ('dp', 'seq'))
- shrink_bias_grad: float32 [2, 1024], P(None, ('dp', 'seq'))
- final_gain_grad: float32 [2, 1024], P(None, ('dp', 'seq'))
- final_bias_grad: float32 [2, 1024], P(None, ('dp', 'seq'))
The draws below stay inside these ranges and needn't reach their ends.
Inputs may be any that keep to these rules, and one draw needn't show every extreme that they name: `doc_start`: documents are contiguous runs of a group; in every group one document begins before position 48 and ends within the last 49 positions, and the group's last position is a document of one token. `lexical_ids`: ids of a vocabulary of 250002; ids 0 to 3 are special tokens.
All inputs are finite; a program needn't handle non-finite values.
Results may differ from the reference program's by a relative error of at most 0.035.
The reference program's roundings to bfloat16 on the way count: a program that leaves them out, or rounds other values in their place, can miss the bound.
Values may be sent and summed in bfloat16 or wider, within the bound.
No kernel may reach another device: no remote copies, remote signals or barrier semaphores. Data moves between devices by JAX's collectives and lax.ppermute only.
A program may use at most 256 MiB of HBM per device.

```python
import math
import jax
import jax.numpy as jnp
from jax import lax

D = 1024
HEAD = 64
FF = 4096
VOCAB = 250002
LAYERS = 2
QTOK = 32
TOK_DEV = 192
GROUPS = 8
GROUP_TOK = 768
TOKENS = 6144


def draw_doc_start(key, part):
    key = jax.random.fold_in(key, 11)
    key_first, key_last, key_rate, key_cut = jax.random.split(key, 4)
    position = jnp.arange(GROUP_TOK, dtype=jnp.int32)[None, :]
    margin = max(TOK_DEV // 4, 1)
    first_cut = jax.random.randint(key_first, (GROUPS, 1), 0, margin)
    last_cut = jax.random.randint(key_last, (GROUPS, 1), GROUP_TOK - margin - 1, GROUP_TOK - 1)
    rate = jnp.left_shift(jnp.ones((GROUPS, 1), jnp.int32), jax.random.randint(key_rate, (GROUPS, 1), 2, 8))
    coin = jax.random.randint(key_cut, (GROUPS, GROUP_TOK), 0, rate)
    outside = (position < first_cut) | (position >= last_cut)
    cut = (coin == 0) & outside | (position == 0) | (position == first_cut) | (position == last_cut) | (position == GROUP_TOK - 1)
    starts = jnp.where(cut, position, 0)
    return lax.cummax(starts, axis=1).astype(jnp.int32)


def draw_lexical_ids(key, part):
    key = jax.random.fold_in(key, 23)
    key_kind, key_special, key_word = jax.random.split(key, 3)
    position = jnp.arange(TOKENS, dtype=jnp.int32)
    threshold = 100 + 600 * position // TOKENS
    special = jax.random.randint(key_kind, (TOKENS,), 0, 1000) < threshold
    special_ids = jax.random.randint(key_special, (TOKENS,), 0, 4)
    word_ids = jax.random.randint(key_word, (TOKENS,), 4, VOCAB)
    drawn = jnp.where(special, special_ids, word_ids)
    drawn = jnp.where(position == 0, 0, drawn)
    drawn = jnp.where(position == TOKENS - 1, VOCAB - 1, drawn)
    return drawn.astype(jnp.int32)


def draw_score_cot(key, part):
    key = jax.random.fold_in(key, 41)
    key_size = jax.random.fold_in(key, 1)
    base = D / 32.0
    drawn = jax.random.truncated_normal(key_size, -3.0, 3.0, (GROUPS, QTOK), jnp.float32) * base
    return drawn.astype(jnp.float32)


def plant(result, own_key, smallest, top_value):
    longest = result.shape.index(max(result.shape))
    spots = []
    for shift in (0, 1):
        where = [jax.random.randint(jax.random.fold_in(own_key, axis), (), 0, length) for axis, length in enumerate(result.shape)]
        where[longest] = (where[longest] + shift) % result.shape[longest]
        spots.append(tuple(where))
    return result.at[spots[0]].set(smallest).at[spots[1]].set(top_value)


def with_spikes(entries, key, source, target, blocks, factor):
    def block_of(dim):
        return (jnp.arange(entries.shape[dim]) // (entries.shape[dim] // blocks)).reshape((-1,) + (1,) * (entries.ndim - 1 - dim))

    one_side = jax.random.permutation(key, blocks)[block_of(target)]
    second = (block_of(target) + blocks // 2) % blocks
    return jnp.where((block_of(source) == one_side) | (block_of(source) == second), factor * entries, entries)


def level_of(own_key, dims, cuts, smallest, largest):
    def one(dim, shards_of):
        steps = jax.random.uniform(jax.random.fold_in(jax.random.fold_in(own_key, 6), dim), (shards_of,), jnp.float32, smallest / len(cuts), largest / len(cuts))
        return jnp.repeat(jnp.exp(steps), dims[dim] // shards_of).reshape((-1,) + (1,) * (len(dims) - dim - 1))

    factor_of = one(*cuts[0])
    for cut in cuts[1:]:
        factor_of = factor_of * one(*cut)
    return factor_of


def normal_values(stream_key, extent, scale, reach, cuts=(), kind=jnp.bfloat16):
    array = scale * jax.random.normal(stream_key, extent, jnp.float32)
    if cuts:
        array = array * level_of(stream_key, extent, cuts, -0.22, 0.18)
    return jnp.clip(array, -reach, reach).astype(kind)


def gaussian_with(key, shape, scale, bound, cuts, heavy, kind=jnp.bfloat16):
    array = scale * jax.random.normal(key, shape, jnp.float32)
    if cuts:
        array = array * level_of(key, shape, cuts, -0.22, 0.18)
    return jnp.clip(with_spikes(array, jax.random.fold_in(key, 3), *heavy), -bound, bound).astype(kind)


def setup_inputs(seed: int = 0) -> dict:
    keys = jax.random.split(jax.random.key(seed), 25)
    return {
        "tokens": gaussian_with(keys[0], (TOKENS, D), 1.0, 6.0, ((0, 32),), (0, 1, 32, 2.75)),
        "doc_start": draw_doc_start(jax.random.fold_in(keys[24], 71), 0),
        "lexical_ids": draw_lexical_ids(jax.random.fold_in(keys[24], 71), 0),
        "queries": normal_values(keys[3], (GROUPS, QTOK, D), (D ** -0.5), 0.5, ((0, 8),)),
        "match_index": plant(jax.random.randint(keys[4], (GROUPS, QTOK), 0, GROUP_TOK), jax.random.fold_in(keys[4], 1), 0, GROUP_TOK - 1).astype(jnp.int32),
        "query_weight": normal_values(keys[5], (LAYERS, D, D), (D // 2) ** -0.5, 0.25, ((1, 32),)),
        "query_bias": normal_values(keys[6], (LAYERS, D), 0.5, 3.0, ((1, 32),)),
        "key_weight": normal_values(keys[7], (LAYERS, D, D), (D // 2) ** -0.5, 0.25, ((1, 32),)),
        "value_weight": normal_values(keys[8], (LAYERS, D, D), D ** -0.5, 0.1875, ((1, 32),)),
        "value_bias": normal_values(keys[9], (LAYERS, D), 0.5, 3.0, ((1, 32),)),
        "out_weight": normal_values(keys[10], (LAYERS, D, D), (max(D // 16, 1)) ** -0.5, 0.75, ((1, 32),)),
        "out_bias": normal_values(keys[11], (LAYERS, D), 0.5, 3.0, ((1, 32),)),
        "norm_gain": jnp.clip(1.0 + 0.15 * jax.random.normal(keys[12], (LAYERS, D), jnp.float32), 0.25, 1.75).astype(jnp.bfloat16),
        "norm_bias": normal_values(keys[13], (LAYERS, D), 0.5, 3.0, ((1, 32),)),
        "expand_weight": normal_values(keys[14], (LAYERS, D, FF), D ** -0.5, 0.1875, ((1, 32),)),
        "expand_bias": normal_values(keys[15], (LAYERS, FF), 0.5, 3.0, ((1, 32),)),
        "shrink_weight": normal_values(keys[16], (LAYERS, FF, D), FF ** -0.5, 0.09375, ((1, 32),)),
        "shrink_bias": normal_values(keys[17], (LAYERS, D), 0.5, 3.0, ((1, 32),)),
        "final_gain": jnp.clip(1.0 + 0.15 * jax.random.normal(keys[18], (LAYERS, D), jnp.float32), 0.25, 1.75).astype(jnp.bfloat16),
        "final_bias": normal_values(keys[19], (LAYERS, D), 0.5, 3.0, ((1, 32),)),
        "lexical_weight": normal_values(keys[20], (D,), D ** -0.5, 0.1875),
        "lexical_bias": normal_values(keys[21], (1,), 1.0, 3.0),
        "score_cot": draw_score_cot(jax.random.fold_in(keys[24], 71), 0),
        "encoded_cot": gaussian_with(keys[23], (TOKENS, D), 1.0, 6.0, ((0, 32),), (0, 1, 32, 2.75)),
    }


EPSILON = 1e-05
NEGATIVE = -1e+30
HIGHEST = lax.Precision.HIGHEST

@jax.custom_vjp
def low(v):
    return lax.optimization_barrier(v.astype(jnp.bfloat16)).astype(jnp.float32)

@jax.custom_vjp
def low_back(v):
    return v

def low_keep(v):
    return (low(v), None)

def low_pass(kept, grad):
    return (grad,)

def back_keep(v):
    return (v, None)

def back_low(kept, grad):
    return (low(grad),)
low.defvjp(low_keep, low_pass)
low_back.defvjp(back_keep, back_low)

def layer_norm(resid, gain_vec, bias_vec):
    center = resid - lax.optimization_barrier(jnp.mean(resid, axis=-1, keepdims=True))
    spread = lax.optimization_barrier(jnp.mean(center * center, axis=-1, keepdims=True))
    return center * lax.rsqrt(spread + EPSILON) * gain_vec + bias_vec

def product(left, right):
    return jnp.dot(left, right, precision=HIGHEST)

def split_heads(matrix):
    return matrix.reshape(matrix.shape[0], matrix.shape[1] // HEAD, HEAD).transpose(1, 0, 2)

def group_attend(blocks):
    query_rows, key_rows, value_rows, starts = blocks
    same_doc = starts[:, None] == starts[None, :]
    score_scale = 1.0 / math.sqrt(HEAD)

    def one_head(pieces):
        query_head, key_head, value_head = pieces
        head_scores = low_back(score_scale * product(query_head, key_head.T))
        head_scores = jnp.where(same_doc, head_scores, NEGATIVE)
        weight_tensors = low(jax.nn.softmax(head_scores, axis=-1))
        return product(weight_tensors, value_head)
    mixed_heads = lax.map(jax.checkpoint(one_head), (split_heads(query_rows), split_heads(key_rows), split_heads(value_rows)))
    return mixed_heads.transpose(1, 0, 2).reshape(query_rows.shape)

def by_group(matrix):
    return matrix.reshape(GROUPS, GROUP_TOK, matrix.shape[-1])

def encoder_layer(hidden, starts, params):
    query_weight, query_bias, key_weight, value_weight, value_bias, out_weight, out_bias, norm_gain, norm_bias, expand_weight, expand_bias, shrink_weight, shrink_bias, final_gain, final_bias = params
    low_in = low(hidden)
    query_rows = low_back(low(product(low_in, query_weight) + query_bias))
    key_rows = low_back(low(product(low_in, key_weight)))
    value_rows = low_back(low(product(low_in, value_weight) + value_bias))
    attended = lax.map(jax.checkpoint(group_attend), (by_group(query_rows), by_group(key_rows), by_group(value_rows), starts))
    attended = low_back(low(attended.reshape(hidden.shape)))
    branch = low_back(product(attended, out_weight) + out_bias)
    normed = layer_norm(hidden + branch, norm_gain, norm_bias)
    inner = low_back(product(low(normed), expand_weight) + expand_bias)
    active = low(jax.nn.gelu(inner, approximate=False))
    second = low_back(product(active, shrink_weight) + shrink_bias)
    return layer_norm(normed + second, final_gain, final_bias)

def reference(tokens, doc_start, lexical_ids, queries, match_index, query_weight, query_bias, key_weight, value_weight, value_bias, out_weight, out_bias, norm_gain, norm_bias, expand_weight, expand_bias, shrink_weight, shrink_bias, final_gain, final_bias, lexical_weight, lexical_bias, score_cot, encoded_cot):
    params = (query_weight.astype(jnp.float32), query_bias.astype(jnp.float32), key_weight.astype(jnp.float32), value_weight.astype(jnp.float32), value_bias.astype(jnp.float32), out_weight.astype(jnp.float32), out_bias.astype(jnp.float32), norm_gain.astype(jnp.float32), norm_bias.astype(jnp.float32), expand_weight.astype(jnp.float32), expand_bias.astype(jnp.float32), shrink_weight.astype(jnp.float32), shrink_bias.astype(jnp.float32), final_gain.astype(jnp.float32), final_bias.astype(jnp.float32))
    query_vecs = queries.astype(jnp.float32)

    def forward(hidden, weight_tensors):
        for layer_index in range(LAYERS):
            layer_params = tuple((member[layer_index] for member in weight_tensors))
            hidden = encoder_layer(hidden, doc_start, layer_params)
        code = low(hidden)
        chosen = jnp.take_along_axis(by_group(code), match_index[:, :, None].astype(jnp.int32), axis=1)
        match = lax.optimization_barrier(jnp.sum(query_vecs * chosen, axis=-1))
        return (code, match)
    (code, match), pull = jax.vjp(forward, tokens.astype(jnp.float32), params)
    grad_tokens, grads = pull((encoded_cot.astype(jnp.float32), score_cot.astype(jnp.float32)))
    lexical = product(code, lexical_weight.astype(jnp.float32)) + lexical_bias.astype(jnp.float32)[0]
    keep_mask = (lexical_ids >= 4).astype(jnp.float32)
    stats = jnp.stack([jnp.sum(keep_mask * jax.nn.softplus(lexical)), jnp.sum(keep_mask * jax.nn.sigmoid(lexical))]) / TOKENS
    return (code.astype(jnp.bfloat16), match, stats, grad_tokens.astype(jnp.bfloat16), grads[0], grads[1], grads[2], grads[3], grads[4], grads[5], grads[6], grads[7], grads[8], grads[9], grads[10], grads[11], grads[12], grads[13], grads[14])
```

```python
import functools
import math

import jax
import jax.numpy as jnp
from jax import lax
from jax.experimental import pallas as pl
from jax.experimental.pallas import tpu as pltpu
from jax.sharding import PartitionSpec as P

HEAD = 64
EPSILON = 1e-05
NEGATIVE = -1e30
HIGHEST = lax.Precision.HIGHEST
AXES = ("dp", "seq")
BF = jnp.bfloat16
F32 = jnp.float32
VMEM_LIMIT = 56 * 1024 * 1024


def dot(left, right, left_dim=1, right_dim=0):
    return lax.dot_general(
        left, right, (((left_dim,), (right_dim,)), ((), ())), preferred_element_type=F32
    )


def head_lanes(shape, half):
    lane = lax.broadcasted_iota(jnp.int32, shape, 1)
    return (lane < HEAD) if half == 0 else (lane >= HEAD)


def attend_kernel(block, qkv_ref, col_ref, row_ref, out_ref, max_ref, sum_ref):
    tokens, width = out_ref.shape
    pairs = width // (2 * HEAD)
    scale = 1.0 / math.sqrt(HEAD)
    for pair in range(pairs):
        lo = pair * 2 * HEAD
        keys = qkv_ref[:, width + lo : width + lo + 2 * HEAD]
        values = qkv_ref[:, 2 * width + lo : 2 * width + lo + 2 * HEAD]
        values_t = values.astype(F32).T.astype(BF)
        for start in range(0, tokens, block):
            queries = qkv_ref[start : start + block, lo : lo + 2 * HEAD] * scale
            queries = queries.astype(BF)
            same = col_ref[...] == row_ref[:, start : start + block]
            halves = []
            for half in range(2):
                lanes = head_lanes(queries.shape, half)
                scores = dot(keys, jnp.where(lanes, queries, jnp.zeros_like(queries)), 1, 1)
                scores = jnp.where(same, scores, NEGATIVE)
                top = jnp.max(scores, axis=0, keepdims=True)
                raised = jnp.exp(scores - top)
                total = jnp.sum(raised, axis=0, keepdims=True)
                probs = (raised * (1.0 / total)).astype(BF)
                mixed = dot(values_t, probs)
                halves.append(mixed[half * HEAD : (half + 1) * HEAD])
                head = 2 * pair + half
                max_ref[head : head + 1, start : start + block] = top
                sum_ref[head : head + 1, start : start + block] = total
            joined = jnp.concatenate(halves, axis=0)
            out_ref[start : start + block, lo : lo + 2 * HEAD] = joined.T.astype(BF)


def attend_back_kernel(
    block, qkv_ref, col_ref, row_ref, max_ref, sum_ref, grad_ref, out_ref, key_acc, value_acc
):
    tokens, width = grad_ref.shape
    pairs = width // (2 * HEAD)
    scale = 1.0 / math.sqrt(HEAD)
    for pair in range(pairs):
        lo = pair * 2 * HEAD
        keys = qkv_ref[:, width + lo : width + lo + 2 * HEAD]
        values = qkv_ref[:, 2 * width + lo : 2 * width + lo + 2 * HEAD]
        keys_t = keys.astype(F32).T.astype(BF)
        key_acc[...] = jnp.zeros_like(key_acc)
        value_acc[...] = jnp.zeros_like(value_acc)
        for start in range(0, tokens, block):
            queries = (qkv_ref[start : start + block, lo : lo + 2 * HEAD] * scale).astype(BF)
            grads = grad_ref[start : start + block, lo : lo + 2 * HEAD]
            same = col_ref[...] == row_ref[:, start : start + block]
            halves = []
            for half in range(2):
                lanes = head_lanes(queries.shape, half)
                own_queries = jnp.where(lanes, queries, jnp.zeros_like(queries))
                own_grads = jnp.where(lanes, grads, jnp.zeros_like(grads))
                head = 2 * pair + half
                top = max_ref[head : head + 1, start : start + block]
                total = sum_ref[head : head + 1, start : start + block]
                scores = dot(keys, own_queries, 1, 1)
                scores = jnp.where(same, scores, NEGATIVE)
                probs = jnp.exp(scores - top) * (1.0 / total)
                grad_probs = dot(values, own_grads, 1, 1)
                shared = jnp.sum(probs * grad_probs, axis=0, keepdims=True)
                grad_scores = (probs * (grad_probs - shared)).astype(BF)
                value_acc[...] += dot(probs.astype(BF), own_grads)
                key_acc[...] += dot(grad_scores, own_queries)
                mixed = dot(keys_t, grad_scores)
                halves.append(mixed[half * HEAD : (half + 1) * HEAD])
            joined = jnp.concatenate(halves, axis=0) * scale
            out_ref[start : start + block, lo : lo + 2 * HEAD] = joined.T.astype(BF)
        out_ref[:, width + lo : width + lo + 2 * HEAD] = key_acc[...].astype(BF)
        out_ref[:, 2 * width + lo : 2 * width + lo + 2 * HEAD] = value_acc[...].astype(BF)


def attend(qkv, starts):
    tokens, width = qkv.shape[0], qkv.shape[1] // 3
    heads = width // HEAD
    whole = pl.BlockSpec(memory_space=pltpu.VMEM)
    return pl.pallas_call(
        functools.partial(attend_kernel, 256),
        out_shape=(
            jax.ShapeDtypeStruct((tokens, width), BF),
            jax.ShapeDtypeStruct((heads, tokens), F32),
            jax.ShapeDtypeStruct((heads, tokens), F32),
        ),
        in_specs=[whole] * 3,
        out_specs=(whole,) * 3,
        compiler_params=pltpu.CompilerParams(vmem_limit_bytes=VMEM_LIMIT),
        cost_estimate=pl.CostEstimate(
            flops=4 * tokens * tokens * width,
            bytes_accessed=8 * tokens * width,
            transcendentals=heads * tokens * tokens,
        ),
    )(qkv, starts[:, None], starts[None, :])


def attend_back(qkv, starts, row_max, row_sum, grads):
    tokens, width = grads.shape
    whole = pl.BlockSpec(memory_space=pltpu.VMEM)
    return pl.pallas_call(
        functools.partial(attend_back_kernel, 256),
        out_shape=jax.ShapeDtypeStruct((tokens, 3 * width), BF),
        in_specs=[whole] * 6,
        out_specs=whole,
        scratch_shapes=[
            pltpu.VMEM((tokens, 2 * HEAD), F32),
            pltpu.VMEM((tokens, 2 * HEAD), F32),
        ],
        compiler_params=pltpu.CompilerParams(vmem_limit_bytes=VMEM_LIMIT),
        cost_estimate=pl.CostEstimate(
            flops=10 * tokens * tokens * width,
            bytes_accessed=14 * tokens * width,
            transcendentals=(width // HEAD) * tokens * tokens,
        ),
    )(qkv, starts[:, None], starts[None, :], row_max, row_sum, grads)


def place_kernel(count, order, sizes, *refs):
    pieces, outs = refs[:count], refs[count:]
    me = lax.axis_index("dp")
    for step, piece in zip(order, pieces):
        where = me ^ step
        first = 0
        for member, rows in enumerate(sizes):
            at = pl.multiple_of(where * rows, rows)
            outs[member][pl.ds(at, rows), :] = piece[first : first + rows, :]
            first += rows


def place(pieces, order, sizes):
    columns = pieces[0].shape[1]
    count = len(pieces)
    whole = pl.BlockSpec(memory_space=pltpu.VMEM)
    return pl.pallas_call(
        functools.partial(place_kernel, count, tuple(order), tuple(sizes)),
        out_shape=tuple(jax.ShapeDtypeStruct((count * rows, columns), BF) for rows in sizes),
        in_specs=[whole] * count,
        out_specs=(whole,) * len(sizes),
        compiler_params=pltpu.CompilerParams(vmem_limit_bytes=VMEM_LIMIT),
        cost_estimate=pl.CostEstimate(
            flops=0, bytes_accessed=4 * count * sum(sizes) * columns, transcendentals=0
        ),
    )(*pieces)


def after(array, *others):
    return lax.optimization_barrier((array,) + others)[0]


def solution(mesh):
    n_dp, n_seq = mesh.shape["dp"], mesh.shape["seq"]
    n_dev = n_dp * n_seq
    special = (n_dp, n_seq) == (8, 4)

    def swap(array, bit):
        return lax.ppermute(array, AXES, [(p, p ^ bit) for p in range(n_dev)])

    def bits_of(count, unit=1):
        bits = []
        while count > 1:
            bits.append(unit)
            unit, count = unit * 2, count // 2
        return bits

    seq_bits, dp_bits = bits_of(n_seq), bits_of(n_dp, n_seq)

    def spread(piece, bits):
        pieces, steps = [piece], [0]
        for bit in reversed(bits):
            pieces = pieces + [swap(p, bit) for p in pieces]
            steps = steps + [s ^ bit for s in steps]
        return pieces, steps

    seq_steps = [0]
    for bit in reversed(seq_bits):
        seq_steps = seq_steps + [s ^ bit for s in seq_steps]

    def gather_seq(rows):
        return jnp.concatenate(spread(rows, seq_bits)[0], axis=0)

    def reduce_seq(left, right, own_rows):
        weight, dims = right
        half = left.shape[0] // 2
        sent = dot(left[half:], weight, *dims).astype(BF)
        kept = dot(left[:half], weight, *dims)
        keep = [kept[i * own_rows : (i + 1) * own_rows] for i in range(n_seq // 2)]
        send = [sent[i * own_rows : (i + 1) * own_rows] for i in range(n_seq // 2)]
        order = seq_bits
        for place_in, bit in enumerate(order):
            got = [swap(block, bit) for block in reversed(send)][::-1]
            total = [a + b.astype(F32) for a, b in zip(keep, got)]
            if place_in + 1 < len(order):
                middle = len(total) // 2
                keep, send = total[:middle], [t.astype(BF) for t in total[middle:]]
        return total[0]

    def halve(array, index_bit, bit):
        chosen = index_bit.astype(jnp.bool_)
        send = jnp.where(chosen, array[0], array[1])
        keep = jnp.where(chosen, array[1], array[0])
        return keep, swap(send, bit)

    def local(
        tokens, doc_start, lexical_ids, queries, match_index,
        query_weight, query_bias, key_weight, value_weight, value_bias,
        out_weight, out_bias, norm_gain, norm_bias, expand_weight, expand_bias,
        shrink_weight, shrink_bias, final_gain, final_bias,
        lexical_weight, lexical_bias, score_cot, encoded_cot,
    ):
        layers, part, dim = query_weight.shape
        hidden_dim = expand_weight.shape[2]
        hidden_part = shrink_weight.shape[1]
        rows_here = tokens.shape[0]
        pairs_here = dim // (2 * HEAD) // n_seq
        width = pairs_here * 2 * HEAD
        own_hidden = hidden_dim // n_seq
        block_rows = dim // n_dp
        dp, seq = lax.axis_index("dp"), lax.axis_index("seq")
        flat = dp * n_seq + seq

        def bit_of(index, bit):
            return lax.bitwise_and(lax.div(index, bit), 1)

        def by_origin(pieces):
            for bit in seq_bits:
                chosen = bit_of(seq, bit).astype(jnp.bool_)
                pieces = [jnp.where(chosen, pieces[j ^ bit], pieces[j]) for j in range(n_seq)]
            return pieces

        def exchange_steps(blocks):
            pieces = by_origin(blocks)
            return [pieces[0]] + [swap(pieces[step], step) for step in range(1, n_seq)]

        def exchange_seq(blocks):
            return by_origin(exchange_steps(blocks))

        small_full = (
            query_bias, value_bias, out_bias, norm_gain, norm_bias, shrink_bias, final_gain, final_bias,
        )
        small = jnp.concatenate(list(small_full) + [expand_bias], axis=1).reshape(1, -1)
        small_len = small.shape[1]
        small = jnp.pad(small, ((0, 15), (0, 3 * width - small_len)))

        def head_split(weight):
            cut = [weight[:, i * 2 * HEAD : (i + 1) * 2 * HEAD] for i in range(pairs_here * n_seq)]
            return [cut[s::n_seq] for s in range(n_seq)]

        def hidden_split(weight):
            cut = [
                weight[:, i * hidden_part : (i + 1) * hidden_part] for i in range(n_dp * n_seq)
            ]
            return [cut[s::n_seq] for s in range(n_seq)]

        def qkv_split(layer):
            three = [head_split(w[layer]) for w in (query_weight, key_weight, value_weight)]
            return [jnp.concatenate(three[0][s] + three[1][s] + three[2][s], axis=1) for s in range(n_seq)]

        first = exchange_seq([jnp.concatenate([b, small], axis=0) for b in qkv_split(0)])
        first_rows = jnp.concatenate([p[:part] for p in first], axis=0)
        first_small = jnp.concatenate([p[part : part + 1] for p in first], axis=0)
        first_small = jnp.pad(first_small, ((0, 16 - n_seq), (0, 0)))
        pieces, steps = spread(jnp.concatenate([first_rows, first_small], axis=0), dp_bits)
        dp_steps = [s // n_seq for s in steps]
        qkv_first, small_all = place(pieces, dp_steps, (block_rows, 16))
        first_pieces = pieces
        small_all = small_all.reshape(n_dp, 16, -1)[:, :n_seq, :small_len]
        small_all = small_all.reshape(n_dev, layers, -1)

        hidden_now = tokens.astype(F32)
        group = gather_seq(tokens)

        blocks = [[] for _ in range(n_seq)]
        for layer in range(layers):
            here = hidden_split(expand_weight[layer])
            more = qkv_split(layer) if layer else None
            for s in range(n_seq):
                blocks[s] += ([more[s]] if layer else []) + here[s]
        second = exchange_seq([jnp.concatenate(b, axis=1) for b in blocks])
        second = jnp.concatenate(second, axis=0)

        if special:
            pieces, steps = spread(out_weight, seq_bits)
            pieces = by_origin([pieces[steps.index(step)] for step in range(n_seq)])
            out_all = []
            for layer in range(layers):
                rows = jnp.concatenate([p[layer] for p in pieces], axis=0)
                if layer:
                    rows = after(rows, out_all[0])
                for bit in (1, 2):
                    moved = swap(rows, n_seq * bit)
                    rows = jnp.where(bit_of(seq, bit) == bit_of(dp, bit), rows, moved)
                moved = swap(rows, n_seq * 4)
                upper = bit_of(dp, 4) == 1
                out_all.append(
                    jnp.concatenate(
                        [jnp.where(upper, moved, rows), jnp.where(upper, rows, moved)], axis=0
                    )
                )
        else:
            whole_out = lax.all_gather(out_weight, AXES, axis=1, tiled=True)
            cut = whole_out.reshape(layers, pairs_here, n_seq, 2 * HEAD, dim)
            cut = lax.dynamic_index_in_dim(cut, seq, 2, keepdims=False)
            out_all = [cut[layer].reshape(width, dim) for layer in range(layers)]

        pieces, steps = spread(after(second[:, :own_hidden], first_pieces[1]), dp_bits)
        (expand_first,) = place(pieces, dp_steps, (block_rows,))
        pieces, steps = spread(after(shrink_weight[0], pieces[1]), dp_bits)
        (shrink_first,) = place(pieces, dp_steps, (hidden_part,))

        qkv_all, expand_all, shrink_all = [qkv_first], [expand_first], [shrink_first]
        at = own_hidden
        for layer in range(1, layers):
            rest = second[:, at : at + 3 * width]
            at += 3 * width
            pieces, steps = spread(after(rest, pieces[1]), dp_bits)
            qkv_all += place(pieces, dp_steps, (block_rows,))
            rest = after(second[:, at : at + own_hidden], pieces[1])
            at += own_hidden
            expand_all.append(lax.all_gather(rest, "dp", axis=0, tiled=True))
            rest = after(shrink_weight[layer], pieces[1])
            shrink_all.append(lax.all_gather(rest, "dp", axis=0, tiled=True))

        full = small_all[:, :, : 8 * part].reshape(n_dev, layers, 8, part)
        full = full.transpose(1, 2, 0, 3).reshape(layers, 8, dim).astype(F32)
        by_column = full[:, :2].reshape(layers, 2, pairs_here, n_seq, 2 * HEAD)
        by_column = lax.dynamic_index_in_dim(by_column, seq, 3, keepdims=False)
        by_column = by_column.reshape(layers, 2, width)
        hidden_bias = small_all[:, :, 8 * part :].reshape(n_dp, n_seq, layers, hidden_part)
        hidden_bias = lax.dynamic_index_in_dim(hidden_bias, seq, 1, keepdims=False)
        hidden_bias = hidden_bias.transpose(1, 0, 2).reshape(layers, own_hidden).astype(F32)

        starts_here = doc_start[0].reshape(n_seq, rows_here)
        starts = jnp.concatenate(
            [
                lax.dynamic_index_in_dim(starts_here, seq ^ step, 0, keepdims=False)
                for step in seq_steps
            ]
        )

        def norm_parts(resid):
            center = resid - jnp.mean(resid, axis=-1, keepdims=True)
            inverse = lax.rsqrt(jnp.mean(center * center, axis=-1, keepdims=True) + EPSILON)
            return center * inverse, inverse

        def norm_back(upstream, gain, rhat, inverse):
            scaled = upstream * gain
            mean_one = jnp.mean(scaled, axis=-1, keepdims=True)
            mean_two = jnp.mean(scaled * rhat, axis=-1, keepdims=True)
            grad = (scaled - mean_one - rhat * mean_two) * inverse
            return grad, jnp.sum(upstream * rhat, axis=0), jnp.sum(upstream, axis=0)

        def column_sums(matrix):
            return jnp.sum(matrix.astype(F32), axis=0)

        kept = []
        for layer in range(layers):
            _, _, out_b, gain_one, bias_one, shrink_b, gain_two, bias_two = (
                full[layer, i] for i in range(8)
            )
            if layer:
                group = gather_seq(hidden_now.astype(BF))
            bias_row = jnp.concatenate(
                [by_column[layer, 0], jnp.zeros((width,), F32), by_column[layer, 1]]
            )
            qkv = (dot(group, qkv_all[layer]) + bias_row).astype(BF)
            attended, row_max, row_sum = attend(qkv, starts)
            summed = reduce_seq(attended, (out_all[layer], (1, 0)), rows_here)
            resid_one = hidden_now + (summed + out_b)
            rhat_one, inverse_one = norm_parts(resid_one)
            normed = rhat_one * gain_one + bias_one
            normed_group = gather_seq(normed.astype(BF))
            inner = dot(normed_group, expand_all[layer]) + hidden_bias[layer]
            cdf = 0.5 * (1.0 + lax.erf(inner * math.sqrt(0.5)))
            active = (inner * cdf).astype(BF)
            slope = cdf + inner * jnp.exp(-0.5 * inner * inner) * (1.0 / math.sqrt(2 * math.pi))
            summed = reduce_seq(active, (shrink_all[layer], (1, 0)), rows_here)
            resid_two = normed + (summed + shrink_b)
            rhat_two, inverse_two = norm_parts(resid_two)
            hidden_now = rhat_two * gain_two + bias_two
            kept.append(
                (group, qkv, attended, row_max, row_sum, rhat_one, inverse_one, normed_group,
                 active, slope, rhat_two, inverse_two)
            )
        encoded = hidden_now.astype(BF)

        local_index = match_index[0] - seq * rows_here
        picker = local_index[:, None] == jnp.arange(rows_here, dtype=jnp.int32)[None, :]
        chosen = dot(picker.astype(BF), encoded)
        query_vecs = queries[0].astype(F32)
        scores = jnp.sum(query_vecs * chosen, axis=-1)[None, :]
        for bit in seq_bits:
            scores = scores + swap(scores, bit)
        lexical = jnp.sum(
            encoded.astype(F32) * lexical_weight.astype(F32)[None, :], axis=-1
        ) + lexical_bias.astype(F32)[0]
        keep_mask = (lexical_ids >= 4).astype(F32)
        local_sums = jnp.stack(
            [
                jnp.sum(keep_mask * jax.nn.softplus(lexical)),
                jnp.sum(keep_mask * jax.nn.sigmoid(lexical)),
            ]
        )
        weighted = score_cot[0][:, None] * query_vecs
        grad_now = encoded_cot.astype(F32) + lax.dot_general(
            picker.astype(F32), weighted, (((0,), (0,)), ((), ())), precision=HIGHEST
        )

        def scatter_dp(grad):
            return lax.psum_scatter(grad, "dp", scatter_dimension=0, tiled=True)

        def scatter_dp_steps(grad):
            rest = grad
            index_unit = 1
            for bit in dp_bits:
                keep_rows = rest.reshape(-1, 2, block_rows, rest.shape[-1])
                keep, got = halve(
                    (keep_rows[:, 0], keep_rows[:, 1]), bit_of(dp, index_unit), bit
                )
                total = keep.astype(F32) + got.astype(F32)
                rest = total.astype(BF)
                index_unit *= 2
            return rest.reshape(block_rows, -1)

        def scatter_out(grad):
            if not special:
                placed = grad.reshape(pairs_here, 1, 2 * HEAD, dim)
                hot = (jnp.arange(n_seq) == seq)[None, :, None, None]
                placed = jnp.where(hot, placed, jnp.zeros_like(placed)).reshape(dim, dim)
                return lax.psum_scatter(placed, AXES, scatter_dimension=0, tiled=True)
            halves = grad.reshape(2, 2 * HEAD, dim)
            keep, got = halve((halves[0], halves[1]), bit_of(dp, 4), 4 * n_seq)
            for bit in (2, 1):
                total = (keep.astype(F32) + got.astype(F32)).astype(BF)
                keep, got = total, swap(total, bit * n_seq)
            return (keep.astype(F32) + got.astype(F32)).astype(BF)

        def unsplit(pieces, size):
            count = pieces[0].shape[1] // size
            return jnp.concatenate(
                [pieces[s][:, i * size : (i + 1) * size] for i in range(count) for s in range(n_seq)],
                axis=1,
            )

        def rows_back(scattered):
            return exchange_steps([scattered[s * part : (s + 1) * part] for s in range(n_seq)])

        def spread_columns(vector):
            hot = (jnp.arange(n_seq) == seq)[None, :, None]
            return jnp.where(hot, vector.reshape(pairs_here, 1, 2 * HEAD), 0.0).reshape(dim)

        def spread_hidden(vector):
            hot = (jnp.arange(n_seq) == seq)[None, :, None]
            return jnp.where(hot, vector.reshape(n_dp, 1, hidden_part), 0.0).reshape(hidden_dim)

        big = [None] * layers
        vectors = [None] * layers
        for layer in reversed(range(layers)):
            _, _, _, gain_one, _, _, gain_two, _ = (full[layer, i] for i in range(8))
            (group, qkv, attended, row_max, row_sum, rhat_one, inverse_one, normed_group,
             active, slope, rhat_two, inverse_two) = kept[layer]
            grad_second, fgain, fbias = norm_back(grad_now, gain_two, rhat_two, inverse_two)
            low_second = grad_second.astype(BF)
            second_group = gather_seq(low_second)
            low_inner = (dot(second_group, shrink_all[layer], 1, 1) * slope).astype(BF)
            summed = reduce_seq(low_inner, (expand_all[layer], (1, 1)), rows_here)
            shrink_grad = dot(active, second_group, 0, 0).astype(BF)
            expand_grad = dot(normed_group, low_inner, 0, 0).astype(BF)
            if layer or not special:
                shrink_rows, expand_rows = scatter_dp(shrink_grad), scatter_dp(expand_grad)
            else:
                shrink_rows, expand_rows = scatter_dp_steps(shrink_grad), scatter_dp_steps(expand_grad)
            grad_normed = grad_second + summed
            grad_first, ngain, nbias = norm_back(grad_normed, gain_one, rhat_one, inverse_one)
            low_first = grad_first.astype(BF)
            first_group = gather_seq(low_first)
            low_attn = dot(first_group, out_all[layer], 1, 1).astype(BF)
            out_rows = scatter_out(dot(attended, first_group, 0, 0).astype(BF))
            grad_qkv = attend_back(qkv, starts, row_max, row_sum, low_attn)
            qkv_rows = scatter_dp_steps(dot(group, grad_qkv, 0, 0).astype(BF))
            summed = reduce_seq(grad_qkv, (qkv_all[layer], (1, 1)), rows_here)
            grad_now = grad_first + summed
            qkv_sums = column_sums(grad_qkv)
            vectors[layer] = [
                spread_columns(qkv_sums[:width]),
                spread_columns(qkv_sums[2 * width :]),
                column_sums(low_first),
                ngain,
                nbias,
                column_sums(low_second),
                fgain,
                fbias,
                spread_hidden(column_sums(low_inner)),
            ]
            big[layer] = (qkv_rows, shrink_rows, expand_rows, out_rows)

        tokens_grad = grad_now.astype(BF)

        table = jnp.concatenate(
            [
                v.reshape(n_dev, -1)
                for layer in range(layers)
                for v in vectors[layer]
            ]
            + [jnp.broadcast_to(local_sums[None, :], (n_dev, 2))],
            axis=1,
        )
        for bit in seq_bits + dp_bits:
            pairs = table.reshape(-1, 2, table.shape[-1])
            keep, got = halve((pairs[:, 0], pairs[:, 1]), bit_of(flat, bit), bit)
            table = keep + got
        table = table.reshape(-1)
        lexical_stats = table[-2:] / (rows_here * n_dev)
        table = table[:-2].reshape(layers, 8 * part + hidden_part)

        def vector_out(index):
            return table[:, index * part : (index + 1) * part]

        layer_outs = []
        for layer in range(layers):
            qkv_rows, shrink_rows, expand_rows, out_rows = big[layer]
            parts = [expand_rows] + ([out_rows] if special else [])
            if layer:
                parts.append(qkv_rows)
            got = rows_back(jnp.concatenate(parts, axis=1))
            expand_out = unsplit(by_origin([g[:, :own_hidden] for g in got]), hidden_part)
            at = own_hidden
            if special:
                source = seq ^ lax.rem(dp, n_seq)
                out_out = got[0][:, at : at + dim]
                for step in range(1, n_seq):
                    out_out = jnp.where(source == step, got[step][:, at : at + dim], out_out)
                at += dim
            else:
                out_out = out_rows
            if layer:
                qkv_out = by_origin([g[:, at:] for g in got])
            else:
                qkv_out = by_origin(rows_back(qkv_rows))
            layer_outs.append(
                [
                    unsplit([b[:, i * width : (i + 1) * width] for b in qkv_out], 2 * HEAD)
                    for i in range(3)
                ]
                + [out_out, expand_out, shrink_rows]
            )
        big_out = [jnp.stack([lo[i].astype(F32) for lo in layer_outs]) for i in range(6)]
        return (
            encoded, scores, lexical_stats, tokens_grad,
            big_out[0], vector_out(0), big_out[1], big_out[2], vector_out(1),
            big_out[3], vector_out(2), vector_out(3), vector_out(4),
            big_out[4], table[:, 8 * part :], big_out[5], vector_out(5),
            vector_out(6), vector_out(7),
        )

    rows = P(AXES, None)
    weight = P(None, AXES, None)
    vector = P(None, AXES)
    placed = (
        rows, P("dp", None), P(AXES), P("dp", None, None), P("dp", None),
        weight, vector, weight, weight, vector, weight, vector, vector, vector,
        weight, vector, weight, vector, vector, vector, P(), P(), P("dp", None), rows,
    )
    results = (
        rows, P("dp", None), P(), rows,
        weight, vector, weight, weight, vector, weight, vector, vector, vector,
        weight, vector, weight, vector, vector, vector,
    )
    return jax.shard_map(local, mesh=mesh, in_specs=placed, out_specs=results, check_vma=False)
```

```python
import functools
import math

import jax
import jax.numpy as jnp
from jax import lax
from jax.experimental import pallas as pl
from jax.experimental.pallas import tpu as pltpu
from jax.sharding import PartitionSpec as P

HEAD = 64
EPSILON = 1e-05
NEGATIVE = -1e30
HIGHEST = lax.Precision.HIGHEST
AXES = ("dp", "seq")
BF = jnp.bfloat16
F32 = jnp.float32
VMEM_LIMIT = 56 * 1024 * 1024


def dot(left, right, left_dim=1, right_dim=0):
    return lax.dot_general(
        left, right, (((left_dim,), (right_dim,)), ((), ())), preferred_element_type=F32
    )


def head_lanes(shape, half):
    lane = lax.broadcasted_iota(jnp.int32, shape, 1)
    return (lane < HEAD) if half == 0 else (lane >= HEAD)


def attend_kernel(block, qkv_ref, col_ref, row_ref, out_ref, max_ref, sum_ref):
    tokens, width = out_ref.shape
    pairs = width // (2 * HEAD)
    scale = 1.0 / math.sqrt(HEAD)
    for pair in range(pairs):
        lo = pair * 2 * HEAD
        keys = qkv_ref[:, width + lo : width + lo + 2 * HEAD]
        values = qkv_ref[:, 2 * width + lo : 2 * width + lo + 2 * HEAD]
        values_t = values.astype(F32).T.astype(BF)
        for start in range(0, tokens, block):
            queries = qkv_ref[start : start + block, lo : lo + 2 * HEAD] * scale
            queries = queries.astype(BF)
            same = col_ref[...] == row_ref[:, start : start + block]
            halves = []
            for half in range(2):
                lanes = head_lanes(queries.shape, half)
                scores = dot(keys, jnp.where(lanes, queries, jnp.zeros_like(queries)), 1, 1)
                scores = jnp.where(same, scores, NEGATIVE)
                top = jnp.max(scores, axis=0, keepdims=True)
                raised = jnp.exp(scores - top)
                total = jnp.sum(raised, axis=0, keepdims=True)
                probs = (raised * (1.0 / total)).astype(BF)
                mixed = dot(values_t, probs)
                halves.append(mixed[half * HEAD : (half + 1) * HEAD])
                head = 2 * pair + half
                max_ref[head : head + 1, start : start + block] = top
                sum_ref[head : head + 1, start : start + block] = total
            joined = jnp.concatenate(halves, axis=0)
            out_ref[start : start + block, lo : lo + 2 * HEAD] = joined.T.astype(BF)


def attend_back_kernel(
    block, qkv_ref, col_ref, row_ref, max_ref, sum_ref, grad_ref, out_ref, key_acc, value_acc
):
    tokens, width = grad_ref.shape
    pairs = width // (2 * HEAD)
    scale = 1.0 / math.sqrt(HEAD)
    for pair in range(pairs):
        lo = pair * 2 * HEAD
        keys = qkv_ref[:, width + lo : width + lo + 2 * HEAD]
        values = qkv_ref[:, 2 * width + lo : 2 * width + lo + 2 * HEAD]
        keys_t = keys.astype(F32).T.astype(BF)
        key_acc[...] = jnp.zeros_like(key_acc)
        value_acc[...] = jnp.zeros_like(value_acc)
        for start in range(0, tokens, block):
            queries = (qkv_ref[start : start + block, lo : lo + 2 * HEAD] * scale).astype(BF)
            grads = grad_ref[start : start + block, lo : lo + 2 * HEAD]
            same = col_ref[...] == row_ref[:, start : start + block]
            halves = []
            for half in range(2):
                lanes = head_lanes(queries.shape, half)
                own_queries = jnp.where(lanes, queries, jnp.zeros_like(queries))
                own_grads = jnp.where(lanes, grads, jnp.zeros_like(grads))
                head = 2 * pair + half
                top = max_ref[head : head + 1, start : start + block]
                total = sum_ref[head : head + 1, start : start + block]
                scores = dot(keys, own_queries, 1, 1)
                scores = jnp.where(same, scores, NEGATIVE)
                probs = jnp.exp(scores - top) * (1.0 / total)
                grad_probs = dot(values, own_grads, 1, 1)
                shared = jnp.sum(probs * grad_probs, axis=0, keepdims=True)
                grad_scores = (probs * (grad_probs - shared)).astype(BF)
                value_acc[...] += dot(probs.astype(BF), own_grads)
                key_acc[...] += dot(grad_scores, own_queries)
                mixed = dot(keys_t, grad_scores)
                halves.append(mixed[half * HEAD : (half + 1) * HEAD])
            joined = jnp.concatenate(halves, axis=0) * scale
            out_ref[start : start + block, lo : lo + 2 * HEAD] = joined.T.astype(BF)
        out_ref[:, width + lo : width + lo + 2 * HEAD] = key_acc[...].astype(BF)
        out_ref[:, 2 * width + lo : 2 * width + lo + 2 * HEAD] = value_acc[...].astype(BF)


def attend(qkv, starts):
    tokens, width = qkv.shape[0], qkv.shape[1] // 3
    heads = width // HEAD
    whole = pl.BlockSpec(memory_space=pltpu.VMEM)
    return pl.pallas_call(
        functools.partial(attend_kernel, 256),
        out_shape=(
            jax.ShapeDtypeStruct((tokens, width), BF),
            jax.ShapeDtypeStruct((heads, tokens), F32),
            jax.ShapeDtypeStruct((heads, tokens), F32),
        ),
        in_specs=[whole] * 3,
        out_specs=(whole,) * 3,
        compiler_params=pltpu.CompilerParams(vmem_limit_bytes=VMEM_LIMIT),
        cost_estimate=pl.CostEstimate(
            flops=40 * tokens * tokens * width, bytes_accessed=16 * tokens * width, transcendentals=0
        ),
    )(qkv, starts[:, None], starts[None, :])


def attend_back(qkv, starts, row_max, row_sum, grads):
    tokens, width = grads.shape
    whole = pl.BlockSpec(memory_space=pltpu.VMEM)
    return pl.pallas_call(
        functools.partial(attend_back_kernel, 256),
        out_shape=jax.ShapeDtypeStruct((tokens, 3 * width), BF),
        in_specs=[whole] * 6,
        out_specs=whole,
        scratch_shapes=[
            pltpu.VMEM((tokens, 2 * HEAD), F32),
            pltpu.VMEM((tokens, 2 * HEAD), F32),
        ],
        compiler_params=pltpu.CompilerParams(vmem_limit_bytes=VMEM_LIMIT),
        cost_estimate=pl.CostEstimate(
            flops=40 * tokens * tokens * width, bytes_accessed=16 * tokens * width, transcendentals=0
        ),
    )(qkv, starts[:, None], starts[None, :], row_max, row_sum, grads)


def place_rows(order, sizes, pieces, outs):
    me = lax.axis_index("dp")
    for steps, piece in zip(order, pieces):
        first = 0
        for step in steps:
            if isinstance(step, tuple):
                where = step[0] * 2 + (lax.rem(me, 2) ^ step[1])
            else:
                where = me ^ step
            for member, rows in enumerate(sizes):
                at = pl.multiple_of(where * rows, rows)
                outs[member][pl.ds(at, rows), :] = piece[first : first + rows, :]
                first += rows


def place_kernel(order, sizes, *refs):
    place_rows(order, sizes, refs[: len(order)], refs[len(order) :])


def place_first_kernel(order, sizes, pairs, layers, *refs):
    pieces, (weights, smalls, full, heads, inner) = refs[: len(order)], refs[len(order) :]
    place_rows(order, sizes, pieces, (weights, smalls))
    seq, n_seq = lax.axis_index("seq"), 4
    n_dp = smalls.shape[0] // 16
    lane = lax.broadcasted_iota(jnp.int32, (4, 128), 1)
    for dp in range(n_dp):
        rows = smalls[dp * 16 : dp * 16 + 16, :].astype(F32)
        for block in range(6):
            part = rows[:, block * 128 : block * 128 + 128]
            total = part[:4]
            for s in range(1, n_seq):
                moved = pltpu.roll(part, 32 * s, 1)[4 * s : 4 * s + 4]
                total = jnp.where(lane // 32 == s, moved, total)
            full[block, 0:4, dp * 128 : dp * 128 + 128] = total
            if block == 2:
                own = part[:4]
                for s in range(1, n_seq):
                    own = jnp.where(seq == s, part[4 * s : 4 * s + 4], own)
                inner[0:layers, dp * 128 : dp * 128 + 128] = own[layers : 2 * layers]
    heads[...] = jnp.zeros_like(heads)
    width = pairs * 128
    for which, base in ((0, 0), (1, 2 * width)):
        for pair in range(pairs):
            column = pl.multiple_of((pair * n_seq + seq) * 128, 128)
            heads[0:layers, base + pair * 128 : base + pair * 128 + 128] = full[
                which, 0:layers, pl.ds(column, 128)
            ]


def place(pieces, order, sizes, unpack=None):
    columns = pieces[0].shape[1]
    order = tuple(tuple(o) if isinstance(o, (list, tuple)) else (o,) for o in order)
    count = sum(len(o) for o in order)
    whole = pl.BlockSpec(memory_space=pltpu.VMEM)
    shapes = [jax.ShapeDtypeStruct((count * rows, columns), BF) for rows in sizes]
    body = functools.partial(place_kernel, order, tuple(sizes))
    if unpack is not None:
        pairs, layers, dim, inner = unpack
        shapes += [
            jax.ShapeDtypeStruct((6, 8, dim), F32),
            jax.ShapeDtypeStruct((8, pairs * 3 * 128), F32),
            jax.ShapeDtypeStruct((8, inner), F32),
        ]
        body = functools.partial(place_first_kernel, order, tuple(sizes), pairs, layers)
    return pl.pallas_call(
        body,
        out_shape=tuple(shapes),
        in_specs=[whole] * len(pieces),
        out_specs=(whole,) * len(shapes),
        compiler_params=pltpu.CompilerParams(vmem_limit_bytes=VMEM_LIMIT),
        cost_estimate=pl.CostEstimate(flops=0, bytes_accessed=0, transcendentals=0),
    )(*pieces)


def split_kernel(n_seq, plan, part, smalls, *refs):
    n_in = 1 + max(p[0] for p in plan)
    weights, rest = refs[:n_in], refs[n_in:]
    small_refs, rest = rest[:smalls], rest[smalls:]
    outs = rest[:n_seq]
    seq = lax.axis_index("seq")
    if smalls:
        table = rest[n_seq]
        table[...] = jnp.zeros_like(table)
        across = table.shape[1] // 128
        for j, small in enumerate(small_refs):
            row, lane = 2 * (j // across), 128 * (j % across)
            table[row : row + 2, lane : lane + small.shape[1]] = small[...].astype(F32)
    for step in range(n_seq):
        target = seq ^ step
        at = 0
        for ref, layer, block, count in plan:
            if not count:
                outs[step][:part, at : at + block] = weights[ref][layer]
                at += block
            for i in range(count):
                column = pl.multiple_of((i * n_seq + target) * block, 128)
                outs[step][:part, at : at + block] = weights[ref][layer, :, pl.ds(column, block)]
                at += block
        if smalls:
            outs[step][part:, :] = table[...].astype(BF)


def split_weights(weights, plan, n_seq, smalls=()):
    part = weights[0].shape[1]
    columns = sum(block * max(count, 1) for _, _, block, count in plan)
    rows = part + (16 if smalls else 0)
    whole = pl.BlockSpec(memory_space=pltpu.VMEM)
    return pl.pallas_call(
        functools.partial(split_kernel, n_seq, tuple(plan), part, len(smalls)),
        out_shape=tuple(jax.ShapeDtypeStruct((rows, columns), BF) for _ in range(n_seq)),
        in_specs=[whole] * (len(weights) + len(smalls)),
        out_specs=(whole,) * n_seq,
        scratch_shapes=[pltpu.VMEM((16, columns), F32)] if smalls else [],
        compiler_params=pltpu.CompilerParams(vmem_limit_bytes=VMEM_LIMIT),
    )(*weights, *smalls)


def join_kernel(n_seq, part, cuts, with_small, extra, *refs):
    pieces, rest = refs[:n_seq], refs[n_seq:]
    if extra:
        extra_ref, rest = rest[0], rest[1:]
    outs = rest[: len(cuts)]
    seq = lax.axis_index("seq")
    for step in range(n_seq):
        row = pl.multiple_of((seq ^ step) * part, part)
        at = 0
        for out, columns in zip(outs, cuts):
            out[pl.ds(row, part), :] = pieces[step][:part, at : at + columns]
            at += columns
    if with_small:
        table = rest[len(cuts)]
        smalls = [pieces[step][part:, :].astype(F32)[:4] for step in range(n_seq)]
        for origin in range(n_seq):
            total = jnp.zeros_like(smalls[0])
            for step in range(n_seq):
                total = jnp.where((seq ^ step) == origin, smalls[step], total)
            table[4 * origin : 4 * origin + 4, :] = total
        outs[0][n_seq * part :, :] = table[...].astype(BF)
    if extra:
        outs[0][n_seq * part :, :] = extra_ref[0]


def join_pieces(pieces, part, cuts, with_small=False, extra=None):
    n_seq = len(pieces)
    rows = [n_seq * part] * len(cuts)
    if with_small:
        rows[0] += 4 * n_seq
    if extra is not None:
        rows[0] += extra.shape[1]
    whole = pl.BlockSpec(memory_space=pltpu.VMEM)
    more = [] if extra is None else [extra]
    return pl.pallas_call(
        functools.partial(
            join_kernel, n_seq, part, tuple(cuts), with_small, extra is not None
        ),
        out_shape=tuple(jax.ShapeDtypeStruct((r, c), BF) for r, c in zip(rows, cuts)),
        in_specs=[whole] * (n_seq + len(more)),
        out_specs=(whole,) * len(cuts),
        scratch_shapes=[pltpu.VMEM((4 * n_seq, cuts[0]), F32)] if with_small else [],
        compiler_params=pltpu.CompilerParams(vmem_limit_bytes=VMEM_LIMIT),
    )(*pieces, *more)


def after(array, *others):
    return lax.optimization_barrier((array,) + others)[0] if others else array


def solution(mesh):
    n_dp, n_seq = mesh.shape["dp"], mesh.shape["seq"]
    n_dev = n_dp * n_seq
    special = (n_dp, n_seq) == (8, 4)

    def swap(array, bit):
        return lax.ppermute(array, AXES, [(p, p ^ bit) for p in range(n_dev)])

    def bits_of(count, unit=1):
        bits = []
        while count > 1:
            bits.append(unit)
            unit, count = unit * 2, count // 2
        return bits

    seq_bits, dp_bits = bits_of(n_seq), bits_of(n_dp, n_seq)

    z_lines = [[d for d in range(n_dp) if d % 2 == y] for y in range(2)]

    seq_steps = [0]
    for bit in reversed(seq_bits):
        seq_steps = seq_steps + [s ^ bit for s in seq_steps]

    def spread(piece, bits):
        pieces, steps = [piece], [0]
        for bit in reversed(bits):
            pieces = pieces + [swap(p, bit) for p in pieces]
            steps = steps + [s ^ bit for s in steps]
        return pieces, steps

    def launch(moves, gate):
        return [
            (home, name, swap(after(array, gate), bit) if bit else array)
            for home, name, array, bit in moves
        ]

    def settle(array, moving):
        if not moving:
            return array
        out = lax.optimization_barrier((array,) + tuple(m[2] for m in moving))
        for (home, name, _), value in zip(moving, out[1:]):
            setattr(home, name, value)
        return out[0]

    def gather_seq(rows, moves=(), gate=None):
        moving = launch(moves, rows if gate is None else gate)
        for bit in reversed(seq_bits):
            got = settle(swap(rows, bit), moving)
            moving = []
            rows = jnp.concatenate([rows, got], axis=0)
        return rows

    def reduce_seq(left, right, moves=(), gate=None):
        weight, dims = right
        moving = launch(moves, left if gate is None else gate)
        half = left.shape[0] // 2
        got = swap(dot(left[half:], weight, *dims).astype(BF), seq_bits[0])
        total = dot(left[:half], weight, *dims) + got.astype(F32)
        for i, bit in enumerate(seq_bits[1:]):
            half = total.shape[0] // 2
            got = swap(total[half:].astype(BF), bit)
            if i + 2 == len(seq_bits):
                got = settle(got, moving)
            total = total[:half] + got.astype(F32)
        return total

    def halve(array, index_bit, bit):
        chosen = index_bit.astype(jnp.bool_)
        send = jnp.where(chosen, array[0], array[1])
        keep = jnp.where(chosen, array[1], array[0])
        return keep, swap(send, bit)

    def local(
        tokens, doc_start, lexical_ids, queries, match_index,
        query_weight, query_bias, key_weight, value_weight, value_bias,
        out_weight, out_bias, norm_gain, norm_bias, expand_weight, expand_bias,
        shrink_weight, shrink_bias, final_gain, final_bias,
        lexical_weight, lexical_bias, score_cot, encoded_cot,
    ):
        layers, part, dim = query_weight.shape
        hidden_dim = expand_weight.shape[2]
        hidden_part = shrink_weight.shape[1]
        rows_here = tokens.shape[0]
        pairs_here = dim // (2 * HEAD) // n_seq
        width = pairs_here * 2 * HEAD
        own_hidden = hidden_dim // n_seq
        block_rows = dim // n_dp
        dp, seq = lax.axis_index("dp"), lax.axis_index("seq")
        flat = dp * n_seq + seq

        def bit_of(index, bit):
            return lax.bitwise_and(lax.div(index, bit), 1)

        def by_origin(pieces):
            for bit in seq_bits:
                chosen = bit_of(seq, bit).astype(jnp.bool_)
                pieces = [jnp.where(chosen, pieces[j ^ bit], pieces[j]) for j in range(n_seq)]
            return pieces

        def exchange_steps(blocks):
            pieces = by_origin(blocks)
            return [pieces[0]] + [swap(pieces[step], step) for step in range(1, n_seq)]

        def exchange_seq(blocks):
            return by_origin(exchange_steps(blocks))

        def head_split(weight):
            cut = [weight[:, i * 2 * HEAD : (i + 1) * 2 * HEAD] for i in range(pairs_here * n_seq)]
            return [cut[s::n_seq] for s in range(n_seq)]

        def hidden_split(weight):
            cut = [
                weight[:, i * hidden_part : (i + 1) * hidden_part] for i in range(n_dp * n_seq)
            ]
            return [cut[s::n_seq] for s in range(n_seq)]

        def qkv_split(layer):
            three = [head_split(w[layer]) for w in (query_weight, key_weight, value_weight)]
            return [jnp.concatenate(three[0][s] + three[1][s] + three[2][s], axis=1) for s in range(n_seq)]

        small_full = (
            query_bias, value_bias, out_bias, norm_gain, norm_bias, shrink_bias, final_gain, final_bias,
        )
        three = [query_weight, key_weight, value_weight]
        hidden_now = tokens.astype(F32)
        if special:
            heads_plan = [(i, 0, 2 * HEAD, pairs_here) for i in range(3)]
            sent = split_weights(three, heads_plan, n_seq, small_full + (expand_bias,))
            got = [sent[0]] + [swap(sent[step], step) for step in range(1, n_seq)]
            (shard,) = join_pieces(got, part, (3 * width,), True)
            class Stream:
                def __init__(self, shard):
                    self.shard = shard

                def far(self):
                    return [(self, "came", self.shard, n_seq * 4)]

                def middle(self):
                    self.line = jnp.concatenate([self.shard, self.came], axis=0)
                    return [
                        (self, "near", self.line, n_seq * 2),
                        (self, "y_line", self.line, n_seq),
                    ]

                def last(self):
                    return [(self, "y_near", self.near, n_seq)]

                def ready(self, sizes):
                    return [(self, "full", self.whole(sizes)[0], 0)]

                def whole(self, sizes, unpack=None):
                    pieces = [self.line, self.near, self.y_line, self.y_near]
                    return place(pieces, [[0, 4], [2, 6], [1, 5], [3, 7]], sizes, unpack)

            first_stream = Stream(shard)
            group = gather_seq(tokens)
            plan = [(3, 0, hidden_part, n_dp)]
            cuts = [own_hidden]
            for layer in range(1, layers):
                plan += [(i, layer, 2 * HEAD, pairs_here) for i in range(3)]
                plan += [(3, layer, hidden_part, n_dp)]
                cuts += [3 * width, own_hidden]
            plan += [(4, layer, dim, 0) for layer in range(layers)]
            cuts += [dim] * layers
            sent = split_weights(three + [expand_weight, out_weight], plan, n_seq)
            sent = [after(p, got[1], got[2], got[3]) for p in sent]
            got = [sent[0]] + [swap(sent[step], step) for step in range(1, n_seq)]
            second = join_pieces(got, part, cuts)

            class OutRows:
                def __init__(self, rows):
                    self.rows, self.moved, self.bit = rows, None, 0

                def take(self):
                    bit, moved = self.bit, self.moved
                    if bit in (1, 2):
                        here = bit_of(seq, bit) == bit_of(dp, bit)
                        self.rows = jnp.where(here, self.rows, moved)
                    elif bit == 4:
                        upper = bit_of(dp, 4) == 1
                        self.rows = jnp.concatenate(
                            [jnp.where(upper, moved, self.rows), jnp.where(upper, self.rows, moved)],
                            axis=0,
                        )
                    self.bit = 0
                    self.rows = lax.optimization_barrier(self.rows)
                    return self.rows

                def step(self, bit):
                    rows = self.take()
                    self.bit = bit
                    return [(self, "moved", rows, n_seq * bit)]

            outs = [OutRows(second[2 * layers - 1 + i]) for i in range(layers)]
            streams = [
                Stream(x)
                for x in (second[0], shrink_weight[0], second[1], second[2], shrink_weight[1])
            ]
            expand_0, shrink_0, qkv_1, expand_1, shrink_1 = streams
            shard = settle(shard, launch(first_stream.far(), shard))
            moving = launch(first_stream.middle(), first_stream.came)
            out_y = launch(outs[0].step(1), first_stream.came)
            settle(shard, moving)
            gate = first_stream.near
            moving = launch(first_stream.last(), first_stream.y_line)
            settle(shard, out_y)
            moving += launch(expand_0.far() + outs[0].step(2), gate)
            group = settle(group, moving)
            qkv_first, _, small_full, small_heads, small_inner = first_stream.whole(
                (block_rows, 16), (pairs_here, layers, dim, own_hidden)
            )
            head_bias, hidden_bias = small_heads[:layers], small_inner[:layers]

            def vector_of(layer, j):
                return small_full[j % 6, layers * (j // 6) + layer]

        else:
            small = lax.all_gather(
                jnp.concatenate(list(small_full) + [expand_bias], axis=1), AXES, axis=0, tiled=False
            )
            full = small[:, :, : 8 * part].reshape(n_dev, layers, 8, part).transpose(1, 2, 0, 3)
            hidden_bias = small[:, :, 8 * part :].transpose(1, 0, 2)
            group = gather_seq(tokens)
            full = full.reshape(layers, 8, dim).astype(F32)
            by_column = full[:, :2].reshape(layers, 2, pairs_here, n_seq, 2 * HEAD)
            by_column = lax.dynamic_index_in_dim(by_column, seq, 3, keepdims=False)
            by_column = by_column.reshape(layers, 2, width)
            head_bias = jnp.concatenate(
                [by_column[:, 0], jnp.zeros((layers, width), F32), by_column[:, 1]], axis=1
            )
            hidden_bias = hidden_bias.reshape(layers, n_dp, n_seq, hidden_part)
            hidden_bias = lax.dynamic_index_in_dim(hidden_bias, seq, 2, keepdims=False)
            hidden_bias = hidden_bias.reshape(layers, own_hidden).astype(F32)

            def vector_of(layer, j):
                return full[layer, j]

        if special:
            out_all = []
        else:
            whole_out = lax.all_gather(out_weight, AXES, axis=1, tiled=True)
            cut = whole_out.reshape(layers, pairs_here, n_seq, 2 * HEAD, dim)
            cut = lax.dynamic_index_in_dim(cut, seq, 2, keepdims=False)
            out_all = [cut[layer].reshape(width, dim) for layer in range(layers)]

        if special:
            qkv_all, expand_all, shrink_all = [qkv_first], [], []

            def beside_of(layer, point):
                if (layer, point) == (0, "attend"):
                    return expand_0.middle() + outs[0].step(4)
                if (layer, point) == (0, "out"):
                    out_all.append(outs[0].take())
                    return expand_0.last() + shrink_0.far()
                if (layer, point) == (0, "normed"):
                    return shrink_0.middle() + expand_0.ready((block_rows,))
                if (layer, point) == (0, "active"):
                    expand_all.append(expand_0.full)
                    return shrink_0.last() + qkv_1.far()
                if (layer, point) == (0, "shrink"):
                    shrink_all.append(shrink_0.whole((hidden_part,))[0])
                    return qkv_1.middle() + outs[1].step(1)
                if (layer, point) == (1, "group"):
                    return qkv_1.last() + expand_1.far() + outs[1].step(2)
                if (layer, point) == (1, "attend"):
                    qkv_all.append(qkv_1.whole((block_rows,))[0])
                    return outs[1].step(4) + expand_1.middle()
                if (layer, point) == (1, "out"):
                    out_all.append(outs[1].take())
                    return expand_1.last() + shrink_1.far()
                if (layer, point) == (1, "normed"):
                    return shrink_1.middle() + expand_1.ready((block_rows,))
                if (layer, point) == (1, "active"):
                    expand_all.append(expand_1.full)
                    return shrink_1.last()
                if (layer, point) == (1, "shrink"):
                    shrink_all.append(shrink_1.whole((hidden_part,))[0])
                return []
        else:
            qkv_all, expand_all, shrink_all = [], [], []

            def beside_of(layer, point):
                return []

            for layer in range(layers):
                mine = exchange_seq(qkv_split(layer))
                mine = lax.all_gather(jnp.concatenate(mine, axis=0), "dp", axis=0, tiled=True)
                qkv_all.append(mine)
                mine = [jnp.concatenate(b, axis=1) for b in hidden_split(expand_weight[layer])]
                mine = jnp.concatenate(exchange_seq(mine), axis=0)
                expand_all.append(lax.all_gather(mine, "dp", axis=0, tiled=True))
                shrink_all.append(lax.all_gather(shrink_weight[layer], "dp", axis=0, tiled=True))

        starts_here = doc_start[0].reshape(n_seq, rows_here)
        starts = jnp.concatenate(
            [
                lax.dynamic_index_in_dim(starts_here, seq ^ step, 0, keepdims=False)
                for step in seq_steps
            ]
        )

        def norm_parts(resid):
            center = resid - jnp.mean(resid, axis=-1, keepdims=True)
            inverse = lax.rsqrt(jnp.mean(center * center, axis=-1, keepdims=True) + EPSILON)
            return center * inverse, inverse

        def norm_back(upstream, gain, rhat, inverse):
            scaled = upstream * gain
            mean_one = jnp.mean(scaled, axis=-1, keepdims=True)
            mean_two = jnp.mean(scaled * rhat, axis=-1, keepdims=True)
            grad = (scaled - mean_one - rhat * mean_two) * inverse
            return grad, jnp.sum(upstream * rhat, axis=0), jnp.sum(upstream, axis=0)

        def column_sums(matrix):
            return jnp.sum(matrix.astype(F32), axis=0)

        kept = []
        for layer in range(layers):
            _, _, out_b, gain_one, bias_one, shrink_b, gain_two, bias_two = (
                vector_of(layer, i) for i in range(8)
            )
            if layer:
                group = gather_seq(hidden_now.astype(BF), beside_of(layer, "group"), summed)
            moving = launch(beside_of(layer, "attend"), group)
            qkv = (dot(group, qkv_all[layer]) + head_bias[layer]).astype(BF)
            attended, row_max, row_sum = attend(qkv, starts)
            attended = settle(attended, moving)
            moves = beside_of(layer, "out")
            summed = reduce_seq(attended, (out_all[layer], (1, 0)), moves)
            resid_one = hidden_now + (summed + out_b)
            rhat_one, inverse_one = norm_parts(resid_one)
            normed = rhat_one * gain_one + bias_one
            normed_group = gather_seq(normed.astype(BF), beside_of(layer, "normed"), summed)
            moves = beside_of(layer, "active")
            moving = launch(moves, moves[0][2] if moves else normed_group)
            inner = dot(normed_group, expand_all[layer]) + hidden_bias[layer]
            cdf = 0.5 * (1.0 + lax.erf(inner * math.sqrt(0.5)))
            active = (inner * cdf).astype(BF)
            slope = cdf + inner * jnp.exp(-0.5 * inner * inner) * (1.0 / math.sqrt(2 * math.pi))
            active = settle(active, moving)
            moves = beside_of(layer, "shrink")
            summed = reduce_seq(active, (shrink_all[layer], (1, 0)), moves)
            resid_two = normed + (summed + shrink_b)
            rhat_two, inverse_two = norm_parts(resid_two)
            hidden_now = rhat_two * gain_two + bias_two
            kept.append(
                (group, qkv, attended, row_max, row_sum, rhat_one, inverse_one, normed_group,
                 active, slope, rhat_two, inverse_two)
            )
        encoded = hidden_now.astype(BF)

        local_index = match_index[0] - seq * rows_here
        picker = local_index[:, None] == jnp.arange(rows_here, dtype=jnp.int32)[None, :]
        chosen = dot(picker.astype(BF), encoded)
        query_vecs = queries[0].astype(F32)
        scores = jnp.sum(query_vecs * chosen, axis=-1)[None, :]
        lexical = jnp.sum(
            encoded.astype(F32) * lexical_weight.astype(F32)[None, :], axis=-1
        ) + lexical_bias.astype(F32)[0]
        keep_mask = (lexical_ids >= 4).astype(F32)
        local_sums = jnp.stack(
            [
                jnp.sum(keep_mask * jax.nn.softplus(lexical)),
                jnp.sum(keep_mask * jax.nn.sigmoid(lexical)),
            ]
        )
        weighted = score_cot[0][:, None] * query_vecs
        grad_now = encoded_cot.astype(F32) + lax.dot_general(
            picker.astype(F32), weighted, (((0,), (0,)), ((), ())), precision=HIGHEST
        )

        def scatter_dp(grad):
            return lax.psum_scatter(grad, "dp", scatter_dimension=0, tiled=True)

        class Sums:
            def __init__(self, grads, rows=block_rows):
                self.blocks = [g.reshape(2, 2, 2, rows, g.shape[-1]) for g in grads]

            def first(self):
                low, up = bit_of(dp, 2) == 1, bit_of(dp, 1) == 1

                def of(flip_low, flip_up):
                    parts = []
                    for b in self.blocks:
                        b = jnp.where(low ^ flip_low, b[:, 1], b[:, 0])
                        parts.append(jnp.where(up ^ flip_up, b[:, 1], b[:, 0]))
                    return jnp.concatenate(parts, axis=-1)

                self.of = of
                self.keep = of(True, False)
                return [(self, "came", of(True, True), n_seq)]

            def middle(self):
                total = (self.keep.astype(F32) + self.came.astype(F32)).astype(BF)
                self.keep = self.of(False, False)
                return [
                    (self, "near", total, 2 * n_seq),
                    (self, "came", self.of(False, True), n_seq),
                ]

            def last(self):
                total = (
                    self.keep.astype(F32) + self.came.astype(F32) + self.near.astype(F32)
                ).astype(BF)
                high = bit_of(dp, 4) == 1
                self.keep = jnp.where(high, total[1], total[0])
                return [(self, "came", jnp.where(high, total[0], total[1]), 4 * n_seq)]

            def rows(self):
                return self.keep.astype(F32) + self.came.astype(F32)

        def scatter_out(grad):
            if not special:
                placed = grad.reshape(pairs_here, 1, 2 * HEAD, dim)
                hot = (jnp.arange(n_seq) == seq)[None, :, None, None]
                placed = jnp.where(hot, placed, jnp.zeros_like(placed)).reshape(dim, dim)
                return lax.psum_scatter(placed, AXES, scatter_dimension=0, tiled=True)
            return None

        def unsplit(pieces, size):
            count = pieces[0].shape[1] // size
            return jnp.concatenate(
                [pieces[s][:, i * size : (i + 1) * size] for i in range(count) for s in range(n_seq)],
                axis=1,
            )

        class Grads:
            pass

        class Back:
            def __init__(self, blocks):
                pieces = by_origin(blocks)
                self.step_0, self.pieces = pieces[0], pieces

            def moves(self):
                return [(self, "step_%d" % i, self.pieces[i], i) for i in range(1, n_seq)]

            def got(self):
                return [getattr(self, "step_%d" % i) for i in range(n_seq)]

        class Table:
            def __init__(self, rows, more):
                self.keep, self.more = rows, more
                self.bits = [4 * n_seq, 2 * n_seq, n_seq] + seq_bits

            def take(self):
                if hasattr(self, "came"):
                    self.keep = self.keep + self.came

            def step(self):
                self.take()
                bit = self.bits.pop(0)
                sent = self.keep
                if bit >= n_seq:
                    middle = self.keep.shape[1] // 2
                    low, up = self.keep[:, :middle], self.keep[:, middle:]
                    chosen = bit_of(dp, bit // n_seq) == 1
                    sent, self.keep = jnp.where(chosen, low, up), jnp.where(chosen, up, low)
                elif bit == seq_bits[0]:
                    columns = self.keep.shape[1]
                    more = jnp.pad(self.more, ((0, 0), (0, columns - self.more.shape[1])))
                    sent = self.keep = jnp.concatenate([self.keep, more], axis=0)
                return [(self, "came", sent, bit)]

        def rows_back(scattered):
            return exchange_steps([scattered[s * part : (s + 1) * part] for s in range(n_seq)])

        def columns_row(vector):
            hot = (jnp.arange(n_seq) == seq)[None, :, None]
            return jnp.where(hot, vector.reshape(pairs_here, 1, 2 * HEAD), 0.0).reshape(1, dim)

        def hidden_rows(vector):
            hot = (jnp.arange(n_seq) == seq)[:, None]
            return jnp.where(hot, vector[None, :], 0.0)

        def reduce_rows(rows, extra=None):
            unit = n_dp
            while unit > 1:
                unit //= 2
                middle = rows.shape[1] // 2
                keep, got = halve(
                    (rows[:, :middle], rows[:, middle:]), bit_of(dp, unit), unit * n_seq
                )
                rows = keep + got
            if extra is not None:
                extra = jnp.pad(extra, ((0, 0), (0, rows.shape[1] - extra.shape[1])))
                rows = jnp.concatenate([rows, extra], axis=0)
            for bit in seq_bits:
                rows = rows + swap(rows, bit)
            return rows

        def own_part(row):
            return lax.dynamic_slice_in_dim(row, seq * part, part)

        big = [None] * layers
        vectors, inner_vectors = [None] * layers, [None] * layers
        lex_row = jnp.zeros((1, n_dp, dim // n_dp), F32).at[0, :, :2].set(local_sums)
        lex_row = lex_row.reshape(1, dim)
        for layer in reversed(range(layers)):
            gain_one, gain_two = vector_of(layer, 3), vector_of(layer, 6)
            (group, qkv, attended, row_max, row_sum, rhat_one, inverse_one, normed_group,
             active, slope, rhat_two, inverse_two) = kept[layer]
            grad_second, fgain, fbias = norm_back(grad_now, gain_two, rhat_two, inverse_two)
            low_second = grad_second.astype(BF)

            def token_rows():
                return jnp.stack(
                    [column_sums(low_first), ngain, nbias, column_sums(low_second), fgain, fbias]
                )

            def layer_rows():
                vectors[0], inner_vectors[0] = token_rows(), hidden_rows(column_sums(low_inner))
                return jnp.concatenate(vectors + [lex_row] + inner_vectors, axis=0)

            above = big[layer + 1] if special and layer + 1 < layers else None
            moves = above.expand.last() + above.qkv.first() if above else []
            second_group = gather_seq(low_second, moves, grad_now)
            low_inner = (dot(second_group, shrink_all[layer], 1, 1) * slope).astype(BF)
            shrink_grad = dot(active, second_group, 0, 0).astype(BF)
            expand_grad = dot(normed_group, low_inner, 0, 0).astype(BF)
            if special:
                big[layer] = mine = Grads()
                mine.shrink, mine.expand = Sums([shrink_grad]), Sums([expand_grad])
                moves = above.qkv.middle() if above else mine.shrink.first()
            else:
                moves = []
            summed = reduce_seq(low_inner, (expand_all[layer], (1, 1)), moves)
            grad_normed = grad_second + summed
            grad_first, ngain, nbias = norm_back(grad_normed, gain_one, rhat_one, inverse_one)
            low_first = grad_first.astype(BF)
            if special:
                moves = above.qkv.last() + mine.shrink.first() if above else mine.shrink.middle()
            first_group = gather_seq(low_first, moves, summed)
            if special:
                moves = mine.shrink.middle() if above else mine.shrink.last() + mine.expand.first()
                moving = launch(moves, first_group)
            low_attn = dot(first_group, out_all[layer], 1, 1).astype(BF)
            out_grad = dot(attended, first_group, 0, 0).astype(BF)
            if special:
                quarter = dim // n_seq
                pieces = exchange_steps(
                    [out_grad[:, s * quarter : (s + 1) * quarter] for s in range(n_seq)]
                )
                pieces = [p.reshape(pairs_here, 1, 2 * HEAD, quarter) for p in by_origin(pieces)]
                out_columns = jnp.concatenate(pieces, axis=1).reshape(dim, quarter)
            grad_qkv = attend_back(qkv, starts, row_max, row_sum, low_attn)
            if special:
                grad_qkv = settle(grad_qkv, moving)
            qkv_grad = dot(group, grad_qkv, 0, 0).astype(BF)
            qkv_sums = column_sums(grad_qkv)
            if special:
                joined = [qkv_grad, out_columns]
                extra = 0
                if layer == 0:
                    extra = 16
                    rows = jnp.concatenate(
                        [
                            qkv_sums[:width].reshape(pairs_here, 2 * HEAD),
                            qkv_sums[2 * width :].reshape(pairs_here, 2 * HEAD),
                        ],
                        axis=1,
                    )
                    hot = (jnp.arange(n_seq) == seq)[None, :, None]
                    rows = jnp.where(hot, rows[:, None, :], 0.0).reshape(n_dp, 1, 4 * HEAD)
                    rows = jnp.pad(rows, ((0, 0), (0, 15), (0, 3 * width - 4 * HEAD))).astype(BF)
                    joined = [
                        jnp.pad(g.reshape(n_dp, block_rows, -1), ((0, 0), (0, 16), (0, 0)))
                        for g in joined
                    ]
                    joined[0] = jnp.concatenate([joined[0][:, :block_rows], rows], axis=1)
                mine.qkv = Sums(joined, block_rows + extra)
                if layer:
                    moves = mine.expand.middle()
                else:
                    table = Table(layer_rows(), scores)
                    moves = mine.shrink.last() + mine.qkv.first() + table.step()
            else:
                moves = []
            summed = reduce_seq(after(grad_qkv, qkv_grad), (qkv_all[layer], (1, 1)), moves)
            if special and layer == 0:

                def back_of(grads, extra=0):
                    grads = [g.astype(BF) for g in grads]
                    blocks = []
                    for s in range(n_seq):
                        rows = [g[s * part : (s + 1) * part] for g in grads]
                        if extra:
                            rows = [jnp.concatenate([r, g[block_rows:]], axis=0) for r, g in zip(rows, grads)]
                        blocks.append(jnp.concatenate(rows, axis=1) if len(rows) > 1 else rows[0])
                    return Back(blocks)

                backs = [None] + [back_of([m.expand.rows(), m.qkv.rows()]) for m in big[1:]]
                moves = mine.qkv.middle() + table.step()
                gate = settle(summed, launch(moves, summed))
                moves = mine.qkv.last() + mine.expand.first() + table.step()
                gate = settle(gate, launch(moves, gate))
                backs[0] = back_of([mine.qkv.rows()], 16)
                moves = mine.expand.middle() + backs[0].moves()
                gate = settle(gate, launch(moves, gate))
                moves = mine.expand.last() + table.step()
                for back in backs[1:]:
                    moves += back.moves()
                gate = settle(gate, launch(moves, gate))
                last_back = back_of([mine.expand.rows()])
                settle(gate, launch(last_back.moves() + table.step(), gate))
            if not special:
                big[layer] = (
                    scatter_dp(shrink_grad),
                    scatter_dp(expand_grad),
                    scatter_out(out_grad),
                    scatter_dp(qkv_grad),
                )
            grad_now = grad_first + summed
            head_rows = [columns_row(qkv_sums[:width]), columns_row(qkv_sums[2 * width :])]
            if layer or not special:
                vectors[layer] = token_rows()
                if layer:
                    vectors[layer] = jnp.concatenate([vectors[layer]] + head_rows, axis=0)
                inner_vectors[layer] = hidden_rows(column_sums(low_inner))

        tokens_grad = grad_now.astype(BF)

        counts = [v.shape[0] for v in vectors] + [1] + [n_seq] * layers
        if special:
            table.take()
            table = table.keep
            scores = table[-1:, : scores.shape[1]]
        else:
            table = reduce_rows(jnp.concatenate(vectors + [lex_row], axis=0), scores)
            scores = table[-1:, : scores.shape[1]]
            inner = reduce_rows(jnp.concatenate(inner_vectors, axis=0))
            last = reduce_rows(jnp.concatenate(head_rows, axis=0))
        cut = [0]
        for count in counts:
            cut.append(cut[-1] + count)
        tables = [table[cut[i] : cut[i + 1]] for i in range(len(counts))]
        if special:
            inner_tables = tables[layers + 1 :]
        else:
            inner_tables = [inner[i * n_seq : (i + 1) * n_seq] for i in range(layers)]
        lexical_stats = tables[layers][0, :2] / (rows_here * n_dev)
        inner_out = jnp.stack(
            [lax.dynamic_index_in_dim(t, seq, 0, keepdims=False) for t in inner_tables]
        )

        layer_outs = []
        for layer in range(layers):
            if special:
                shrink_rows = big[layer].shrink.rows()
                got = backs[layer].got()
                if layer:
                    got = by_origin(got)
                    expand_out, got = [g[:, :own_hidden] for g in got], [g[:, own_hidden:] for g in got]
                else:
                    source = seq ^ lax.rem(dp, n_seq)
                    row = got[0][part : part + 1, : 4 * HEAD]
                    for step in range(1, n_seq):
                        row = jnp.where(source == step, got[step][part : part + 1, : 4 * HEAD], row)
                    last = row.reshape(2, 2 * HEAD).astype(F32)
                    got = by_origin([g[:part] for g in got])
                    expand_out = by_origin(last_back.got())
                out_out = jnp.concatenate([g[:, 3 * width :] for g in got], axis=1)
            else:
                shrink_rows, expand_rows, out_out, qkv_rows = big[layer]
                got, expand_out = by_origin(rows_back(qkv_rows)), by_origin(rows_back(expand_rows))
            layer_outs.append(
                [
                    unsplit([g[:, i * width : (i + 1) * width] for g in got], 2 * HEAD)
                    for i in range(3)
                ]
                + [out_out, unsplit(expand_out, hidden_part), shrink_rows]
            )
        def vector_out(index):
            if index < 2:
                return jnp.stack(
                    [own_part(tables[i][6 + index] if i else last[index]) for i in range(layers)]
                )
            return jnp.stack([own_part(tables[i][index - 2]) for i in range(layers)])

        big_out = [jnp.stack([lo[i].astype(F32) for lo in layer_outs]) for i in range(6)]
        return (
            encoded, scores, lexical_stats, tokens_grad,
            big_out[0], vector_out(0), big_out[1], big_out[2], vector_out(1),
            big_out[3], vector_out(2), vector_out(3), vector_out(4),
            big_out[4], inner_out, big_out[5], vector_out(5),
            vector_out(6), vector_out(7),
        )

    rows = P(AXES, None)
    weight = P(None, AXES, None)
    vector = P(None, AXES)
    placed = (
        rows, P("dp", None), P(AXES), P("dp", None, None), P("dp", None),
        weight, vector, weight, weight, vector, weight, vector, vector, vector,
        weight, vector, weight, vector, vector, vector, P(), P(), P("dp", None), rows,
    )
    results = (
        rows, P("dp", None), P(), rows,
        weight, vector, weight, weight, vector, weight, vector, vector, vector,
        weight, vector, weight, vector, vector, vector,
    )
    return jax.shard_map(local, mesh=mesh, in_specs=placed, out_specs=results, check_vma=False)
```

```python
import functools
import math

import jax
import jax.numpy as jnp
from jax import lax
from jax.experimental import pallas as pl
from jax.experimental.pallas import tpu as pltpu
from jax.sharding import PartitionSpec as P

HEAD = 64
EPSILON = 1e-05
NEGATIVE = -1e30
HIGHEST = lax.Precision.HIGHEST
AXES = ("dp", "seq")
BF = jnp.bfloat16
F32 = jnp.float32
VMEM_LIMIT = 56 * 1024 * 1024


def dot(left, right, left_dim=1, right_dim=0):
    return lax.dot_general(
        left, right, (((left_dim,), (right_dim,)), ((), ())), preferred_element_type=F32
    )


def head_lanes(shape, half):
    lane = lax.broadcasted_iota(jnp.int32, shape, 1)
    return (lane < HEAD) if half == 0 else (lane >= HEAD)


def attend_kernel(block, qkv_ref, col_ref, row_ref, out_ref, max_ref, sum_ref):
    tokens, width = out_ref.shape
    pairs = width // (2 * HEAD)
    scale = 1.0 / math.sqrt(HEAD)
    for pair in range(pairs):
        lo = pair * 2 * HEAD
        keys = qkv_ref[:, width + lo : width + lo + 2 * HEAD]
        values = qkv_ref[:, 2 * width + lo : 2 * width + lo + 2 * HEAD]
        values_t = values.astype(F32).T.astype(BF)
        for start in range(0, tokens, block):
            queries = qkv_ref[start : start + block, lo : lo + 2 * HEAD] * scale
            queries = queries.astype(BF)
            same = col_ref[...] == row_ref[:, start : start + block]
            halves = []
            for half in range(2):
                lanes = head_lanes(queries.shape, half)
                scores = dot(keys, jnp.where(lanes, queries, jnp.zeros_like(queries)), 1, 1)
                scores = jnp.where(same, scores, NEGATIVE)
                top = jnp.max(scores, axis=0, keepdims=True)
                raised = jnp.exp(scores - top)
                total = jnp.sum(raised, axis=0, keepdims=True)
                probs = (raised * (1.0 / total)).astype(BF)
                mixed = dot(values_t, probs)
                halves.append(mixed[half * HEAD : (half + 1) * HEAD])
                head = 2 * pair + half
                max_ref[head : head + 1, start : start + block] = top
                sum_ref[head : head + 1, start : start + block] = total
            joined = jnp.concatenate(halves, axis=0)
            out_ref[start : start + block, lo : lo + 2 * HEAD] = joined.T.astype(BF)


def attend_back_kernel(
    block, qkv_ref, col_ref, row_ref, max_ref, sum_ref, grad_ref, out_ref, key_acc, value_acc
):
    tokens, width = grad_ref.shape
    pairs = width // (2 * HEAD)
    scale = 1.0 / math.sqrt(HEAD)
    for pair in range(pairs):
        lo = pair * 2 * HEAD
        keys = qkv_ref[:, width + lo : width + lo + 2 * HEAD]
        values = qkv_ref[:, 2 * width + lo : 2 * width + lo + 2 * HEAD]
        keys_t = keys.astype(F32).T.astype(BF)
        key_acc[...] = jnp.zeros_like(key_acc)
        value_acc[...] = jnp.zeros_like(value_acc)
        for start in range(0, tokens, block):
            queries = (qkv_ref[start : start + block, lo : lo + 2 * HEAD] * scale).astype(BF)
            grads = grad_ref[start : start + block, lo : lo + 2 * HEAD]
            same = col_ref[...] == row_ref[:, start : start + block]
            halves = []
            for half in range(2):
                lanes = head_lanes(queries.shape, half)
                own_queries = jnp.where(lanes, queries, jnp.zeros_like(queries))
                own_grads = jnp.where(lanes, grads, jnp.zeros_like(grads))
                head = 2 * pair + half
                top = max_ref[head : head + 1, start : start + block]
                total = sum_ref[head : head + 1, start : start + block]
                scores = dot(keys, own_queries, 1, 1)
                scores = jnp.where(same, scores, NEGATIVE)
                probs = jnp.exp(scores - top) * (1.0 / total)
                grad_probs = dot(values, own_grads, 1, 1)
                shared = jnp.sum(probs * grad_probs, axis=0, keepdims=True)
                grad_scores = (probs * (grad_probs - shared)).astype(BF)
                value_acc[...] += dot(probs.astype(BF), own_grads)
                key_acc[...] += dot(grad_scores, own_queries)
                mixed = dot(keys_t, grad_scores)
                halves.append(mixed[half * HEAD : (half + 1) * HEAD])
            joined = jnp.concatenate(halves, axis=0) * scale
            out_ref[start : start + block, lo : lo + 2 * HEAD] = joined.T.astype(BF)
        out_ref[:, width + lo : width + lo + 2 * HEAD] = key_acc[...].astype(BF)
        out_ref[:, 2 * width + lo : 2 * width + lo + 2 * HEAD] = value_acc[...].astype(BF)


def attend(qkv, starts):
    tokens, width = qkv.shape[0], qkv.shape[1] // 3
    heads = width // HEAD
    whole = pl.BlockSpec(memory_space=pltpu.VMEM)
    return pl.pallas_call(
        functools.partial(attend_kernel, math.gcd(tokens, 768)),
        out_shape=(
            jax.ShapeDtypeStruct((tokens, width), BF),
            jax.ShapeDtypeStruct((heads, tokens), F32),
            jax.ShapeDtypeStruct((heads, tokens), F32),
        ),
        in_specs=[whole] * 3,
        out_specs=(whole,) * 3,
        compiler_params=pltpu.CompilerParams(vmem_limit_bytes=VMEM_LIMIT),
        cost_estimate=pl.CostEstimate(
            flops=40 * tokens * tokens * width, bytes_accessed=16 * tokens * width, transcendentals=0
        ),
    )(qkv, starts[:, None], starts[None, :])


def attend_back(qkv, starts, row_max, row_sum, grads):
    tokens, width = grads.shape
    whole = pl.BlockSpec(memory_space=pltpu.VMEM)
    return pl.pallas_call(
        functools.partial(attend_back_kernel, math.gcd(tokens, 768)),
        out_shape=jax.ShapeDtypeStruct((tokens, 3 * width), BF),
        in_specs=[whole] * 6,
        out_specs=whole,
        scratch_shapes=[
            pltpu.VMEM((tokens, 2 * HEAD), F32),
            pltpu.VMEM((tokens, 2 * HEAD), F32),
        ],
        compiler_params=pltpu.CompilerParams(vmem_limit_bytes=VMEM_LIMIT),
        cost_estimate=pl.CostEstimate(
            flops=40 * tokens * tokens * width, bytes_accessed=16 * tokens * width, transcendentals=0
        ),
    )(qkv, starts[:, None], starts[None, :], row_max, row_sum, grads)


def place_rows(order, sizes, pieces, outs):
    me = lax.axis_index("dp")
    for steps, piece in zip(order, pieces):
        first = 0
        for step in steps:
            if isinstance(step, tuple):
                where = step[0] * 2 + (lax.rem(me, 2) ^ step[1])
            else:
                where = me ^ step
            for member, rows in enumerate(sizes):
                at = pl.multiple_of(where * rows, rows)
                outs[member][pl.ds(at, rows), :] = piece[first : first + rows, :]
                first += rows


def place_kernel(order, sizes, *refs):
    place_rows(order, sizes, refs[: len(order)], refs[len(order) :])


def place_first_kernel(order, sizes, pairs, layers, *refs):
    pieces, (weights, smalls, full, heads, inner) = refs[: len(order)], refs[len(order) :]
    place_rows(order, sizes, pieces, (weights, smalls))
    seq, n_seq = lax.axis_index("seq"), 4
    n_dp = smalls.shape[0] // 16
    lane = lax.broadcasted_iota(jnp.int32, (4, 128), 1)
    for dp in range(n_dp):
        rows = smalls[dp * 16 : dp * 16 + 16, :].astype(F32)
        for block in range(6):
            part = rows[:, block * 128 : block * 128 + 128]
            total = part[:4]
            for s in range(1, n_seq):
                moved = pltpu.roll(part, 32 * s, 1)[4 * s : 4 * s + 4]
                total = jnp.where(lane // 32 == s, moved, total)
            full[block, 0:4, dp * 128 : dp * 128 + 128] = total
            if block == 2:
                own = part[:4]
                for s in range(1, n_seq):
                    own = jnp.where(seq == s, part[4 * s : 4 * s + 4], own)
                inner[0:layers, dp * 128 : dp * 128 + 128] = own[layers : 2 * layers]
    heads[...] = jnp.zeros_like(heads)
    width = pairs * 128
    for which, base in ((0, 0), (1, 2 * width)):
        for pair in range(pairs):
            column = pl.multiple_of((pair * n_seq + seq) * 128, 128)
            heads[0:layers, base + pair * 128 : base + pair * 128 + 128] = full[
                which, 0:layers, pl.ds(column, 128)
            ]


def place(pieces, order, sizes, unpack=None):
    columns = pieces[0].shape[1]
    order = tuple(tuple(o) if isinstance(o, (list, tuple)) else (o,) for o in order)
    count = sum(len(o) for o in order)
    whole = pl.BlockSpec(memory_space=pltpu.VMEM)
    shapes = [jax.ShapeDtypeStruct((count * rows, columns), BF) for rows in sizes]
    body = functools.partial(place_kernel, order, tuple(sizes))
    if unpack is not None:
        pairs, layers, dim, inner = unpack
        shapes += [
            jax.ShapeDtypeStruct((6, 8, dim), F32),
            jax.ShapeDtypeStruct((8, pairs * 3 * 128), F32),
            jax.ShapeDtypeStruct((8, inner), F32),
        ]
        body = functools.partial(place_first_kernel, order, tuple(sizes), pairs, layers)
    return pl.pallas_call(
        body,
        out_shape=tuple(shapes),
        in_specs=[whole] * len(pieces),
        out_specs=(whole,) * len(shapes),
        compiler_params=pltpu.CompilerParams(vmem_limit_bytes=VMEM_LIMIT),
        cost_estimate=pl.CostEstimate(flops=0, bytes_accessed=0, transcendentals=0),
    )(*pieces)


def split_kernel(n_seq, plan, part, smalls, *refs):
    n_in = 1 + max(p[0] for p in plan)
    weights, rest = refs[:n_in], refs[n_in:]
    small_refs, rest = rest[:smalls], rest[smalls:]
    outs = rest[:n_seq]
    seq = lax.axis_index("seq")
    if smalls:
        table = rest[n_seq]
        table[...] = jnp.zeros_like(table)
        across = table.shape[1] // 128
        for j, small in enumerate(small_refs):
            row, lane = 2 * (j // across), 128 * (j % across)
            table[row : row + 2, lane : lane + small.shape[1]] = small[...].astype(F32)
    for step in range(n_seq):
        target = seq ^ step
        at = 0
        for ref, layer, block, count in plan:
            if not count:
                outs[step][:part, at : at + block] = weights[ref][layer]
                at += block
            for i in range(count):
                column = pl.multiple_of((i * n_seq + target) * block, 128)
                outs[step][:part, at : at + block] = weights[ref][layer, :, pl.ds(column, block)]
                at += block
        if smalls:
            outs[step][part:, :] = table[...].astype(BF)


def split_weights(weights, plan, n_seq, smalls=()):
    part = weights[0].shape[1]
    columns = sum(block * max(count, 1) for _, _, block, count in plan)
    rows = part + (16 if smalls else 0)
    whole = pl.BlockSpec(memory_space=pltpu.VMEM)
    return pl.pallas_call(
        functools.partial(split_kernel, n_seq, tuple(plan), part, len(smalls)),
        out_shape=tuple(jax.ShapeDtypeStruct((rows, columns), BF) for _ in range(n_seq)),
        in_specs=[whole] * (len(weights) + len(smalls)),
        out_specs=(whole,) * n_seq,
        scratch_shapes=[pltpu.VMEM((16, columns), F32)] if smalls else [],
        compiler_params=pltpu.CompilerParams(vmem_limit_bytes=VMEM_LIMIT),
    )(*weights, *smalls)


def join_kernel(n_seq, part, cuts, with_small, extra, *refs):
    pieces, rest = refs[:n_seq], refs[n_seq:]
    if extra:
        extra_ref, rest = rest[0], rest[1:]
    outs = rest[: len(cuts)]
    seq = lax.axis_index("seq")
    for step in range(n_seq):
        row = pl.multiple_of((seq ^ step) * part, part)
        at = 0
        for out, columns in zip(outs, cuts):
            out[pl.ds(row, part), :] = pieces[step][:part, at : at + columns]
            at += columns
    if with_small:
        table = rest[len(cuts)]
        smalls = [pieces[step][part:, :].astype(F32)[:4] for step in range(n_seq)]
        for origin in range(n_seq):
            total = jnp.zeros_like(smalls[0])
            for step in range(n_seq):
                total = jnp.where((seq ^ step) == origin, smalls[step], total)
            table[4 * origin : 4 * origin + 4, :] = total
        outs[0][n_seq * part :, :] = table[...].astype(BF)
    if extra:
        outs[0][n_seq * part :, :] = extra_ref[0]


def join_pieces(pieces, part, cuts, with_small=False, extra=None):
    n_seq = len(pieces)
    rows = [n_seq * part] * len(cuts)
    if with_small:
        rows[0] += 4 * n_seq
    if extra is not None:
        rows[0] += extra.shape[1]
    whole = pl.BlockSpec(memory_space=pltpu.VMEM)
    more = [] if extra is None else [extra]
    return pl.pallas_call(
        functools.partial(
            join_kernel, n_seq, part, tuple(cuts), with_small, extra is not None
        ),
        out_shape=tuple(jax.ShapeDtypeStruct((r, c), BF) for r, c in zip(rows, cuts)),
        in_specs=[whole] * (n_seq + len(more)),
        out_specs=(whole,) * len(cuts),
        scratch_shapes=[pltpu.VMEM((4 * n_seq, cuts[0]), F32)] if with_small else [],
        compiler_params=pltpu.CompilerParams(vmem_limit_bytes=VMEM_LIMIT),
    )(*pieces, *more)


def after(array, *others):
    return lax.optimization_barrier((array,) + others)[0] if others else array


def solution(mesh):
    n_dp, n_seq = mesh.shape["dp"], mesh.shape["seq"]
    n_dev = n_dp * n_seq
    special = (n_dp, n_seq) == (8, 4)

    def swap(array, bit):
        return lax.ppermute(array, AXES, [(p, p ^ bit) for p in range(n_dev)])

    def bits_of(count, unit=1):
        bits = []
        while count > 1:
            bits.append(unit)
            unit, count = unit * 2, count // 2
        return bits

    seq_bits, dp_bits = bits_of(n_seq), bits_of(n_dp, n_seq)

    z_lines = [[d for d in range(n_dp) if d % 2 == y] for y in range(2)]

    x_steps = [0]
    for bit in reversed(seq_bits[1:]):
        x_steps = x_steps + [s ^ bit for s in x_steps]
    seq_steps = [step ^ core for step in x_steps for core in (0, 1)]

    def spread(piece, bits):
        pieces, steps = [piece], [0]
        for bit in reversed(bits):
            pieces = pieces + [swap(p, bit) for p in pieces]
            steps = steps + [s ^ bit for s in steps]
        return pieces, steps

    def launch(moves, gate):
        return [
            (home, name, swap(after(array, gate), bit) if bit else array)
            for home, name, array, bit in moves
        ]

    def settle(array, moving):
        if not moving:
            return array
        arrays = tuple(array) if isinstance(array, (tuple, list)) else (array,)
        out = lax.optimization_barrier(arrays + tuple(m[2] for m in moving))
        for (home, name, _), value in zip(moving, out[len(arrays) :]):
            setattr(home, name, value)
        return list(out[: len(arrays)]) if isinstance(array, (tuple, list)) else out[0]

    def gather_seq(rows, moves=(), gate=None):
        moving = launch(moves, rows if gate is None else gate)
        pieces = [rows]
        for bit in reversed(seq_bits[1:]):
            came = [swap(p, bit) for p in pieces]
            came[0] = settle(came[0], moving)
            moving = []
            pieces = pieces + came
        pairs = [jnp.concatenate([p, swap(p, 1)], axis=0) for p in pieces]
        return pairs[0], (jnp.concatenate(pairs[1:], axis=0) if len(pairs) > 2 else pairs[1])

    def both(halves):
        return jnp.concatenate(halves, axis=0)

    def reduce_seq(left, right, moves=(), gate=None):
        near, far = left
        moving = launch(moves, far if gate is None else gate)
        size = near.shape[0] // 2

        def chip(rows, own):
            parts = right(rows, own) if callable(right) else dot(rows, right[0], *right[1])
            return parts[:size] + swap(parts[size:].astype(BF), 1).astype(F32)

        total = [None] + [
            chip(far[i * 2 * size : (i + 1) * 2 * size], False) for i in range(len(x_steps) - 1)
        ]
        for i, bit in enumerate(seq_bits[1:]):
            middle = len(total) // 2
            got = [swap(t.astype(BF), bit) for t in total[middle:]]
            if i + 2 == len(seq_bits):
                got[0] = settle(got[0], moving)
            if total[0] is None:
                total[0] = chip(near, True)
            total = [a + b.astype(F32) for a, b in zip(total[:middle], got)]
        return total[0]

    def halve(array, index_bit, bit):
        chosen = index_bit.astype(jnp.bool_)
        send = jnp.where(chosen, array[0], array[1])
        keep = jnp.where(chosen, array[1], array[0])
        return keep, swap(send, bit)

    def local(
        tokens, doc_start, lexical_ids, queries, match_index,
        query_weight, query_bias, key_weight, value_weight, value_bias,
        out_weight, out_bias, norm_gain, norm_bias, expand_weight, expand_bias,
        shrink_weight, shrink_bias, final_gain, final_bias,
        lexical_weight, lexical_bias, score_cot, encoded_cot,
    ):
        layers, part, dim = query_weight.shape
        hidden_dim = expand_weight.shape[2]
        hidden_part = shrink_weight.shape[1]
        rows_here = tokens.shape[0]
        pairs_here = dim // (2 * HEAD) // n_seq
        width = pairs_here * 2 * HEAD
        own_hidden = hidden_dim // n_seq
        block_rows = dim // n_dp
        dp, seq = lax.axis_index("dp"), lax.axis_index("seq")
        flat = dp * n_seq + seq

        def bit_of(index, bit):
            return lax.bitwise_and(lax.div(index, bit), 1)

        def by_origin(pieces):
            for bit in seq_bits:
                chosen = bit_of(seq, bit).astype(jnp.bool_)
                pieces = [jnp.where(chosen, pieces[j ^ bit], pieces[j]) for j in range(n_seq)]
            return pieces

        def exchange_steps(blocks):
            pieces = by_origin(blocks)
            return [pieces[0]] + [swap(pieces[step], step) for step in range(1, n_seq)]

        def exchange_seq(blocks):
            return by_origin(exchange_steps(blocks))

        def head_split(weight):
            cut = [weight[:, i * 2 * HEAD : (i + 1) * 2 * HEAD] for i in range(pairs_here * n_seq)]
            return [cut[s::n_seq] for s in range(n_seq)]

        def hidden_split(weight):
            cut = [
                weight[:, i * hidden_part : (i + 1) * hidden_part] for i in range(n_dp * n_seq)
            ]
            return [cut[s::n_seq] for s in range(n_seq)]

        def qkv_split(layer):
            three = [head_split(w[layer]) for w in (query_weight, key_weight, value_weight)]
            return [jnp.concatenate(three[0][s] + three[1][s] + three[2][s], axis=1) for s in range(n_seq)]

        small_full = (
            query_bias, value_bias, out_bias, norm_gain, norm_bias, shrink_bias, final_gain, final_bias,
        )
        three = [query_weight, key_weight, value_weight]
        hidden_now = tokens.astype(F32)
        if special:
            heads_plan = [(i, 0, 2 * HEAD, pairs_here) for i in range(3)]
            sent = split_weights(three, heads_plan, n_seq, small_full + (expand_bias,))
            got = [sent[0]] + [swap(sent[step], step) for step in range(1, n_seq)]
            (shard,) = join_pieces(got, part, (3 * width,), True)
            class Stream:
                def __init__(self, shard):
                    self.shard = shard

                def far(self):
                    return [(self, "came", self.shard, n_seq * 4)]

                def middle(self):
                    self.line = jnp.concatenate([self.shard, self.came], axis=0)
                    return [
                        (self, "near", self.line, n_seq * 2),
                        (self, "y_line", self.line, n_seq),
                    ]

                def last(self):
                    return [(self, "y_near", self.near, n_seq)]

                def ready(self, sizes):
                    return [(self, "full", self.whole(sizes)[0], 0)]

                def whole(self, sizes, unpack=None):
                    pieces = [self.line, self.near, self.y_line, self.y_near]
                    return place(pieces, [[0, 4], [2, 6], [1, 5], [3, 7]], sizes, unpack)

            first_stream = Stream(shard)
            plan = [(3, 0, hidden_part, n_dp)]
            cuts = [own_hidden]
            for layer in range(1, layers):
                plan += [(i, layer, 2 * HEAD, pairs_here) for i in range(3)]
                plan += [(3, layer, hidden_part, n_dp)]
                cuts += [3 * width, own_hidden]
            plan += [(4, layer, dim, 0) for layer in range(layers)]
            cuts += [dim] * layers
            sent = split_weights(three + [expand_weight, out_weight], plan, n_seq)
            sent = [after(p, got[1], got[2], got[3]) for p in sent]
            got = [sent[0]] + [swap(sent[step], step) for step in range(1, n_seq)]
            second = join_pieces(got, part, cuts)
            group = both(gather_seq(after(tokens, *got[2:])))

            class OutRows:
                def __init__(self, rows):
                    self.rows, self.moved, self.bit = rows, None, 0

                def take(self):
                    bit, moved = self.bit, self.moved
                    if bit in (1, 2):
                        here = bit_of(seq, bit) == bit_of(dp, bit)
                        self.rows = jnp.where(here, self.rows, moved)
                    elif bit == 4:
                        upper = bit_of(dp, 4) == 1
                        self.rows = jnp.concatenate(
                            [jnp.where(upper, moved, self.rows), jnp.where(upper, self.rows, moved)],
                            axis=0,
                        )
                    self.bit = 0
                    self.rows = lax.optimization_barrier(self.rows)
                    return self.rows

                def step(self, bit):
                    rows = self.take()
                    self.bit = bit
                    return [(self, "moved", rows, n_seq * bit)]

            outs = [OutRows(second[2 * layers - 1 + i]) for i in range(layers)]
            streams = [
                Stream(x)
                for x in (second[0], shrink_weight[0], second[1], second[2], shrink_weight[1])
            ]
            expand_0, shrink_0, qkv_1, expand_1, shrink_1 = streams
            shard = settle(shard, launch(first_stream.far(), shard))
            moving = launch(first_stream.middle(), first_stream.came)
            out_y = launch(outs[0].step(1), first_stream.came)
            shard = settle(shard, moving[:1])
            moving = moving[1:] + launch(first_stream.last() + expand_0.far(), first_stream.near)
            shard = settle(shard, out_y)
            moving += launch(outs[0].step(2), outs[0].moved)
            group = settle(group, moving)
            qkv_first, _, small_full, small_heads, small_inner = first_stream.whole(
                (block_rows, 16), (pairs_here, layers, dim, own_hidden)
            )
            head_bias, hidden_bias = small_heads[:layers], small_inner[:layers]

            def vector_of(layer, j):
                return small_full[j % 6, layers * (j // 6) + layer]

        else:
            small = lax.all_gather(
                jnp.concatenate(list(small_full) + [expand_bias], axis=1), AXES, axis=0, tiled=False
            )
            full = small[:, :, : 8 * part].reshape(n_dev, layers, 8, part).transpose(1, 2, 0, 3)
            hidden_bias = small[:, :, 8 * part :].transpose(1, 0, 2)
            group = both(gather_seq(tokens))
            full = full.reshape(layers, 8, dim).astype(F32)
            by_column = full[:, :2].reshape(layers, 2, pairs_here, n_seq, 2 * HEAD)
            by_column = lax.dynamic_index_in_dim(by_column, seq, 3, keepdims=False)
            by_column = by_column.reshape(layers, 2, width)
            head_bias = jnp.concatenate(
                [by_column[:, 0], jnp.zeros((layers, width), F32), by_column[:, 1]], axis=1
            )
            hidden_bias = hidden_bias.reshape(layers, n_dp, n_seq, hidden_part)
            hidden_bias = lax.dynamic_index_in_dim(hidden_bias, seq, 2, keepdims=False)
            hidden_bias = hidden_bias.reshape(layers, own_hidden).astype(F32)

            def vector_of(layer, j):
                return full[layer, j]

        if special:
            out_all = []
        else:
            whole_out = lax.all_gather(out_weight, AXES, axis=1, tiled=True)
            cut = whole_out.reshape(layers, pairs_here, n_seq, 2 * HEAD, dim)
            cut = lax.dynamic_index_in_dim(cut, seq, 2, keepdims=False)
            out_all = [cut[layer].reshape(width, dim) for layer in range(layers)]

        if special:
            qkv_all, expand_all, shrink_all = [qkv_first], [], []

            def beside_of(layer, point):
                if (layer, point) == (0, "attend"):
                    return outs[0].step(4) + expand_0.middle()
                if (layer, point) == (0, "out"):
                    out_all.append(outs[0].take())
                    return expand_0.last() + shrink_0.far() + outs[1].step(1)
                if (layer, point) == (0, "normed"):
                    return shrink_0.middle() + expand_0.ready((block_rows,))
                if (layer, point) == (0, "active"):
                    expand_all.append(expand_0.full)
                    return shrink_0.last() + qkv_1.far() + outs[1].step(2)
                if (layer, point) == (0, "shrink"):
                    shrink_all.append(shrink_0.whole((hidden_part,))[0])
                    return qkv_1.middle() + outs[1].step(4)
                if (layer, point) == (1, "group"):
                    return qkv_1.last() + expand_1.far()
                if (layer, point) == (1, "attend"):
                    qkv_all.append(qkv_1.whole((block_rows,))[0])
                    return expand_1.middle()
                if (layer, point) == (1, "out"):
                    out_all.append(outs[1].take())
                    return expand_1.last() + shrink_1.far()
                if (layer, point) == (1, "normed"):
                    return shrink_1.middle() + expand_1.ready((block_rows,))
                if (layer, point) == (1, "active"):
                    expand_all.append(expand_1.full)
                    return shrink_1.last()
                if (layer, point) == (1, "shrink"):
                    shrink_all.append(shrink_1.whole((hidden_part,))[0])
                return []
        else:
            qkv_all, expand_all, shrink_all = [], [], []

            def beside_of(layer, point):
                return []

            for layer in range(layers):
                mine = exchange_seq(qkv_split(layer))
                mine = lax.all_gather(jnp.concatenate(mine, axis=0), "dp", axis=0, tiled=True)
                qkv_all.append(mine)
                mine = [jnp.concatenate(b, axis=1) for b in hidden_split(expand_weight[layer])]
                mine = jnp.concatenate(exchange_seq(mine), axis=0)
                expand_all.append(lax.all_gather(mine, "dp", axis=0, tiled=True))
                shrink_all.append(lax.all_gather(shrink_weight[layer], "dp", axis=0, tiled=True))

        starts_here = doc_start[0].reshape(n_seq, rows_here)
        starts = jnp.concatenate(
            [
                lax.dynamic_index_in_dim(starts_here, seq ^ step, 0, keepdims=False)
                for step in seq_steps
            ]
        )

        def norm_parts(resid):
            center = resid - jnp.mean(resid, axis=-1, keepdims=True)
            inverse = lax.rsqrt(jnp.mean(center * center, axis=-1, keepdims=True) + EPSILON)
            return center * inverse, inverse

        def norm_back(upstream, gain, rhat, inverse):
            scaled = upstream * gain
            mean_one = jnp.mean(scaled, axis=-1, keepdims=True)
            mean_two = jnp.mean(scaled * rhat, axis=-1, keepdims=True)
            grad = (scaled - mean_one - rhat * mean_two) * inverse
            return grad, jnp.sum(upstream * rhat, axis=0), jnp.sum(upstream, axis=0)

        def column_sums(matrix):
            return jnp.sum(matrix.astype(F32), axis=0)

        kept = []
        for layer in range(layers):
            _, _, out_b, gain_one, bias_one, shrink_b, gain_two, bias_two = (
                vector_of(layer, i) for i in range(8)
            )
            if layer:
                group = both(gather_seq(hidden_now.astype(BF), beside_of(layer, "group"), summed))
            moving = launch(beside_of(layer, "attend"), group)
            qkv = (dot(group, qkv_all[layer]) + head_bias[layer]).astype(BF)
            attended, row_max, row_sum = attend(qkv, starts)
            attended = settle(attended, moving)
            moves = beside_of(layer, "out")
            chip_rows = 2 * rows_here
            halves = (attended[:chip_rows], attended[chip_rows:])
            summed = reduce_seq(halves, (out_all[layer], (1, 0)), moves)
            resid_one = hidden_now + (summed + out_b)
            rhat_one, inverse_one = norm_parts(resid_one)
            normed = rhat_one * gain_one + bias_one
            normed_halves = gather_seq(normed.astype(BF), beside_of(layer, "normed"), summed)
            moves = beside_of(layer, "active")
            moving = launch(moves, moves[0][2] if moves else normed_halves[1])
            active, slope = [], []
            for rows in normed_halves:
                inner = dot(rows, expand_all[layer]) + hidden_bias[layer]
                cdf = 0.5 * (1.0 + lax.erf(inner * math.sqrt(0.5)))
                active.append((inner * cdf).astype(BF))
                slope.append(
                    cdf + inner * jnp.exp(-0.5 * inner * inner) * (1.0 / math.sqrt(2 * math.pi))
                )
            active = settle(active, moving)
            moves = beside_of(layer, "shrink")
            summed = reduce_seq(active, (shrink_all[layer], (1, 0)), moves)
            normed_group, active = both(normed_halves), both(active)
            resid_two = normed + (summed + shrink_b)
            rhat_two, inverse_two = norm_parts(resid_two)
            hidden_now = rhat_two * gain_two + bias_two
            kept.append(
                (group, qkv, attended, row_max, row_sum, rhat_one, inverse_one, normed_group,
                 active, slope, rhat_two, inverse_two)
            )
        encoded = hidden_now.astype(BF)

        local_index = match_index[0] - seq * rows_here
        picker = local_index[:, None] == jnp.arange(rows_here, dtype=jnp.int32)[None, :]
        chosen = dot(picker.astype(BF), encoded)
        query_vecs = queries[0].astype(F32)
        scores = jnp.sum(query_vecs * chosen, axis=-1)[None, :]
        lexical = jnp.sum(
            encoded.astype(F32) * lexical_weight.astype(F32)[None, :], axis=-1
        ) + lexical_bias.astype(F32)[0]
        keep_mask = (lexical_ids >= 4).astype(F32)
        local_sums = jnp.stack(
            [
                jnp.sum(keep_mask * jax.nn.softplus(lexical)),
                jnp.sum(keep_mask * jax.nn.sigmoid(lexical)),
            ]
        )
        weighted = score_cot[0][:, None] * query_vecs
        grad_now = encoded_cot.astype(F32) + lax.dot_general(
            picker.astype(F32), weighted, (((0,), (0,)), ((), ())), precision=HIGHEST
        )

        def scatter_dp(grad):
            return lax.psum_scatter(grad, "dp", scatter_dimension=0, tiled=True)

        class Sums:
            def __init__(self, grads, rows=block_rows):
                self.blocks = [g.reshape(2, 2, 2, rows, g.shape[-1]) for g in grads]

            def first(self):
                low, up = bit_of(dp, 2) == 1, bit_of(dp, 1) == 1

                def of(flip_low, flip_up):
                    parts = []
                    for b in self.blocks:
                        b = jnp.where(low ^ flip_low, b[:, 1], b[:, 0])
                        parts.append(jnp.where(up ^ flip_up, b[:, 1], b[:, 0]))
                    return jnp.concatenate(parts, axis=-1)

                self.of = of
                self.keep = of(True, False)
                return [(self, "came", of(True, True), n_seq)]

            def middle_z(self):
                total = (self.keep.astype(F32) + self.came.astype(F32)).astype(BF)
                return [(self, "near", total, 2 * n_seq)]

            def middle_y(self):
                self.keep = self.of(False, False)
                return [(self, "came", self.of(False, True), n_seq)]

            def middle(self):
                return self.middle_z() + self.middle_y()

            def last(self):
                total = (
                    self.keep.astype(F32) + self.came.astype(F32) + self.near.astype(F32)
                ).astype(BF)
                high = bit_of(dp, 4) == 1
                self.keep = jnp.where(high, total[1], total[0])
                return [(self, "came", jnp.where(high, total[0], total[1]), 4 * n_seq)]

            def rows(self):
                return self.keep.astype(F32) + self.came.astype(F32)

        def scatter_out(grad):
            if not special:
                placed = grad.reshape(pairs_here, 1, 2 * HEAD, dim)
                hot = (jnp.arange(n_seq) == seq)[None, :, None, None]
                placed = jnp.where(hot, placed, jnp.zeros_like(placed)).reshape(dim, dim)
                return lax.psum_scatter(placed, AXES, scatter_dimension=0, tiled=True)
            return None

        def unsplit(pieces, size):
            count = pieces[0].shape[1] // size
            return jnp.concatenate(
                [pieces[s][:, i * size : (i + 1) * size] for i in range(count) for s in range(n_seq)],
                axis=1,
            )

        class Grads:
            pass

        class Back:
            def __init__(self, blocks):
                pieces = by_origin(blocks)
                self.step_0, self.pieces = pieces[0], pieces

            def moves(self):
                return [(self, "step_%d" % i, self.pieces[i], i) for i in range(1, n_seq)]

            def got(self):
                return [getattr(self, "step_%d" % i) for i in range(n_seq)]

        class Table:
            def __init__(self, rows, more):
                self.keep, self.more = rows, more
                self.bits = [4 * n_seq, 2 * n_seq, n_seq]

            def take(self):
                if hasattr(self, "came"):
                    self.keep = self.keep + self.came

            def step(self):
                self.take()
                bit = self.bits.pop(0)
                middle = self.keep.shape[1] // 2
                low, up = self.keep[:, :middle], self.keep[:, middle:]
                chosen = bit_of(dp, bit // n_seq) == 1
                self.keep = jnp.where(chosen, up, low)
                return [(self, "came", jnp.where(chosen, low, up), bit)]

            def group_step(self):
                self.take()
                more = jnp.pad(self.more, ((0, 0), (0, self.keep.shape[1] - self.more.shape[1])))
                self.keep = jnp.concatenate([self.keep, more], axis=0)
                return [(self, "came_%d" % i, self.keep, i) for i in range(1, n_seq)]

            def whole(self):
                rest = [getattr(self, "came_%d" % i) for i in range(1, n_seq)]
                return sum(by_origin([self.keep] + rest))

        def rows_back(scattered):
            return exchange_steps([scattered[s * part : (s + 1) * part] for s in range(n_seq)])

        def columns_row(vector):
            hot = (jnp.arange(n_seq) == seq)[None, :, None]
            return jnp.where(hot, vector.reshape(pairs_here, 1, 2 * HEAD), 0.0).reshape(1, dim)

        def hidden_rows(vector):
            hot = (jnp.arange(n_seq) == seq)[:, None]
            return jnp.where(hot, vector[None, :], 0.0)

        def reduce_rows(rows, extra=None):
            unit = n_dp
            while unit > 1:
                unit //= 2
                middle = rows.shape[1] // 2
                keep, got = halve(
                    (rows[:, :middle], rows[:, middle:]), bit_of(dp, unit), unit * n_seq
                )
                rows = keep + got
            if extra is not None:
                extra = jnp.pad(extra, ((0, 0), (0, rows.shape[1] - extra.shape[1])))
                rows = jnp.concatenate([rows, extra], axis=0)
            for bit in seq_bits:
                rows = rows + swap(rows, bit)
            return rows

        def own_part(row):
            return lax.dynamic_slice_in_dim(row, seq * part, part)

        big = [None] * layers
        vectors, inner_vectors = [None] * layers, [None] * layers
        lex_row = jnp.zeros((1, n_dp, dim // n_dp), F32).at[0, :, :2].set(local_sums)
        lex_row = lex_row.reshape(1, dim)
        for layer in reversed(range(layers)):
            gain_one, gain_two = vector_of(layer, 3), vector_of(layer, 6)
            (group, qkv, attended, row_max, row_sum, rhat_one, inverse_one, normed_group,
             active, slope, rhat_two, inverse_two) = kept[layer]
            grad_second, fgain, fbias = norm_back(grad_now, gain_two, rhat_two, inverse_two)
            low_second = grad_second.astype(BF)

            def token_rows():
                return jnp.stack(
                    [column_sums(low_first), ngain, nbias, column_sums(low_second), fgain, fbias]
                )

            def layer_rows():
                vectors[0], inner_vectors[0] = token_rows(), hidden_rows(inner_sums)
                return jnp.concatenate(vectors + [lex_row] + inner_vectors, axis=0)

            above = big[layer + 1] if special and layer + 1 < layers else None
            moves = above.expand.last() + above.qkv.first() if above else []
            halves = gather_seq(low_second, moves, grad_now)
            moving = launch(above.qkv.middle(), above.qkv.came) if above else []
            low_inner = [
                (dot(rows, shrink_all[layer], 1, 1) * slope[i]).astype(BF)
                for i, rows in enumerate(halves)
            ]
            low_inner[1] = settle(low_inner[1], moving)
            second_group = both(halves)
            inner_group = both(low_inner)
            shrink_grad = dot(active, second_group, 0, 0).astype(BF)
            expand_grad = dot(normed_group, inner_group, 0, 0).astype(BF)
            moves = []
            if special:
                big[layer] = mine = Grads()
                mine.shrink, mine.expand = Sums([shrink_grad]), Sums([expand_grad])
                moves = (above.qkv.last() if above else []) + mine.shrink.first()
            summed = reduce_seq(low_inner, (expand_all[layer], (1, 1)), moves)
            inner_sums = sum(column_sums(half) for half in low_inner)
            grad_normed = grad_second + summed
            grad_first, ngain, nbias = norm_back(grad_normed, gain_one, rhat_one, inverse_one)
            low_first = grad_first.astype(BF)
            if special:
                moves = mine.shrink.middle()
            first_group = both(gather_seq(low_first, moves, summed))
            if special:
                moves = mine.shrink.last() + mine.expand.first()
                moving = launch(moves, first_group)
            low_attn = dot(first_group, out_all[layer], 1, 1).astype(BF)
            out_grad = dot(attended, first_group, 0, 0).astype(BF)
            if special:
                quarter = dim // n_seq
                pieces = [out_grad[:, s * quarter : (s + 1) * quarter] for s in range(n_seq)]
                if layer == 0:
                    done = [
                        g.rows().astype(BF) for m in big[1:] for g in (m.expand, m.qkv)
                    ]
                    for s in range(n_seq):
                        rows = jnp.concatenate([g[s * part : (s + 1) * part] for g in done], axis=1)
                        cut = [
                            rows[:, i : i + quarter] for i in range(0, rows.shape[1], quarter)
                        ]
                        pieces[s] = jnp.concatenate([pieces[s]] + cut, axis=0)
                pieces = exchange_steps(pieces)
                if layer == 0:
                    upper_rows = by_origin([p[width:] for p in pieces])
                    pieces = [p[:width] for p in pieces]
                pieces = [p.reshape(pairs_here, 1, 2 * HEAD, quarter) for p in by_origin(pieces)]
                out_columns = jnp.concatenate(pieces, axis=1).reshape(dim, quarter)
            grad_qkv = attend_back(qkv, starts, row_max, row_sum, low_attn)
            if special:
                grad_qkv = settle(grad_qkv, moving)
            qkv_grad = dot(group, grad_qkv, 0, 0).astype(BF)
            qkv_sums = column_sums(grad_qkv)
            if special:
                joined = [qkv_grad, out_columns]
                extra = 0
                if layer == 0:
                    extra = 16
                    rows = jnp.concatenate(
                        [
                            qkv_sums[:width].reshape(pairs_here, 2 * HEAD),
                            qkv_sums[2 * width :].reshape(pairs_here, 2 * HEAD),
                        ],
                        axis=1,
                    )
                    hot = (jnp.arange(n_seq) == seq)[None, :, None]
                    rows = jnp.where(hot, rows[:, None, :], 0.0).reshape(n_dp, 1, 4 * HEAD)
                    rows = jnp.pad(rows, ((0, 0), (0, 15), (0, 3 * width - 4 * HEAD))).astype(BF)
                    joined = [
                        jnp.pad(g.reshape(n_dp, block_rows, -1), ((0, 0), (0, 16), (0, 0)))
                        for g in joined
                    ]
                    joined[0] = jnp.concatenate([joined[0][:, :block_rows], rows], axis=1)
                mine.qkv = Sums(joined, block_rows + extra)
                if layer:
                    moves = mine.expand.middle()
                else:
                    table = Table(layer_rows(), scores)
                    qkv_grad = settle(qkv_grad, launch(table.step(), grad_qkv))
                    moves = mine.qkv.first() + mine.expand.middle_z() + table.step()
            else:
                moves = []
            left = after(grad_qkv, qkv_grad)
            left = (left[:chip_rows], left[chip_rows:])
            summed = reduce_seq(left, (qkv_all[layer], (1, 1)), moves, qkv_grad)
            if special and layer == 0:

                def back_of(grads, extra=0):
                    grads = [g.astype(BF) for g in grads]
                    blocks = []
                    for s in range(n_seq):
                        rows = [g[s * part : (s + 1) * part] for g in grads]
                        if extra:
                            rows = [jnp.concatenate([r, g[block_rows:]], axis=0) for r, g in zip(rows, grads)]
                        blocks.append(jnp.concatenate(rows, axis=1) if len(rows) > 1 else rows[0])
                    return Back(blocks)

                gate = summed
                moves = mine.qkv.middle() + table.step()
                gate = settle(gate, launch(moves, gate))
                moves = mine.qkv.last() + mine.expand.middle_y() + table.group_step()
                gate = settle(gate, launch(moves, gate))
                last_back = back_of([mine.qkv.rows()], 16)
                moves = mine.expand.last() + last_back.moves()
                gate = settle(gate, launch(moves, gate))
                expand_back = back_of([mine.expand.rows()])
                settle(gate, launch(expand_back.moves(), gate))
            if not special:
                big[layer] = (
                    scatter_dp(shrink_grad),
                    scatter_dp(expand_grad),
                    scatter_out(out_grad),
                    scatter_dp(qkv_grad),
                )
            grad_now = grad_first + summed
            head_rows = [columns_row(qkv_sums[:width]), columns_row(qkv_sums[2 * width :])]
            if layer or not special:
                vectors[layer] = token_rows()
                if layer:
                    vectors[layer] = jnp.concatenate([vectors[layer]] + head_rows, axis=0)
                inner_vectors[layer] = hidden_rows(inner_sums)

        tokens_grad = grad_now.astype(BF)

        counts = [v.shape[0] for v in vectors] + [1] + [n_seq] * layers
        if special:
            table = table.whole()
            scores = table[-1:, : scores.shape[1]]
        else:
            table = reduce_rows(jnp.concatenate(vectors + [lex_row], axis=0), scores)
            scores = table[-1:, : scores.shape[1]]
            inner = reduce_rows(jnp.concatenate(inner_vectors, axis=0))
            last = reduce_rows(jnp.concatenate(head_rows, axis=0))
        cut = [0]
        for count in counts:
            cut.append(cut[-1] + count)
        tables = [table[cut[i] : cut[i + 1]] for i in range(len(counts))]
        if special:
            inner_tables = tables[layers + 1 :]
        else:
            inner_tables = [inner[i * n_seq : (i + 1) * n_seq] for i in range(layers)]
        lexical_stats = tables[layers][0, :2] / (rows_here * n_dev)
        inner_out = jnp.stack(
            [lax.dynamic_index_in_dim(t, seq, 0, keepdims=False) for t in inner_tables]
        )

        layer_outs = []
        for layer in range(layers):
            if special:
                shrink_rows = big[layer].shrink.rows()
                if layer:
                    count = (own_hidden + 3 * width + quarter) // quarter
                    got = []
                    for g in upper_rows:
                        g = g[(layer - 1) * count * part : layer * count * part]
                        cut = [g[i * part : (i + 1) * part] for i in range(count)]
                        got.append(jnp.concatenate(cut, axis=1))
                    expand_out = [g[:, :own_hidden] for g in got]
                    got = [g[:, own_hidden:] for g in got]
                else:
                    got = last_back.got()
                    source = seq ^ lax.rem(dp, n_seq)
                    row = got[0][part : part + 1, : 4 * HEAD]
                    for step in range(1, n_seq):
                        row = jnp.where(source == step, got[step][part : part + 1, : 4 * HEAD], row)
                    last = row.reshape(2, 2 * HEAD).astype(F32)
                    got = by_origin([g[:part] for g in got])
                    expand_out = by_origin(expand_back.got())
                out_out = jnp.concatenate([g[:, 3 * width :] for g in got], axis=1)
            else:
                shrink_rows, expand_rows, out_out, qkv_rows = big[layer]
                got, expand_out = by_origin(rows_back(qkv_rows)), by_origin(rows_back(expand_rows))
            layer_outs.append(
                [
                    unsplit([g[:, i * width : (i + 1) * width] for g in got], 2 * HEAD)
                    for i in range(3)
                ]
                + [out_out, unsplit(expand_out, hidden_part), shrink_rows]
            )
        def vector_out(index):
            if index < 2:
                return jnp.stack(
                    [own_part(tables[i][6 + index] if i else last[index]) for i in range(layers)]
                )
            return jnp.stack([own_part(tables[i][index - 2]) for i in range(layers)])

        big_out = [jnp.stack([lo[i].astype(F32) for lo in layer_outs]) for i in range(6)]
        return (
            encoded, scores, lexical_stats, tokens_grad,
            big_out[0], vector_out(0), big_out[1], big_out[2], vector_out(1),
            big_out[3], vector_out(2), vector_out(3), vector_out(4),
            big_out[4], inner_out, big_out[5], vector_out(5),
            vector_out(6), vector_out(7),
        )

    rows = P(AXES, None)
    weight = P(None, AXES, None)
    vector = P(None, AXES)
    placed = (
        rows, P("dp", None), P(AXES), P("dp", None, None), P("dp", None),
        weight, vector, weight, weight, vector, weight, vector, vector, vector,
        weight, vector, weight, vector, vector, vector, P(), P(), P("dp", None), rows,
    )
    results = (
        rows, P("dp", None), P(), rows,
        weight, vector, weight, weight, vector, weight, vector, vector, vector,
        weight, vector, weight, vector, vector, vector,
    )
    return jax.shard_map(local, mesh=mesh, in_specs=placed, out_specs=results, check_vma=False)
```

```python
import functools
import math

import jax
import jax.numpy as jnp
from jax import lax
from jax.experimental import pallas as pl
from jax.experimental.pallas import tpu as pltpu
from jax.sharding import PartitionSpec as P

HEAD = 64
EPSILON = 1e-05
NEGATIVE = -1e30
HIGHEST = lax.Precision.HIGHEST
AXES = ("dp", "seq")
BF = jnp.bfloat16
F32 = jnp.float32
VMEM_LIMIT = 56 * 1024 * 1024


def dot(left, right, left_dim=1, right_dim=0):
    return lax.dot_general(
        left, right, (((left_dim,), (right_dim,)), ((), ())), preferred_element_type=F32
    )


def head_lanes(shape, half):
    lane = lax.broadcasted_iota(jnp.int32, shape, 1)
    return (lane < HEAD) if half == 0 else (lane >= HEAD)


def attend_kernel(block, qkv_ref, col_ref, row_ref, out_ref, max_ref, sum_ref):
    tokens, width = out_ref.shape
    pairs = width // (2 * HEAD)
    scale = 1.0 / math.sqrt(HEAD)
    for pair in range(pairs):
        lo = pair * 2 * HEAD
        keys = qkv_ref[:, width + lo : width + lo + 2 * HEAD]
        values = qkv_ref[:, 2 * width + lo : 2 * width + lo + 2 * HEAD]
        values_t = values.astype(F32).T.astype(BF)
        for start in range(0, tokens, block):
            queries = qkv_ref[start : start + block, lo : lo + 2 * HEAD] * scale
            queries = queries.astype(BF)
            same = col_ref[...] == row_ref[:, start : start + block]
            halves = []
            for half in range(2):
                lanes = head_lanes(queries.shape, half)
                scores = dot(keys, jnp.where(lanes, queries, jnp.zeros_like(queries)), 1, 1)
                scores = jnp.where(same, scores, NEGATIVE)
                top = jnp.max(scores, axis=0, keepdims=True)
                raised = jnp.exp(scores - top)
                total = jnp.sum(raised, axis=0, keepdims=True)
                probs = (raised * (1.0 / total)).astype(BF)
                mixed = dot(values_t, probs)
                halves.append(mixed[half * HEAD : (half + 1) * HEAD])
                head = 2 * pair + half
                max_ref[head : head + 1, start : start + block] = top
                sum_ref[head : head + 1, start : start + block] = total
            joined = jnp.concatenate(halves, axis=0)
            out_ref[start : start + block, lo : lo + 2 * HEAD] = joined.T.astype(BF)


def attend_back_kernel(
    block, qkv_ref, col_ref, row_ref, max_ref, sum_ref, grad_ref, out_ref, key_acc, value_acc
):
    tokens, width = grad_ref.shape
    pairs = width // (2 * HEAD)
    scale = 1.0 / math.sqrt(HEAD)
    for pair in range(pairs):
        lo = pair * 2 * HEAD
        keys = qkv_ref[:, width + lo : width + lo + 2 * HEAD]
        values = qkv_ref[:, 2 * width + lo : 2 * width + lo + 2 * HEAD]
        keys_t = keys.astype(F32).T.astype(BF)
        key_acc[...] = jnp.zeros_like(key_acc)
        value_acc[...] = jnp.zeros_like(value_acc)
        for start in range(0, tokens, block):
            queries = (qkv_ref[start : start + block, lo : lo + 2 * HEAD] * scale).astype(BF)
            grads = grad_ref[start : start + block, lo : lo + 2 * HEAD]
            same = col_ref[...] == row_ref[:, start : start + block]
            halves = []
            for half in range(2):
                lanes = head_lanes(queries.shape, half)
                own_queries = jnp.where(lanes, queries, jnp.zeros_like(queries))
                own_grads = jnp.where(lanes, grads, jnp.zeros_like(grads))
                head = 2 * pair + half
                top = max_ref[head : head + 1, start : start + block]
                total = sum_ref[head : head + 1, start : start + block]
                scores = dot(keys, own_queries, 1, 1)
                scores = jnp.where(same, scores, NEGATIVE)
                probs = jnp.exp(scores - top) * (1.0 / total)
                grad_probs = dot(values, own_grads, 1, 1)
                shared = jnp.sum(probs * grad_probs, axis=0, keepdims=True)
                grad_scores = (probs * (grad_probs - shared)).astype(BF)
                value_acc[...] += dot(probs.astype(BF), own_grads)
                key_acc[...] += dot(grad_scores, own_queries)
                mixed = dot(keys_t, grad_scores)
                halves.append(mixed[half * HEAD : (half + 1) * HEAD])
            joined = jnp.concatenate(halves, axis=0) * scale
            out_ref[start : start + block, lo : lo + 2 * HEAD] = joined.T.astype(BF)
        out_ref[:, width + lo : width + lo + 2 * HEAD] = key_acc[...].astype(BF)
        out_ref[:, 2 * width + lo : 2 * width + lo + 2 * HEAD] = value_acc[...].astype(BF)


def attend(qkv, starts):
    tokens, width = qkv.shape[0], qkv.shape[1] // 3
    heads = width // HEAD
    whole = pl.BlockSpec(memory_space=pltpu.VMEM)
    return pl.pallas_call(
        functools.partial(attend_kernel, math.gcd(tokens, 768)),
        out_shape=(
            jax.ShapeDtypeStruct((tokens, width), BF),
            jax.ShapeDtypeStruct((heads, tokens), F32),
            jax.ShapeDtypeStruct((heads, tokens), F32),
        ),
        in_specs=[whole] * 3,
        out_specs=(whole,) * 3,
        compiler_params=pltpu.CompilerParams(vmem_limit_bytes=VMEM_LIMIT),
        cost_estimate=pl.CostEstimate(
            flops=40 * tokens * tokens * width, bytes_accessed=16 * tokens * width, transcendentals=0
        ),
    )(qkv, starts[:, None], starts[None, :])


def attend_back(qkv, starts, row_max, row_sum, grads):
    tokens, width = grads.shape
    whole = pl.BlockSpec(memory_space=pltpu.VMEM)
    return pl.pallas_call(
        functools.partial(attend_back_kernel, math.gcd(tokens, 768)),
        out_shape=jax.ShapeDtypeStruct((tokens, 3 * width), BF),
        in_specs=[whole] * 6,
        out_specs=whole,
        scratch_shapes=[
            pltpu.VMEM((tokens, 2 * HEAD), F32),
            pltpu.VMEM((tokens, 2 * HEAD), F32),
        ],
        compiler_params=pltpu.CompilerParams(vmem_limit_bytes=VMEM_LIMIT),
        cost_estimate=pl.CostEstimate(
            flops=40 * tokens * tokens * width, bytes_accessed=16 * tokens * width, transcendentals=0
        ),
    )(qkv, starts[:, None], starts[None, :], row_max, row_sum, grads)


def place_rows(order, sizes, pieces, outs):
    me = lax.axis_index("dp")
    for steps, piece in zip(order, pieces):
        first = 0
        for step in steps:
            if isinstance(step, tuple):
                where = step[0] * 2 + (lax.rem(me, 2) ^ step[1])
            else:
                where = me ^ step
            for member, rows in enumerate(sizes):
                at = pl.multiple_of(where * rows, rows)
                outs[member][pl.ds(at, rows), :] = piece[first : first + rows, :]
                first += rows


def place_kernel(order, sizes, *refs):
    place_rows(order, sizes, refs[: len(order)], refs[len(order) :])


def place_first_kernel(order, sizes, pairs, layers, *refs):
    pieces, (weights, smalls, full, heads, inner) = refs[: len(order)], refs[len(order) :]
    place_rows(order, sizes, pieces, (weights, smalls))
    seq, n_seq = lax.axis_index("seq"), 4
    n_dp = smalls.shape[0] // 16
    lane = lax.broadcasted_iota(jnp.int32, (4, 128), 1)
    for dp in range(n_dp):
        rows = smalls[dp * 16 : dp * 16 + 16, :].astype(F32)
        for block in range(6):
            part = rows[:, block * 128 : block * 128 + 128]
            total = part[:4]
            for s in range(1, n_seq):
                moved = pltpu.roll(part, 32 * s, 1)[4 * s : 4 * s + 4]
                total = jnp.where(lane // 32 == s, moved, total)
            full[block, 0:4, dp * 128 : dp * 128 + 128] = total
            if block == 2:
                own = part[:4]
                for s in range(1, n_seq):
                    own = jnp.where(seq == s, part[4 * s : 4 * s + 4], own)
                inner[0:layers, dp * 128 : dp * 128 + 128] = own[layers : 2 * layers]
    heads[...] = jnp.zeros_like(heads)
    width = pairs * 128
    for which, base in ((0, 0), (1, 2 * width)):
        for pair in range(pairs):
            column = pl.multiple_of((pair * n_seq + seq) * 128, 128)
            heads[0:layers, base + pair * 128 : base + pair * 128 + 128] = full[
                which, 0:layers, pl.ds(column, 128)
            ]


def place(pieces, order, sizes, unpack=None, missing=0):
    columns = pieces[0].shape[1]
    order = tuple(tuple(o) if isinstance(o, (list, tuple)) else (o,) for o in order)
    count = sum(len(o) for o in order) + missing
    whole = pl.BlockSpec(memory_space=pltpu.VMEM)
    shapes = [jax.ShapeDtypeStruct((count * rows, columns), BF) for rows in sizes]
    body = functools.partial(place_kernel, order, tuple(sizes))
    if unpack is not None:
        pairs, layers, dim, inner = unpack
        shapes += [
            jax.ShapeDtypeStruct((6, 8, dim), F32),
            jax.ShapeDtypeStruct((8, pairs * 3 * 128), F32),
            jax.ShapeDtypeStruct((8, inner), F32),
        ]
        body = functools.partial(place_first_kernel, order, tuple(sizes), pairs, layers)
    return pl.pallas_call(
        body,
        out_shape=tuple(shapes),
        in_specs=[whole] * len(pieces),
        out_specs=(whole,) * len(shapes),
        compiler_params=pltpu.CompilerParams(vmem_limit_bytes=VMEM_LIMIT),
        cost_estimate=pl.CostEstimate(flops=0, bytes_accessed=0, transcendentals=0),
    )(*pieces)


def place_more_kernel(order, rows, buffer, piece, out, sem):
    me = lax.axis_index("dp")
    copies = []
    for i, step in enumerate(order):
        at = pl.multiple_of((me ^ step) * rows, rows)
        copies.append(
            pltpu.make_async_copy(
                piece.at[pl.ds(i * rows, rows)], out.at[pl.ds(at, rows)], sem.at[i]
            )
        )
    for copy in copies:
        copy.start()
    for copy in copies:
        copy.wait()


def place_more(buffer, piece, order):
    anywhere = pl.BlockSpec(memory_space=pl.ANY)
    return pl.pallas_call(
        functools.partial(place_more_kernel, tuple(order), piece.shape[0] // len(order)),
        out_shape=jax.ShapeDtypeStruct(buffer.shape, buffer.dtype),
        in_specs=[anywhere, pl.BlockSpec(memory_space=pltpu.VMEM)],
        out_specs=anywhere,
        scratch_shapes=[pltpu.SemaphoreType.DMA((len(order),))],
        input_output_aliases={0: 0},
        compiler_params=pltpu.CompilerParams(vmem_limit_bytes=VMEM_LIMIT),
        cost_estimate=pl.CostEstimate(flops=0, bytes_accessed=0, transcendentals=0),
    )(buffer, piece)


def split_kernel(n_seq, plan, part, smalls, *refs):
    n_in = 1 + max(p[0] for p in plan)
    weights, rest = refs[:n_in], refs[n_in:]
    small_refs, rest = rest[:smalls], rest[smalls:]
    outs = rest[:n_seq]
    seq = lax.axis_index("seq")
    if smalls:
        table = rest[n_seq]
        table[...] = jnp.zeros_like(table)
        across = table.shape[1] // 128
        for j, small in enumerate(small_refs):
            row, lane = 2 * (j // across), 128 * (j % across)
            table[row : row + 2, lane : lane + small.shape[1]] = small[...].astype(F32)
    for step in range(n_seq):
        target = seq ^ step
        at = 0
        for ref, layer, block, count in plan:
            if not count:
                outs[step][:part, at : at + block] = weights[ref][layer]
                at += block
            for i in range(count):
                column = pl.multiple_of((i * n_seq + target) * block, 128)
                outs[step][:part, at : at + block] = weights[ref][layer, :, pl.ds(column, block)]
                at += block
        if smalls:
            outs[step][part:, :] = table[...].astype(BF)


def split_weights(weights, plan, n_seq, smalls=()):
    part = weights[0].shape[1]
    columns = sum(block * max(count, 1) for _, _, block, count in plan)
    rows = part + (16 if smalls else 0)
    whole = pl.BlockSpec(memory_space=pltpu.VMEM)
    return pl.pallas_call(
        functools.partial(split_kernel, n_seq, tuple(plan), part, len(smalls)),
        out_shape=tuple(jax.ShapeDtypeStruct((rows, columns), BF) for _ in range(n_seq)),
        in_specs=[whole] * (len(weights) + len(smalls)),
        out_specs=(whole,) * n_seq,
        scratch_shapes=[pltpu.VMEM((16, columns), F32)] if smalls else [],
        compiler_params=pltpu.CompilerParams(vmem_limit_bytes=VMEM_LIMIT),
    )(*weights, *smalls)


def join_kernel(n_seq, part, cuts, with_small, extra, *refs):
    pieces, rest = refs[:n_seq], refs[n_seq:]
    if extra:
        extra_ref, rest = rest[0], rest[1:]
    outs = rest[: len(cuts)]
    seq = lax.axis_index("seq")
    for step in range(n_seq):
        row = pl.multiple_of((seq ^ step) * part, part)
        at = 0
        for out, columns in zip(outs, cuts):
            out[pl.ds(row, part), :] = pieces[step][:part, at : at + columns]
            at += columns
    if with_small:
        table = rest[len(cuts)]
        smalls = [pieces[step][part:, :].astype(F32)[:4] for step in range(n_seq)]
        for origin in range(n_seq):
            total = jnp.zeros_like(smalls[0])
            for step in range(n_seq):
                total = jnp.where((seq ^ step) == origin, smalls[step], total)
            table[4 * origin : 4 * origin + 4, :] = total
        outs[0][n_seq * part :, :] = table[...].astype(BF)
    if extra:
        outs[0][n_seq * part :, :] = extra_ref[0]


def join_pieces(pieces, part, cuts, with_small=False, extra=None):
    n_seq = len(pieces)
    rows = [n_seq * part] * len(cuts)
    if with_small:
        rows[0] += 4 * n_seq
    if extra is not None:
        rows[0] += extra.shape[1]
    whole = pl.BlockSpec(memory_space=pltpu.VMEM)
    more = [] if extra is None else [extra]
    return pl.pallas_call(
        functools.partial(
            join_kernel, n_seq, part, tuple(cuts), with_small, extra is not None
        ),
        out_shape=tuple(jax.ShapeDtypeStruct((r, c), BF) for r, c in zip(rows, cuts)),
        in_specs=[whole] * (n_seq + len(more)),
        out_specs=(whole,) * len(cuts),
        scratch_shapes=[pltpu.VMEM((4 * n_seq, cuts[0]), F32)] if with_small else [],
        compiler_params=pltpu.CompilerParams(vmem_limit_bytes=VMEM_LIMIT),
    )(*pieces, *more)


def after(array, *others):
    return lax.optimization_barrier((array,) + others)[0] if others else array


def solution(mesh):
    n_dp, n_seq = mesh.shape["dp"], mesh.shape["seq"]
    n_dev = n_dp * n_seq
    special = (n_dp, n_seq) == (8, 4)

    def swap(array, bit):
        return lax.ppermute(array, AXES, [(p, p ^ bit) for p in range(n_dev)])

    def bits_of(count, unit=1):
        bits = []
        while count > 1:
            bits.append(unit)
            unit, count = unit * 2, count // 2
        return bits

    seq_bits, dp_bits = bits_of(n_seq), bits_of(n_dp, n_seq)

    z_lines = [[d for d in range(n_dp) if d % 2 == y] for y in range(2)]

    x_steps = [0]
    for bit in reversed(seq_bits[1:]):
        x_steps = x_steps + [s ^ bit for s in x_steps]
    seq_steps = [step ^ core for step in x_steps for core in (0, 1)]

    def spread(piece, bits):
        pieces, steps = [piece], [0]
        for bit in reversed(bits):
            pieces = pieces + [swap(p, bit) for p in pieces]
            steps = steps + [s ^ bit for s in steps]
        return pieces, steps

    def launch(moves, gate):
        return [
            (home, name, swap(after(array, gate), bit) if bit else array)
            for home, name, array, bit in moves
        ]

    def settle(array, moving):
        if not moving:
            return array
        arrays = tuple(array) if isinstance(array, (tuple, list)) else (array,)
        out = lax.optimization_barrier(arrays + tuple(m[2] for m in moving))
        for (home, name, _), value in zip(moving, out[len(arrays) :]):
            setattr(home, name, value)
        return list(out[: len(arrays)]) if isinstance(array, (tuple, list)) else out[0]

    def gather_seq(rows, moves=(), gate=None):
        moving = launch(moves, rows if gate is None else gate)
        pieces = [rows]
        for bit in reversed(seq_bits[1:]):
            came = [swap(p, bit) for p in pieces]
            came[0] = settle(came[0], moving)
            moving = []
            pieces = pieces + came
        pairs = [jnp.concatenate([p, swap(p, 1)], axis=0) for p in pieces]
        return pairs[0], (jnp.concatenate(pairs[1:], axis=0) if len(pairs) > 2 else pairs[1])

    def both(halves):
        return jnp.concatenate(halves, axis=0)

    def reduce_seq(left, right, moves=(), gate=None, marks=None):
        near, far = left
        moving = launch(moves, far if gate is None else gate)
        size = near.shape[0] // 2

        def chip(rows, own):
            parts = right(rows, own) if callable(right) else dot(rows, right[0], *right[1])
            return parts[:size] + swap(parts[size:].astype(BF), 1).astype(F32)

        total = [None] + [
            chip(far[i * 2 * size : (i + 1) * 2 * size], False) for i in range(len(x_steps) - 1)
        ]
        if marks is not None:
            marks.append(total[-1])
        for i, bit in enumerate(seq_bits[1:]):
            middle = len(total) // 2
            got = [swap(t.astype(BF), bit) for t in total[middle:]]
            if i + 2 == len(seq_bits):
                got[0] = settle(got[0], moving)
            if total[0] is None:
                total[0] = chip(near, True)
            total = [a + b.astype(F32) for a, b in zip(total[:middle], got)]
        return total[0]

    def halve(array, index_bit, bit):
        chosen = index_bit.astype(jnp.bool_)
        send = jnp.where(chosen, array[0], array[1])
        keep = jnp.where(chosen, array[1], array[0])
        return keep, swap(send, bit)

    def local(
        tokens, doc_start, lexical_ids, queries, match_index,
        query_weight, query_bias, key_weight, value_weight, value_bias,
        out_weight, out_bias, norm_gain, norm_bias, expand_weight, expand_bias,
        shrink_weight, shrink_bias, final_gain, final_bias,
        lexical_weight, lexical_bias, score_cot, encoded_cot,
    ):
        layers, part, dim = query_weight.shape
        hidden_dim = expand_weight.shape[2]
        hidden_part = shrink_weight.shape[1]
        rows_here = tokens.shape[0]
        pairs_here = dim // (2 * HEAD) // n_seq
        width = pairs_here * 2 * HEAD
        own_hidden = hidden_dim // n_seq
        block_rows = dim // n_dp
        dp, seq = lax.axis_index("dp"), lax.axis_index("seq")
        flat = dp * n_seq + seq

        def bit_of(index, bit):
            return lax.bitwise_and(lax.div(index, bit), 1)

        def by_origin(pieces):
            for bit in seq_bits:
                chosen = bit_of(seq, bit).astype(jnp.bool_)
                pieces = [jnp.where(chosen, pieces[j ^ bit], pieces[j]) for j in range(n_seq)]
            return pieces

        def exchange_steps(blocks):
            pieces = by_origin(blocks)
            return [pieces[0]] + [swap(pieces[step], step) for step in range(1, n_seq)]

        def exchange_seq(blocks):
            return by_origin(exchange_steps(blocks))

        def head_split(weight):
            cut = [weight[:, i * 2 * HEAD : (i + 1) * 2 * HEAD] for i in range(pairs_here * n_seq)]
            return [cut[s::n_seq] for s in range(n_seq)]

        def hidden_split(weight):
            cut = [
                weight[:, i * hidden_part : (i + 1) * hidden_part] for i in range(n_dp * n_seq)
            ]
            return [cut[s::n_seq] for s in range(n_seq)]

        def qkv_split(layer):
            three = [head_split(w[layer]) for w in (query_weight, key_weight, value_weight)]
            return [jnp.concatenate(three[0][s] + three[1][s] + three[2][s], axis=1) for s in range(n_seq)]

        small_full = (
            query_bias, value_bias, out_bias, norm_gain, norm_bias, shrink_bias, final_gain, final_bias,
        )
        three = [query_weight, key_weight, value_weight]
        hidden_now = tokens.astype(F32)
        if special:
            heads_plan = [(i, 0, 2 * HEAD, pairs_here) for i in range(3)]
            sent = split_weights(three, heads_plan, n_seq, small_full + (expand_bias,))
            got = [sent[0]] + [swap(sent[step], step) for step in range(1, n_seq)]
            (shard,) = join_pieces(got, part, (3 * width,), True)
            class Stream:
                def __init__(self, shard):
                    self.shard = shard

                def far(self):
                    return [(self, "came", self.shard, n_seq * 4)]

                def middle(self):
                    self.line = jnp.concatenate([self.shard, self.came], axis=0)
                    return [
                        (self, "near", self.line, n_seq * 2),
                        (self, "y_line", self.line, n_seq),
                    ]

                def last(self):
                    return [(self, "y_near", self.near, n_seq)]

                def open(self, rows):
                    pieces = [self.line, self.near, self.y_line]
                    opened = place(pieces, [[0, 4], [2, 6], [1, 5]], (rows,), missing=2)[0]
                    return [(self, "opened", opened, 0)]

                def closed(self):
                    return place_more(self.opened, self.y_near, (3, 7))

                def ready(self, sizes):
                    return [(self, "full", self.whole(sizes)[0], 0)]

                def whole(self, sizes, unpack=None):
                    pieces = [self.line, self.near, self.y_line, self.y_near]
                    return place(pieces, [[0, 4], [2, 6], [1, 5], [3, 7]], sizes, unpack)

            first_stream = Stream(shard)
            plan = [(3, 0, hidden_part, n_dp)]
            cuts = [own_hidden]
            for layer in range(1, layers):
                plan += [(i, layer, 2 * HEAD, pairs_here) for i in range(3)]
                plan += [(3, layer, hidden_part, n_dp)]
                cuts += [3 * width, own_hidden]
            plan += [(4, layer, dim, 0) for layer in range(layers)]
            cuts += [dim] * layers
            sent = split_weights(three + [expand_weight, out_weight], plan, n_seq)
            sent = [after(p, got[1], got[2], got[3]) for p in sent]
            got = [sent[0]] + [swap(sent[step], step) for step in range(1, n_seq)]
            second = join_pieces(got, part, cuts)
            group = both(gather_seq(after(tokens, *got[2:])))

            class OutRows:
                def __init__(self, rows):
                    self.rows, self.moved, self.bit = rows, None, 0

                def take(self):
                    bit, moved = self.bit, self.moved
                    if bit in (1, 2):
                        here = bit_of(seq, bit) == bit_of(dp, bit)
                        self.rows = jnp.where(here, self.rows, moved)
                    elif bit == 4:
                        upper = bit_of(dp, 4) == 1
                        self.rows = jnp.concatenate(
                            [jnp.where(upper, moved, self.rows), jnp.where(upper, self.rows, moved)],
                            axis=0,
                        )
                    self.bit = 0
                    self.rows = lax.optimization_barrier(self.rows)
                    return self.rows

                def step(self, bit):
                    rows = self.take()
                    self.bit = bit
                    return [(self, "moved", rows, n_seq * bit)]

            outs = [OutRows(second[2 * layers - 1 + i]) for i in range(layers)]
            streams = [
                Stream(x)
                for x in (second[0], shrink_weight[0], second[1], second[2], shrink_weight[1])
            ]
            expand_0, shrink_0, qkv_1, expand_1, shrink_1 = streams
            shard = settle(shard, launch(first_stream.far(), shard))
            moving = launch(first_stream.middle(), first_stream.came)
            out_y = launch(outs[0].step(1), first_stream.came)
            shard = settle(shard, moving[:1])
            moving = moving[1:] + launch(first_stream.last() + expand_0.far(), first_stream.near)
            shard = settle(shard, out_y)
            moving += launch(outs[0].step(2), outs[0].moved)
            group = settle(group, moving)
            qkv_first, _, small_full, small_heads, small_inner = first_stream.whole(
                (block_rows, 16), (pairs_here, layers, dim, own_hidden)
            )
            head_bias, hidden_bias = small_heads[:layers], small_inner[:layers]

            def vector_of(layer, j):
                return small_full[j % 6, layers * (j // 6) + layer]

        else:
            small = lax.all_gather(
                jnp.concatenate(list(small_full) + [expand_bias], axis=1), AXES, axis=0, tiled=False
            )
            full = small[:, :, : 8 * part].reshape(n_dev, layers, 8, part).transpose(1, 2, 0, 3)
            hidden_bias = small[:, :, 8 * part :].transpose(1, 0, 2)
            group = both(gather_seq(tokens))
            full = full.reshape(layers, 8, dim).astype(F32)
            by_column = full[:, :2].reshape(layers, 2, pairs_here, n_seq, 2 * HEAD)
            by_column = lax.dynamic_index_in_dim(by_column, seq, 3, keepdims=False)
            by_column = by_column.reshape(layers, 2, width)
            head_bias = jnp.concatenate(
                [by_column[:, 0], jnp.zeros((layers, width), F32), by_column[:, 1]], axis=1
            )
            hidden_bias = hidden_bias.reshape(layers, n_dp, n_seq, hidden_part)
            hidden_bias = lax.dynamic_index_in_dim(hidden_bias, seq, 2, keepdims=False)
            hidden_bias = hidden_bias.reshape(layers, own_hidden).astype(F32)

            def vector_of(layer, j):
                return full[layer, j]

        if special:
            out_all = []
        else:
            whole_out = lax.all_gather(out_weight, AXES, axis=1, tiled=True)
            cut = whole_out.reshape(layers, pairs_here, n_seq, 2 * HEAD, dim)
            cut = lax.dynamic_index_in_dim(cut, seq, 2, keepdims=False)
            out_all = [cut[layer].reshape(width, dim) for layer in range(layers)]

        if special:
            qkv_all, expand_all, shrink_all = [qkv_first], [], []

            def beside_of(layer, point):
                if (layer, point) == (0, "attend"):
                    return outs[0].step(4) + expand_0.middle()
                if (layer, point) == (0, "out"):
                    out_all.append(outs[0].take())
                    return expand_0.last() + shrink_0.far() + outs[1].step(1)
                if (layer, point) == (0, "normed"):
                    return shrink_0.middle() + expand_0.ready((block_rows,))
                if (layer, point) == (0, "active"):
                    expand_all.append(expand_0.full)
                    return shrink_0.last() + qkv_1.far() + outs[1].step(2) + shrink_0.open(hidden_part)
                if (layer, point) == (0, "shrink"):
                    shrink_all.append(shrink_0.closed())
                    return qkv_1.middle() + outs[1].step(4)
                if (layer, point) == (1, "group"):
                    return qkv_1.last() + expand_1.far()
                if (layer, point) == (1, "attend"):
                    qkv_all.append(qkv_1.whole((block_rows,))[0])
                    return expand_1.middle()
                if (layer, point) == (1, "out"):
                    out_all.append(outs[1].take())
                    return expand_1.last() + shrink_1.far()
                if (layer, point) == (1, "normed"):
                    return shrink_1.middle() + expand_1.ready((block_rows,))
                if (layer, point) == (1, "active"):
                    expand_all.append(expand_1.full)
                    return shrink_1.last() + shrink_1.open(hidden_part)
                if (layer, point) == (1, "shrink"):
                    shrink_all.append(shrink_1.closed())
                return []
        else:
            qkv_all, expand_all, shrink_all = [], [], []

            def beside_of(layer, point):
                return []

            for layer in range(layers):
                mine = exchange_seq(qkv_split(layer))
                mine = lax.all_gather(jnp.concatenate(mine, axis=0), "dp", axis=0, tiled=True)
                qkv_all.append(mine)
                mine = [jnp.concatenate(b, axis=1) for b in hidden_split(expand_weight[layer])]
                mine = jnp.concatenate(exchange_seq(mine), axis=0)
                expand_all.append(lax.all_gather(mine, "dp", axis=0, tiled=True))
                shrink_all.append(lax.all_gather(shrink_weight[layer], "dp", axis=0, tiled=True))

        starts_here = doc_start[0].reshape(n_seq, rows_here)
        starts = jnp.concatenate(
            [
                lax.dynamic_index_in_dim(starts_here, seq ^ step, 0, keepdims=False)
                for step in seq_steps
            ]
        )

        def norm_parts(resid):
            center = resid - jnp.mean(resid, axis=-1, keepdims=True)
            inverse = lax.rsqrt(jnp.mean(center * center, axis=-1, keepdims=True) + EPSILON)
            return center * inverse, inverse

        def norm_back(upstream, gain, rhat, inverse):
            scaled = upstream * gain
            mean_one = jnp.mean(scaled, axis=-1, keepdims=True)
            mean_two = jnp.mean(scaled * rhat, axis=-1, keepdims=True)
            grad = (scaled - mean_one - rhat * mean_two) * inverse
            return grad, jnp.sum(upstream * rhat, axis=0), jnp.sum(upstream, axis=0)

        def column_sums(matrix):
            return jnp.sum(matrix.astype(F32), axis=0)

        kept = []
        for layer in range(layers):
            _, _, out_b, gain_one, bias_one, shrink_b, gain_two, bias_two = (
                vector_of(layer, i) for i in range(8)
            )
            if layer:
                group = both(gather_seq(hidden_now.astype(BF), beside_of(layer, "group"), summed))
            moving = launch(beside_of(layer, "attend"), group)
            qkv = (dot(group, qkv_all[layer]) + head_bias[layer]).astype(BF)
            attended, row_max, row_sum = attend(qkv, starts)
            attended = settle(attended, moving)
            moves = beside_of(layer, "out")
            chip_rows = 2 * rows_here
            halves = (attended[:chip_rows], attended[chip_rows:])
            summed = reduce_seq(halves, (out_all[layer], (1, 0)), moves)
            resid_one = hidden_now + (summed + out_b)
            rhat_one, inverse_one = norm_parts(resid_one)
            normed = rhat_one * gain_one + bias_one
            normed_halves = gather_seq(normed.astype(BF), beside_of(layer, "normed"), summed)
            moves = beside_of(layer, "active")
            moving = launch(moves, moves[0][2] if moves else normed_halves[1])
            active, slope = [], []
            for rows in normed_halves:
                inner = dot(rows, expand_all[layer]) + hidden_bias[layer]
                cdf = 0.5 * (1.0 + lax.erf(inner * math.sqrt(0.5)))
                active.append((inner * cdf).astype(BF))
                slope.append(
                    cdf + inner * jnp.exp(-0.5 * inner * inner) * (1.0 / math.sqrt(2 * math.pi))
                )
            active = settle(active, moving)
            moves = beside_of(layer, "shrink")
            summed = reduce_seq(active, (shrink_all[layer], (1, 0)), moves)
            normed_group, active = both(normed_halves), both(active)
            resid_two = normed + (summed + shrink_b)
            rhat_two, inverse_two = norm_parts(resid_two)
            hidden_now = rhat_two * gain_two + bias_two
            kept.append(
                (group, qkv, attended, row_max, row_sum, rhat_one, inverse_one, normed_group,
                 active, slope, rhat_two, inverse_two)
            )
        encoded = hidden_now.astype(BF)

        local_index = match_index[0] - seq * rows_here
        picker = local_index[:, None] == jnp.arange(rows_here, dtype=jnp.int32)[None, :]
        chosen = dot(picker.astype(BF), encoded)
        query_vecs = queries[0].astype(F32)
        scores = jnp.sum(query_vecs * chosen, axis=-1)[None, :]
        lexical = jnp.sum(
            encoded.astype(F32) * lexical_weight.astype(F32)[None, :], axis=-1
        ) + lexical_bias.astype(F32)[0]
        keep_mask = (lexical_ids >= 4).astype(F32)
        local_sums = jnp.stack(
            [
                jnp.sum(keep_mask * jax.nn.softplus(lexical)),
                jnp.sum(keep_mask * jax.nn.sigmoid(lexical)),
            ]
        )
        weighted = score_cot[0][:, None] * query_vecs
        grad_now = encoded_cot.astype(F32) + lax.dot_general(
            picker.astype(F32), weighted, (((0,), (0,)), ((), ())), precision=HIGHEST
        )

        def scatter_dp(grad):
            return lax.psum_scatter(grad, "dp", scatter_dimension=0, tiled=True)

        class Sums:
            def __init__(self, grads, rows=block_rows):
                self.blocks = [g.reshape(2, 2, 2, rows, g.shape[-1]) for g in grads]

            def first(self):
                low, up = bit_of(dp, 2) == 1, bit_of(dp, 1) == 1

                def of(flip_low, flip_up):
                    parts = []
                    for b in self.blocks:
                        b = jnp.where(low ^ flip_low, b[:, 1], b[:, 0])
                        parts.append(jnp.where(up ^ flip_up, b[:, 1], b[:, 0]))
                    return jnp.concatenate(parts, axis=-1)

                self.of = of
                self.keep = of(True, False)
                return [(self, "came", of(True, True), n_seq)]

            def middle_z(self):
                total = (self.keep.astype(F32) + self.came.astype(F32)).astype(BF)
                return [(self, "near", total, 2 * n_seq)]

            def middle_y(self):
                self.keep = self.of(False, False)
                return [(self, "came", self.of(False, True), n_seq)]

            def middle(self):
                return self.middle_z() + self.middle_y()

            def last(self):
                total = (
                    self.keep.astype(F32) + self.came.astype(F32) + self.near.astype(F32)
                ).astype(BF)
                high = bit_of(dp, 4) == 1
                self.keep = jnp.where(high, total[1], total[0])
                return [(self, "came", jnp.where(high, total[0], total[1]), 4 * n_seq)]

            def rows(self):
                return self.keep.astype(F32) + self.came.astype(F32)

        def scatter_out(grad):
            if not special:
                placed = grad.reshape(pairs_here, 1, 2 * HEAD, dim)
                hot = (jnp.arange(n_seq) == seq)[None, :, None, None]
                placed = jnp.where(hot, placed, jnp.zeros_like(placed)).reshape(dim, dim)
                return lax.psum_scatter(placed, AXES, scatter_dimension=0, tiled=True)
            return None

        def unsplit(pieces, size):
            count = pieces[0].shape[1] // size
            return jnp.concatenate(
                [pieces[s][:, i * size : (i + 1) * size] for i in range(count) for s in range(n_seq)],
                axis=1,
            )

        class Grads:
            pass

        class Back:
            def __init__(self, blocks):
                pieces = by_origin(blocks)
                self.step_0, self.pieces = pieces[0], pieces

            def moves(self):
                return [(self, "step_%d" % i, self.pieces[i], i) for i in range(1, n_seq)]

            def got(self):
                return [getattr(self, "step_%d" % i) for i in range(n_seq)]

        class Table:
            def __init__(self, rows, more):
                self.keep, self.more = rows, more
                self.bits = [4 * n_seq, 2 * n_seq, n_seq]

            def take(self):
                if hasattr(self, "came"):
                    self.keep = self.keep + self.came

            def step(self):
                self.take()
                bit = self.bits.pop(0)
                middle = self.keep.shape[1] // 2
                low, up = self.keep[:, :middle], self.keep[:, middle:]
                chosen = bit_of(dp, bit // n_seq) == 1
                self.keep = jnp.where(chosen, up, low)
                return [(self, "came", jnp.where(chosen, low, up), bit)]

            def group_step(self):
                self.take()
                more = jnp.pad(self.more, ((0, 0), (0, self.keep.shape[1] - self.more.shape[1])))
                self.keep = jnp.concatenate([self.keep, more], axis=0)
                return [(self, "came_%d" % i, self.keep, i) for i in range(1, n_seq)]

            def whole(self):
                rest = [getattr(self, "came_%d" % i) for i in range(1, n_seq)]
                return sum(by_origin([self.keep] + rest))

        def rows_back(scattered):
            return exchange_steps([scattered[s * part : (s + 1) * part] for s in range(n_seq)])

        def columns_row(vector):
            hot = (jnp.arange(n_seq) == seq)[None, :, None]
            return jnp.where(hot, vector.reshape(pairs_here, 1, 2 * HEAD), 0.0).reshape(1, dim)

        def hidden_rows(vector):
            hot = (jnp.arange(n_seq) == seq)[:, None]
            return jnp.where(hot, vector[None, :], 0.0)

        def reduce_rows(rows, extra=None):
            unit = n_dp
            while unit > 1:
                unit //= 2
                middle = rows.shape[1] // 2
                keep, got = halve(
                    (rows[:, :middle], rows[:, middle:]), bit_of(dp, unit), unit * n_seq
                )
                rows = keep + got
            if extra is not None:
                extra = jnp.pad(extra, ((0, 0), (0, rows.shape[1] - extra.shape[1])))
                rows = jnp.concatenate([rows, extra], axis=0)
            for bit in seq_bits:
                rows = rows + swap(rows, bit)
            return rows

        def own_part(row):
            return lax.dynamic_slice_in_dim(row, seq * part, part)

        big = [None] * layers
        vectors, inner_vectors = [None] * layers, [None] * layers
        lex_row = jnp.zeros((1, n_dp, dim // n_dp), F32).at[0, :, :2].set(local_sums)
        lex_row = lex_row.reshape(1, dim)
        for layer in reversed(range(layers)):
            gain_one, gain_two = vector_of(layer, 3), vector_of(layer, 6)
            (group, qkv, attended, row_max, row_sum, rhat_one, inverse_one, normed_group,
             active, slope, rhat_two, inverse_two) = kept[layer]
            grad_second, fgain, fbias = norm_back(grad_now, gain_two, rhat_two, inverse_two)
            low_second = grad_second.astype(BF)

            def token_rows():
                return jnp.stack(
                    [column_sums(low_first), ngain, nbias, column_sums(low_second), fgain, fbias]
                )

            def layer_rows():
                vectors[0] = jnp.concatenate([token_rows()] + head_rows, axis=0)
                inner_vectors[0] = hidden_rows(inner_sums)
                return jnp.concatenate(vectors + [lex_row] + inner_vectors, axis=0)

            above = big[layer + 1] if special and layer + 1 < layers else None
            moves = above.expand.last() + above.qkv.first() if above else []
            halves = gather_seq(low_second, moves, grad_now)
            moving = launch(above.qkv.middle(), above.qkv.came) if above else []
            low_inner = [
                (dot(rows, shrink_all[layer], 1, 1) * slope[i]).astype(BF)
                for i, rows in enumerate(halves)
            ]
            low_inner[1] = settle(low_inner[1], moving)
            second_group = both(halves)
            inner_group = both(low_inner)
            shrink_grad = dot(active, second_group, 0, 0).astype(BF)
            moves, marks = [], []
            if special:
                big[layer] = mine = Grads()
                mine.shrink = Sums([shrink_grad])
                moves = (above.qkv.last() if above else []) + mine.shrink.first()
            summed = reduce_seq(low_inner, (expand_all[layer], (1, 1)), moves, None, marks)
            inner_group = after(inner_group, *marks)
            expand_grad = dot(normed_group, inner_group, 0, 0).astype(BF)
            if special:
                mine.expand = Sums([expand_grad])
            inner_sums = column_sums(inner_group)
            grad_normed = grad_second + summed
            grad_first, ngain, nbias = norm_back(grad_normed, gain_one, rhat_one, inverse_one)
            low_first = grad_first.astype(BF)
            if special:
                moves = mine.shrink.middle()
            first_group = both(gather_seq(low_first, moves, summed))
            if special:
                gate = mine.shrink.near
                moves = mine.shrink.last() + mine.expand.first()
                moving = launch(moves, gate)
            low_attn = dot(first_group, out_all[layer], 1, 1).astype(BF)
            out_grad = dot(attended, first_group, 0, 0).astype(BF)
            if special:
                quarter = dim // n_seq
                pieces = [out_grad[:, s * quarter : (s + 1) * quarter] for s in range(n_seq)]
                out_back = Back(pieces)
                moving += launch(out_back.moves(), first_group)
            grad_qkv = attend_back(qkv, starts, row_max, row_sum, low_attn)
            if special:
                grad_qkv = settle(grad_qkv, moving)

            def late_grads(grad_qkv):
                qkv_grad = dot(group, grad_qkv, 0, 0).astype(BF)
                if special:
                    pieces = out_back.got()
                    pieces = [p.reshape(pairs_here, 1, 2 * HEAD, quarter) for p in by_origin(pieces)]
                    out_columns = jnp.concatenate(pieces, axis=1).reshape(dim, quarter)
                    mine.qkv = Sums([qkv_grad, out_columns])
                return qkv_grad

            gate, moves, marks = grad_qkv, [], []
            if special and layer == 0:
                late_grads(grad_qkv)
                tail_moving = launch(mine.qkv.first() + mine.expand.middle_z(), grad_qkv)
            elif special:
                moves = mine.expand.middle()
            left = (grad_qkv[:chip_rows], grad_qkv[chip_rows:])
            summed = reduce_seq(left, (qkv_all[layer], (1, 1)), moves, gate, marks)
            grad_qkv = after(grad_qkv, *marks)
            qkv_sums = column_sums(grad_qkv)
            if layer or not special:
                qkv_grad = late_grads(grad_qkv)
            head_rows = [columns_row(qkv_sums[:width]), columns_row(qkv_sums[2 * width :])]
            if special and layer == 0:
                table = Table(layer_rows(), scores)
                for home, name, array in launch(table.step(), marks[0]):
                    setattr(home, name, array)
            if not special:
                big[layer] = (
                    scatter_dp(shrink_grad),
                    scatter_dp(expand_grad),
                    scatter_out(out_grad),
                    scatter_dp(qkv_grad),
                )
            grad_now = grad_first + summed
            if layer or not special:
                vectors[layer] = jnp.concatenate([token_rows()] + head_rows, axis=0)
                inner_vectors[layer] = hidden_rows(inner_sums)

        tokens_grad = grad_now.astype(BF)

        counts = [v.shape[0] for v in vectors] + [1] + [n_seq] * layers

        def small_outs(table, inner_tables=None):
            cut = [0]
            for count in counts:
                cut.append(cut[-1] + count)
            tables = [table[cut[i] : cut[i + 1]] for i in range(len(counts))]
            inner_tables = inner_tables or tables[layers + 1 :]
            inner_out = jnp.stack(
                [lax.dynamic_index_in_dim(t, seq, 0, keepdims=False) for t in inner_tables]
            )
            scores = table[-1:, : queries.shape[1]]
            stats = tables[layers][0, :2] / (rows_here * n_dev)
            vector_outs = [
                jnp.stack([own_part(tables[i][row]) for i in range(layers)])
                for row in (6, 7, 0, 1, 2, 3, 4, 5)
            ]
            return [scores, stats, inner_out] + vector_outs

        def stacked(arrays):
            return jnp.stack([a.astype(F32) for a in arrays])

        def head_outs(gots):
            outs = [
                stacked(
                    [
                        unsplit([g[:, i * width : (i + 1) * width] for g in got], 2 * HEAD)
                        for got in gots
                    ]
                )
                for i in range(3)
            ]
            return outs + [
                stacked([jnp.concatenate([g[:, 3 * width :] for g in got], axis=1) for got in gots])
            ]

        if special:

            def back_of(grads):
                grads = [g.astype(BF) for g in grads]
                return Back(
                    [
                        jnp.concatenate([g[s * part : (s + 1) * part] for g in grads], axis=1)
                        for s in range(n_seq)
                    ]
                )

            low = big[0]
            gate = settle(marks[0], tail_moving)
            moves = low.qkv.middle()
            for home, name, array in launch(table.step(), gate):
                setattr(home, name, array)
            gate, tokens_grad = settle([gate, tokens_grad], launch(moves + table.step(), gate))
            moves = low.qkv.last() + low.expand.middle_y() + table.group_step()
            gate = settle(gate, launch(moves, gate))
            back = back_of([low.qkv.rows()] + [g.rows() for m in big[1:] for g in (m.expand, m.qkv)])
            moving = launch(low.expand.last(), gate)
            gate = settle(gate, launch(back.moves(), gate))
            got = by_origin(back.got())
            size = 3 * width + dim // n_seq
            gots, upper_expand = [[g[:, :size] for g in got]], []
            for layer in range(1, layers):
                at = size + (layer - 1) * (own_hidden + size)
                upper_expand.append(
                    unsplit([g[:, at : at + own_hidden] for g in got], hidden_part).astype(F32)
                )
                gots.append([g[:, at + own_hidden : at + own_hidden + size] for g in got])
            smalls = small_outs(table.whole())
            heads = head_outs(gots)
            shrink_out = stacked([m.shrink.rows() for m in big])
            ready = settle(smalls + heads + upper_expand + [shrink_out, gate], moving)
            smalls, heads = ready[:11], ready[11:15]
            upper_expand, shrink_out, gate = ready[15:-2], ready[-2], ready[-1]
            back = back_of([low.expand.rows()])
            settle(gate, launch(back.moves(), gate))
            expand_out = stacked([unsplit(by_origin(back.got()), hidden_part)] + upper_expand)
        else:
            table = reduce_rows(jnp.concatenate(vectors + [lex_row], axis=0), scores)
            inner = reduce_rows(jnp.concatenate(inner_vectors, axis=0))
            smalls = small_outs(table, [inner[i * n_seq : (i + 1) * n_seq] for i in range(layers)])
            gots = [by_origin(rows_back(b[3])) for b in big]
            gots = [[jnp.concatenate([g, g[:, :0]], axis=1) for g in got] for got in gots]
            heads = head_outs(gots)[:3] + [stacked([b[2] for b in big])]
            expand_out = stacked([unsplit(by_origin(rows_back(b[1])), hidden_part) for b in big])
            shrink_out = stacked([b[0] for b in big])
        scores, lexical_stats, inner_out = smalls[:3]
        vector_outs = smalls[3:]
        return (
            encoded, scores, lexical_stats, tokens_grad,
            heads[0], vector_outs[0], heads[1], heads[2], vector_outs[1],
            heads[3], vector_outs[2], vector_outs[3], vector_outs[4],
            expand_out, inner_out, shrink_out, vector_outs[5],
            vector_outs[6], vector_outs[7],
        )

    rows = P(AXES, None)
    weight = P(None, AXES, None)
    vector = P(None, AXES)
    placed = (
        rows, P("dp", None), P(AXES), P("dp", None, None), P("dp", None),
        weight, vector, weight, weight, vector, weight, vector, vector, vector,
        weight, vector, weight, vector, vector, vector, P(), P(), P("dp", None), rows,
    )
    results = (
        rows, P("dp", None), P(), rows,
        weight, vector, weight, weight, vector, weight, vector, vector, vector,
        weight, vector, weight, vector, vector, vector,
    )
    return jax.shard_map(local, mesh=mesh, in_specs=placed, out_specs=results, check_vma=False)
```

```python
import functools
import math

import jax
import jax.numpy as jnp
from jax import lax
from jax.experimental import pallas as pl
from jax.experimental.pallas import tpu as pltpu
from jax.sharding import PartitionSpec as P

HEAD = 64
EPSILON = 1e-05
NEGATIVE = -1e30
HIGHEST = lax.Precision.HIGHEST
AXES = ("dp", "seq")
BF = jnp.bfloat16
F32 = jnp.float32
VMEM_LIMIT = 56 * 1024 * 1024


def dot(left, right, left_dim=1, right_dim=0):
    return lax.dot_general(
        left, right, (((left_dim,), (right_dim,)), ((), ())), preferred_element_type=F32
    )


def head_lanes(shape, half):
    lane = lax.broadcasted_iota(jnp.int32, shape, 1)
    return (lane < HEAD) if half == 0 else (lane >= HEAD)


def attend_kernel(block, qkv_ref, col_ref, row_ref, out_ref, max_ref, sum_ref):
    tokens, width = out_ref.shape
    pairs = width // (2 * HEAD)
    scale = 1.0 / math.sqrt(HEAD)
    for pair in range(pairs):
        lo = pair * 2 * HEAD
        keys = qkv_ref[:, width + lo : width + lo + 2 * HEAD]
        values = qkv_ref[:, 2 * width + lo : 2 * width + lo + 2 * HEAD]
        values_t = values.astype(F32).T.astype(BF)
        for start in range(0, tokens, block):
            queries = qkv_ref[start : start + block, lo : lo + 2 * HEAD] * scale
            queries = queries.astype(BF)
            same = col_ref[...] == row_ref[:, start : start + block]
            halves = []
            for half in range(2):
                lanes = head_lanes(queries.shape, half)
                scores = dot(keys, jnp.where(lanes, queries, jnp.zeros_like(queries)), 1, 1)
                scores = jnp.where(same, scores, NEGATIVE)
                top = jnp.max(scores, axis=0, keepdims=True)
                raised = jnp.exp(scores - top)
                total = jnp.sum(raised, axis=0, keepdims=True)
                probs = (raised * (1.0 / total)).astype(BF)
                mixed = dot(values_t, probs)
                halves.append(mixed[half * HEAD : (half + 1) * HEAD])
                head = 2 * pair + half
                max_ref[head : head + 1, start : start + block] = top
                sum_ref[head : head + 1, start : start + block] = total
            joined = jnp.concatenate(halves, axis=0)
            out_ref[start : start + block, lo : lo + 2 * HEAD] = joined.T.astype(BF)


def attend_back_kernel(
    block, qkv_ref, col_ref, row_ref, max_ref, sum_ref, grad_ref, out_ref, key_acc, value_acc
):
    tokens, width = grad_ref.shape
    pairs = width // (2 * HEAD)
    scale = 1.0 / math.sqrt(HEAD)
    for pair in range(pairs):
        lo = pair * 2 * HEAD
        keys = qkv_ref[:, width + lo : width + lo + 2 * HEAD]
        values = qkv_ref[:, 2 * width + lo : 2 * width + lo + 2 * HEAD]
        keys_t = keys.astype(F32).T.astype(BF)
        key_acc[...] = jnp.zeros_like(key_acc)
        value_acc[...] = jnp.zeros_like(value_acc)
        for start in range(0, tokens, block):
            queries = (qkv_ref[start : start + block, lo : lo + 2 * HEAD] * scale).astype(BF)
            grads = grad_ref[start : start + block, lo : lo + 2 * HEAD]
            same = col_ref[...] == row_ref[:, start : start + block]
            halves = []
            for half in range(2):
                lanes = head_lanes(queries.shape, half)
                own_queries = jnp.where(lanes, queries, jnp.zeros_like(queries))
                own_grads = jnp.where(lanes, grads, jnp.zeros_like(grads))
                head = 2 * pair + half
                top = max_ref[head : head + 1, start : start + block]
                total = sum_ref[head : head + 1, start : start + block]
                scores = dot(keys, own_queries, 1, 1)
                scores = jnp.where(same, scores, NEGATIVE)
                probs = jnp.exp(scores - top) * (1.0 / total)
                grad_probs = dot(values, own_grads, 1, 1)
                shared = jnp.sum(probs * grad_probs, axis=0, keepdims=True)
                grad_scores = (probs * (grad_probs - shared)).astype(BF)
                value_acc[...] += dot(probs.astype(BF), own_grads)
                key_acc[...] += dot(grad_scores, own_queries)
                mixed = dot(keys_t, grad_scores)
                halves.append(mixed[half * HEAD : (half + 1) * HEAD])
            joined = jnp.concatenate(halves, axis=0) * scale
            out_ref[start : start + block, lo : lo + 2 * HEAD] = joined.T.astype(BF)
        out_ref[:, width + lo : width + lo + 2 * HEAD] = key_acc[...].astype(BF)
        out_ref[:, 2 * width + lo : 2 * width + lo + 2 * HEAD] = value_acc[...].astype(BF)


def attend(qkv, starts):
    tokens, width = qkv.shape[0], qkv.shape[1] // 3
    heads = width // HEAD
    whole = pl.BlockSpec(memory_space=pltpu.VMEM)
    return pl.pallas_call(
        functools.partial(attend_kernel, math.gcd(tokens, 768)),
        out_shape=(
            jax.ShapeDtypeStruct((tokens, width), BF),
            jax.ShapeDtypeStruct((heads, tokens), F32),
            jax.ShapeDtypeStruct((heads, tokens), F32),
        ),
        in_specs=[whole] * 3,
        out_specs=(whole,) * 3,
        compiler_params=pltpu.CompilerParams(vmem_limit_bytes=VMEM_LIMIT),
        cost_estimate=pl.CostEstimate(
            flops=40 * tokens * tokens * width, bytes_accessed=16 * tokens * width, transcendentals=0
        ),
    )(qkv, starts[:, None], starts[None, :])


def attend_back(qkv, starts, row_max, row_sum, grads):
    tokens, width = grads.shape
    whole = pl.BlockSpec(memory_space=pltpu.VMEM)
    return pl.pallas_call(
        functools.partial(attend_back_kernel, math.gcd(tokens, 768)),
        out_shape=jax.ShapeDtypeStruct((tokens, 3 * width), BF),
        in_specs=[whole] * 6,
        out_specs=whole,
        scratch_shapes=[
            pltpu.VMEM((tokens, 2 * HEAD), F32),
            pltpu.VMEM((tokens, 2 * HEAD), F32),
        ],
        compiler_params=pltpu.CompilerParams(vmem_limit_bytes=VMEM_LIMIT),
        cost_estimate=pl.CostEstimate(
            flops=40 * tokens * tokens * width, bytes_accessed=16 * tokens * width, transcendentals=0
        ),
    )(qkv, starts[:, None], starts[None, :], row_max, row_sum, grads)


def place_rows(order, sizes, pieces, outs):
    me = lax.axis_index("dp")
    for steps, piece in zip(order, pieces):
        first = 0
        for step in steps:
            if isinstance(step, tuple):
                where = step[0] * 2 + (lax.rem(me, 2) ^ step[1])
            else:
                where = me ^ step
            for member, rows in enumerate(sizes):
                at = pl.multiple_of(where * rows, rows)
                outs[member][pl.ds(at, rows), :] = piece[first : first + rows, :]
                first += rows


def place_kernel(order, sizes, *refs):
    place_rows(order, sizes, refs[: len(order)], refs[len(order) :])


def place_first_kernel(order, sizes, pairs, layers, *refs):
    pieces, (weights, smalls, full, heads, inner) = refs[: len(order)], refs[len(order) :]
    place_rows(order, sizes, pieces, (weights, smalls))
    seq, n_seq = lax.axis_index("seq"), 4
    n_dp = smalls.shape[0] // 16
    lane = lax.broadcasted_iota(jnp.int32, (4, 128), 1)
    for dp in range(n_dp):
        rows = smalls[dp * 16 : dp * 16 + 16, :].astype(F32)
        for block in range(6):
            part = rows[:, block * 128 : block * 128 + 128]
            total = part[:4]
            for s in range(1, n_seq):
                moved = pltpu.roll(part, 32 * s, 1)[4 * s : 4 * s + 4]
                total = jnp.where(lane // 32 == s, moved, total)
            full[block, 0:4, dp * 128 : dp * 128 + 128] = total
            if block == 2:
                own = part[:4]
                for s in range(1, n_seq):
                    own = jnp.where(seq == s, part[4 * s : 4 * s + 4], own)
                inner[0:layers, dp * 128 : dp * 128 + 128] = own[layers : 2 * layers]
    heads[...] = jnp.zeros_like(heads)
    width = pairs * 128
    for which, base in ((0, 0), (1, 2 * width)):
        for pair in range(pairs):
            column = pl.multiple_of((pair * n_seq + seq) * 128, 128)
            heads[0:layers, base + pair * 128 : base + pair * 128 + 128] = full[
                which, 0:layers, pl.ds(column, 128)
            ]


def place(pieces, order, sizes, unpack=None, missing=0):
    columns = pieces[0].shape[1]
    order = tuple(tuple(o) if isinstance(o, (list, tuple)) else (o,) for o in order)
    count = sum(len(o) for o in order) + missing
    whole = pl.BlockSpec(memory_space=pltpu.VMEM)
    shapes = [jax.ShapeDtypeStruct((count * rows, columns), BF) for rows in sizes]
    body = functools.partial(place_kernel, order, tuple(sizes))
    if unpack is not None:
        pairs, layers, dim, inner = unpack
        shapes += [
            jax.ShapeDtypeStruct((6, 8, dim), F32),
            jax.ShapeDtypeStruct((8, pairs * 3 * 128), F32),
            jax.ShapeDtypeStruct((8, inner), F32),
        ]
        body = functools.partial(place_first_kernel, order, tuple(sizes), pairs, layers)
    return pl.pallas_call(
        body,
        out_shape=tuple(shapes),
        in_specs=[whole] * len(pieces),
        out_specs=(whole,) * len(shapes),
        compiler_params=pltpu.CompilerParams(vmem_limit_bytes=VMEM_LIMIT),
        cost_estimate=pl.CostEstimate(flops=0, bytes_accessed=0, transcendentals=0),
    )(*pieces)


def place_more_kernel(order, rows, buffer, piece, out, sem):
    me = lax.axis_index("dp")
    copies = []
    for i, step in enumerate(order):
        at = pl.multiple_of((me ^ step) * rows, rows)
        copies.append(
            pltpu.make_async_copy(
                piece.at[pl.ds(i * rows, rows)], out.at[pl.ds(at, rows)], sem.at[i]
            )
        )
    for copy in copies:
        copy.start()
    for copy in copies:
        copy.wait()


def place_more(buffer, piece, order):
    anywhere = pl.BlockSpec(memory_space=pl.ANY)
    return pl.pallas_call(
        functools.partial(place_more_kernel, tuple(order), piece.shape[0] // len(order)),
        out_shape=jax.ShapeDtypeStruct(buffer.shape, buffer.dtype),
        in_specs=[anywhere, pl.BlockSpec(memory_space=pltpu.VMEM)],
        out_specs=anywhere,
        scratch_shapes=[pltpu.SemaphoreType.DMA((len(order),))],
        input_output_aliases={0: 0},
        compiler_params=pltpu.CompilerParams(vmem_limit_bytes=VMEM_LIMIT),
        cost_estimate=pl.CostEstimate(flops=0, bytes_accessed=0, transcendentals=0),
    )(buffer, piece)


def split_kernel(n_seq, plan, part, smalls, *refs):
    n_in = 1 + max(p[0] for p in plan)
    weights, rest = refs[:n_in], refs[n_in:]
    small_refs, rest = rest[:smalls], rest[smalls:]
    outs = rest[:n_seq]
    seq = lax.axis_index("seq")
    if smalls:
        table = rest[n_seq]
        table[...] = jnp.zeros_like(table)
        across = table.shape[1] // 128
        for j, small in enumerate(small_refs):
            row, lane = 2 * (j // across), 128 * (j % across)
            table[row : row + 2, lane : lane + small.shape[1]] = small[...].astype(F32)
    for step in range(n_seq):
        target = seq ^ step
        at = 0
        for ref, layer, block, count in plan:
            if not count:
                outs[step][:part, at : at + block] = weights[ref][layer]
                at += block
            for i in range(count):
                column = pl.multiple_of((i * n_seq + target) * block, 128)
                outs[step][:part, at : at + block] = weights[ref][layer, :, pl.ds(column, block)]
                at += block
        if smalls:
            outs[step][part:, :] = table[...].astype(BF)


def split_weights(weights, plan, n_seq, smalls=()):
    part = weights[0].shape[1]
    columns = sum(block * max(count, 1) for _, _, block, count in plan)
    rows = part + (16 if smalls else 0)
    whole = pl.BlockSpec(memory_space=pltpu.VMEM)
    return pl.pallas_call(
        functools.partial(split_kernel, n_seq, tuple(plan), part, len(smalls)),
        out_shape=tuple(jax.ShapeDtypeStruct((rows, columns), BF) for _ in range(n_seq)),
        in_specs=[whole] * (len(weights) + len(smalls)),
        out_specs=(whole,) * n_seq,
        scratch_shapes=[pltpu.VMEM((16, columns), F32)] if smalls else [],
        compiler_params=pltpu.CompilerParams(vmem_limit_bytes=VMEM_LIMIT),
    )(*weights, *smalls)


def join_kernel(n_seq, part, cuts, with_small, extra, *refs):
    pieces, rest = refs[:n_seq], refs[n_seq:]
    if extra:
        extra_ref, rest = rest[0], rest[1:]
    outs = rest[: len(cuts)]
    seq = lax.axis_index("seq")
    for step in range(n_seq):
        row = pl.multiple_of((seq ^ step) * part, part)
        at = 0
        for out, columns in zip(outs, cuts):
            out[pl.ds(row, part), :] = pieces[step][:part, at : at + columns]
            at += columns
    if with_small:
        table = rest[len(cuts)]
        smalls = [pieces[step][part:, :].astype(F32)[:4] for step in range(n_seq)]
        for origin in range(n_seq):
            total = jnp.zeros_like(smalls[0])
            for step in range(n_seq):
                total = jnp.where((seq ^ step) == origin, smalls[step], total)
            table[4 * origin : 4 * origin + 4, :] = total
        outs[0][n_seq * part :, :] = table[...].astype(BF)
    if extra:
        outs[0][n_seq * part :, :] = extra_ref[0]


def join_pieces(pieces, part, cuts, with_small=False, extra=None):
    n_seq = len(pieces)
    rows = [n_seq * part] * len(cuts)
    if with_small:
        rows[0] += 4 * n_seq
    if extra is not None:
        rows[0] += extra.shape[1]
    whole = pl.BlockSpec(memory_space=pltpu.VMEM)
    more = [] if extra is None else [extra]
    return pl.pallas_call(
        functools.partial(
            join_kernel, n_seq, part, tuple(cuts), with_small, extra is not None
        ),
        out_shape=tuple(jax.ShapeDtypeStruct((r, c), BF) for r, c in zip(rows, cuts)),
        in_specs=[whole] * (n_seq + len(more)),
        out_specs=(whole,) * len(cuts),
        scratch_shapes=[pltpu.VMEM((4 * n_seq, cuts[0]), F32)] if with_small else [],
        compiler_params=pltpu.CompilerParams(vmem_limit_bytes=VMEM_LIMIT),
    )(*pieces, *more)


def after(array, *others):
    return lax.optimization_barrier((array,) + others)[0] if others else array


def solution(mesh):
    n_dp, n_seq = mesh.shape["dp"], mesh.shape["seq"]
    n_dev = n_dp * n_seq
    special = (n_dp, n_seq) == (8, 4)

    def swap(array, bit):
        return lax.ppermute(array, AXES, [(p, p ^ bit) for p in range(n_dev)])

    def bits_of(count, unit=1):
        bits = []
        while count > 1:
            bits.append(unit)
            unit, count = unit * 2, count // 2
        return bits

    seq_bits, dp_bits = bits_of(n_seq), bits_of(n_dp, n_seq)

    z_lines = [[d for d in range(n_dp) if d % 2 == y] for y in range(2)]

    x_steps = [0]
    for bit in reversed(seq_bits[1:]):
        x_steps = x_steps + [s ^ bit for s in x_steps]
    seq_steps = [step ^ core for step in x_steps for core in (0, 1)]

    def spread(piece, bits):
        pieces, steps = [piece], [0]
        for bit in reversed(bits):
            pieces = pieces + [swap(p, bit) for p in pieces]
            steps = steps + [s ^ bit for s in steps]
        return pieces, steps

    def launch(moves, gate):
        return [
            (home, name, swap(after(array, gate), bit) if bit else array)
            for home, name, array, bit in moves
        ]

    def settle(array, moving):
        if not moving:
            return array
        arrays = tuple(array) if isinstance(array, (tuple, list)) else (array,)
        out = lax.optimization_barrier(arrays + tuple(m[2] for m in moving))
        for (home, name, _), value in zip(moving, out[len(arrays) :]):
            setattr(home, name, value)
        return list(out[: len(arrays)]) if isinstance(array, (tuple, list)) else out[0]

    def gather_seq(rows, moves=(), gate=None):
        moving = launch(moves, rows if gate is None else gate)
        pieces = [rows]
        for bit in reversed(seq_bits[1:]):
            came = [swap(p, bit) for p in pieces]
            came[0] = settle(came[0], moving)
            moving = []
            pieces = pieces + came
        pairs = [jnp.concatenate([p, swap(p, 1)], axis=0) for p in pieces]
        return pairs[0], (jnp.concatenate(pairs[1:], axis=0) if len(pairs) > 2 else pairs[1])

    def both(halves):
        return jnp.concatenate(halves, axis=0)

    def reduce_seq(left, right, moves=(), gate=None, marks=None):
        near, far = left
        moving = launch(moves, far if gate is None else gate)
        size = near.shape[0] // 2

        def chip(rows, own):
            parts = right(rows, own) if callable(right) else dot(rows, right[0], *right[1])
            return parts[:size] + swap(parts[size:].astype(BF), 1).astype(F32)

        total = [None] + [
            chip(far[i * 2 * size : (i + 1) * 2 * size], False) for i in range(len(x_steps) - 1)
        ]
        if marks is not None:
            marks.append(total[-1])
        for i, bit in enumerate(seq_bits[1:]):
            middle = len(total) // 2
            got = [swap(t.astype(BF), bit) for t in total[middle:]]
            if i + 2 == len(seq_bits):
                got[0] = settle(got[0], moving)
            if total[0] is None:
                total[0] = chip(near, True)
            total = [a + b.astype(F32) for a, b in zip(total[:middle], got)]
        return total[0]

    def halve(array, index_bit, bit):
        chosen = index_bit.astype(jnp.bool_)
        send = jnp.where(chosen, array[0], array[1])
        keep = jnp.where(chosen, array[1], array[0])
        return keep, swap(send, bit)

    def local(
        tokens, doc_start, lexical_ids, queries, match_index,
        query_weight, query_bias, key_weight, value_weight, value_bias,
        out_weight, out_bias, norm_gain, norm_bias, expand_weight, expand_bias,
        shrink_weight, shrink_bias, final_gain, final_bias,
        lexical_weight, lexical_bias, score_cot, encoded_cot,
    ):
        layers, part, dim = query_weight.shape
        hidden_dim = expand_weight.shape[2]
        hidden_part = shrink_weight.shape[1]
        rows_here = tokens.shape[0]
        pairs_here = dim // (2 * HEAD) // n_seq
        width = pairs_here * 2 * HEAD
        own_hidden = hidden_dim // n_seq
        block_rows = dim // n_dp
        dp, seq = lax.axis_index("dp"), lax.axis_index("seq")
        flat = dp * n_seq + seq

        def bit_of(index, bit):
            return lax.bitwise_and(lax.div(index, bit), 1)

        def by_origin(pieces):
            for bit in seq_bits:
                chosen = bit_of(seq, bit).astype(jnp.bool_)
                pieces = [jnp.where(chosen, pieces[j ^ bit], pieces[j]) for j in range(n_seq)]
            return pieces

        def exchange_steps(blocks):
            pieces = by_origin(blocks)
            return [pieces[0]] + [swap(pieces[step], step) for step in range(1, n_seq)]

        def exchange_seq(blocks):
            return by_origin(exchange_steps(blocks))

        def head_split(weight):
            cut = [weight[:, i * 2 * HEAD : (i + 1) * 2 * HEAD] for i in range(pairs_here * n_seq)]
            return [cut[s::n_seq] for s in range(n_seq)]

        def hidden_split(weight):
            cut = [
                weight[:, i * hidden_part : (i + 1) * hidden_part] for i in range(n_dp * n_seq)
            ]
            return [cut[s::n_seq] for s in range(n_seq)]

        def qkv_split(layer):
            three = [head_split(w[layer]) for w in (query_weight, key_weight, value_weight)]
            return [jnp.concatenate(three[0][s] + three[1][s] + three[2][s], axis=1) for s in range(n_seq)]

        small_full = (
            query_bias, value_bias, out_bias, norm_gain, norm_bias, shrink_bias, final_gain, final_bias,
        )
        three = [query_weight, key_weight, value_weight]
        hidden_now = tokens.astype(F32)
        if special:
            heads_plan = [(i, 0, 2 * HEAD, pairs_here) for i in range(3)]
            sent = split_weights(three, heads_plan, n_seq, small_full + (expand_bias,))
            got = [sent[0]] + [swap(sent[step], step) for step in range(1, n_seq)]
            (shard,) = join_pieces(got, part, (3 * width,), True)
            class Stream:
                def __init__(self, shard):
                    self.shard = shard

                def far(self):
                    return [(self, "came", self.shard, n_seq * 4)]

                def middle(self):
                    self.line = jnp.concatenate([self.shard, self.came], axis=0)
                    return [
                        (self, "near", self.line, n_seq * 2),
                        (self, "y_line", self.line, n_seq),
                    ]

                def last(self):
                    return [(self, "y_near", self.near, n_seq)]

                def open(self, rows):
                    pieces = [self.line, self.near, self.y_line]
                    opened = place(pieces, [[0, 4], [2, 6], [1, 5]], (rows,), missing=2)[0]
                    return [(self, "opened", opened, 0)]

                def closed(self):
                    return place_more(self.opened, self.y_near, (3, 7))

                def ready(self, sizes):
                    return [(self, "full", self.whole(sizes)[0], 0)]

                def whole(self, sizes, unpack=None):
                    pieces = [self.line, self.near, self.y_line, self.y_near]
                    return place(pieces, [[0, 4], [2, 6], [1, 5], [3, 7]], sizes, unpack)

            first_stream = Stream(shard)
            plan = [(3, 0, hidden_part, n_dp)]
            cuts = [own_hidden]
            for layer in range(1, layers):
                plan += [(i, layer, 2 * HEAD, pairs_here) for i in range(3)]
                plan += [(3, layer, hidden_part, n_dp)]
                cuts += [3 * width, own_hidden]
            plan += [(4, layer, dim, 0) for layer in range(layers)]
            cuts += [dim] * layers
            sent = split_weights(three + [expand_weight, out_weight], plan, n_seq)
            sent = [after(p, got[1], got[2], got[3]) for p in sent]
            got = [sent[0]] + [swap(sent[step], step) for step in range(1, n_seq)]
            second = join_pieces(got, part, cuts)
            group = both(gather_seq(after(tokens, *got[2:])))

            class OutRows:
                def __init__(self, rows):
                    self.rows, self.moved, self.bit = rows, None, 0

                def take(self):
                    bit, moved = self.bit, self.moved
                    if bit in (1, 2):
                        here = bit_of(seq, bit) == bit_of(dp, bit)
                        self.rows = jnp.where(here, self.rows, moved)
                    elif bit == 4:
                        upper = bit_of(dp, 4) == 1
                        self.rows = jnp.concatenate(
                            [jnp.where(upper, moved, self.rows), jnp.where(upper, self.rows, moved)],
                            axis=0,
                        )
                    self.bit = 0
                    self.rows = lax.optimization_barrier(self.rows)
                    return self.rows

                def step(self, bit):
                    rows = self.take()
                    self.bit = bit
                    return [(self, "moved", rows, n_seq * bit)]

            outs = [OutRows(second[2 * layers - 1 + i]) for i in range(layers)]
            streams = [
                Stream(x)
                for x in (second[0], shrink_weight[0], second[1], second[2], shrink_weight[1])
            ]
            expand_0, shrink_0, qkv_1, expand_1, shrink_1 = streams
            shard = settle(shard, launch(first_stream.far(), shard))
            moving = launch(first_stream.middle(), first_stream.came)
            out_y = launch(outs[0].step(1), first_stream.came)
            shard = settle(shard, moving[:1])
            moving = moving[1:] + launch(first_stream.last() + expand_0.far(), first_stream.near)
            shard = settle(shard, out_y)
            moving += launch(outs[0].step(2), outs[0].moved)
            group = settle(group, moving)
            qkv_first, _, small_full, small_heads, small_inner = first_stream.whole(
                (block_rows, 16), (pairs_here, layers, dim, own_hidden)
            )
            head_bias, hidden_bias = small_heads[:layers], small_inner[:layers]

            def vector_of(layer, j):
                return small_full[j % 6, layers * (j // 6) + layer]

        else:
            small = lax.all_gather(
                jnp.concatenate(list(small_full) + [expand_bias], axis=1), AXES, axis=0, tiled=False
            )
            full = small[:, :, : 8 * part].reshape(n_dev, layers, 8, part).transpose(1, 2, 0, 3)
            hidden_bias = small[:, :, 8 * part :].transpose(1, 0, 2)
            group = both(gather_seq(tokens))
            full = full.reshape(layers, 8, dim).astype(F32)
            by_column = full[:, :2].reshape(layers, 2, pairs_here, n_seq, 2 * HEAD)
            by_column = lax.dynamic_index_in_dim(by_column, seq, 3, keepdims=False)
            by_column = by_column.reshape(layers, 2, width)
            head_bias = jnp.concatenate(
                [by_column[:, 0], jnp.zeros((layers, width), F32), by_column[:, 1]], axis=1
            )
            hidden_bias = hidden_bias.reshape(layers, n_dp, n_seq, hidden_part)
            hidden_bias = lax.dynamic_index_in_dim(hidden_bias, seq, 2, keepdims=False)
            hidden_bias = hidden_bias.reshape(layers, own_hidden).astype(F32)

            def vector_of(layer, j):
                return full[layer, j]

        if special:
            out_all = []
        else:
            whole_out = lax.all_gather(out_weight, AXES, axis=1, tiled=True)
            cut = whole_out.reshape(layers, pairs_here, n_seq, 2 * HEAD, dim)
            cut = lax.dynamic_index_in_dim(cut, seq, 2, keepdims=False)
            out_all = [cut[layer].reshape(width, dim) for layer in range(layers)]

        if special:
            qkv_all, expand_all, shrink_all = [qkv_first], [], []

            def beside_of(layer, point):
                if (layer, point) == (0, "attend"):
                    return outs[0].step(4) + expand_0.middle()
                if (layer, point) == (0, "out"):
                    out_all.append(outs[0].take())
                    return shrink_0.far() + expand_0.last() + outs[1].step(1)
                if (layer, point) == (0, "normed"):
                    return shrink_0.middle() + expand_0.ready((block_rows,))
                if (layer, point) == (0, "active"):
                    expand_all.append(expand_0.full)
                    return shrink_0.last() + qkv_1.far() + outs[1].step(2) + shrink_0.open(hidden_part)
                if (layer, point) == (0, "shrink"):
                    shrink_all.append(shrink_0.closed())
                    return qkv_1.middle() + outs[1].step(4)
                if (layer, point) == (1, "group"):
                    return expand_1.far() + qkv_1.last()
                if (layer, point) == (1, "attend"):
                    qkv_all.append(qkv_1.whole((block_rows,))[0])
                    return expand_1.middle()
                if (layer, point) == (1, "out"):
                    out_all.append(outs[1].take())
                    return shrink_1.far() + expand_1.last()
                if (layer, point) == (1, "normed"):
                    return shrink_1.middle() + expand_1.ready((block_rows,))
                if (layer, point) == (1, "active"):
                    expand_all.append(expand_1.full)
                    return shrink_1.last() + shrink_1.open(hidden_part)
                if (layer, point) == (1, "shrink"):
                    shrink_all.append(shrink_1.closed())
                return []
        else:
            qkv_all, expand_all, shrink_all = [], [], []

            def beside_of(layer, point):
                return []

            for layer in range(layers):
                mine = exchange_seq(qkv_split(layer))
                mine = lax.all_gather(jnp.concatenate(mine, axis=0), "dp", axis=0, tiled=True)
                qkv_all.append(mine)
                mine = [jnp.concatenate(b, axis=1) for b in hidden_split(expand_weight[layer])]
                mine = jnp.concatenate(exchange_seq(mine), axis=0)
                expand_all.append(lax.all_gather(mine, "dp", axis=0, tiled=True))
                shrink_all.append(lax.all_gather(shrink_weight[layer], "dp", axis=0, tiled=True))

        starts_here = doc_start[0].reshape(n_seq, rows_here)
        starts = jnp.concatenate(
            [
                lax.dynamic_index_in_dim(starts_here, seq ^ step, 0, keepdims=False)
                for step in seq_steps
            ]
        )

        def norm_parts(resid):
            center = resid - jnp.mean(resid, axis=-1, keepdims=True)
            inverse = lax.rsqrt(jnp.mean(center * center, axis=-1, keepdims=True) + EPSILON)
            return center * inverse, inverse

        def norm_back(upstream, gain, rhat, inverse):
            scaled = upstream * gain
            mean_one = jnp.mean(scaled, axis=-1, keepdims=True)
            mean_two = jnp.mean(scaled * rhat, axis=-1, keepdims=True)
            grad = (scaled - mean_one - rhat * mean_two) * inverse
            return grad, jnp.sum(upstream * rhat, axis=0), jnp.sum(upstream, axis=0)

        def column_sums(matrix):
            return jnp.sum(matrix.astype(F32), axis=0)

        kept = []
        for layer in range(layers):
            _, _, out_b, gain_one, bias_one, shrink_b, gain_two, bias_two = (
                vector_of(layer, i) for i in range(8)
            )
            if layer:
                group = both(gather_seq(hidden_now.astype(BF), beside_of(layer, "group"), summed))
            moving = launch(beside_of(layer, "attend"), group)
            qkv = (dot(group, qkv_all[layer]) + head_bias[layer]).astype(BF)
            attended, row_max, row_sum = attend(qkv, starts)
            attended = settle(attended, moving)
            moves = beside_of(layer, "out")
            chip_rows = 2 * rows_here
            halves = (attended[:chip_rows], attended[chip_rows:])
            summed = reduce_seq(halves, (out_all[layer], (1, 0)), moves)
            resid_one = hidden_now + (summed + out_b)
            rhat_one, inverse_one = norm_parts(resid_one)
            normed = rhat_one * gain_one + bias_one
            normed_halves = gather_seq(normed.astype(BF), beside_of(layer, "normed"), summed)
            moves = beside_of(layer, "active")
            moving = launch(moves, moves[0][2] if moves else normed_halves[1])
            active, slope = [], []
            for rows in normed_halves:
                inner = dot(rows, expand_all[layer]) + hidden_bias[layer]
                cdf = 0.5 * (1.0 + lax.erf(inner * math.sqrt(0.5)))
                active.append((inner * cdf).astype(BF))
                slope.append(
                    cdf + inner * jnp.exp(-0.5 * inner * inner) * (1.0 / math.sqrt(2 * math.pi))
                )
            active = settle(active, moving)
            moves = beside_of(layer, "shrink")
            summed = reduce_seq(active, (shrink_all[layer], (1, 0)), moves)
            normed_group, active = both(normed_halves), both(active)
            resid_two = normed + (summed + shrink_b)
            rhat_two, inverse_two = norm_parts(resid_two)
            hidden_now = rhat_two * gain_two + bias_two
            kept.append(
                (group, qkv, attended, row_max, row_sum, rhat_one, inverse_one, normed_group,
                 active, slope, rhat_two, inverse_two)
            )
        encoded = hidden_now.astype(BF)

        local_index = match_index[0] - seq * rows_here
        picker = local_index[:, None] == jnp.arange(rows_here, dtype=jnp.int32)[None, :]
        chosen = dot(picker.astype(BF), encoded)
        query_vecs = queries[0].astype(F32)
        scores = jnp.sum(query_vecs * chosen, axis=-1)[None, :]
        lexical = jnp.sum(
            encoded.astype(F32) * lexical_weight.astype(F32)[None, :], axis=-1
        ) + lexical_bias.astype(F32)[0]
        keep_mask = (lexical_ids >= 4).astype(F32)
        local_sums = jnp.stack(
            [
                jnp.sum(keep_mask * jax.nn.softplus(lexical)),
                jnp.sum(keep_mask * jax.nn.sigmoid(lexical)),
            ]
        )
        weighted = score_cot[0][:, None] * query_vecs
        grad_now = encoded_cot.astype(F32) + lax.dot_general(
            picker.astype(F32), weighted, (((0,), (0,)), ((), ())), precision=HIGHEST
        )

        def scatter_dp(grad):
            return lax.psum_scatter(grad, "dp", scatter_dimension=0, tiled=True)

        class Sums:
            def __init__(self, grads, rows=block_rows):
                self.blocks = [g.reshape(2, 2, 2, rows, g.shape[-1]) for g in grads]

            def first(self):
                low, up = bit_of(dp, 2) == 1, bit_of(dp, 1) == 1

                def of(flip_low, flip_up):
                    parts = []
                    for b in self.blocks:
                        b = jnp.where(low ^ flip_low, b[:, 1], b[:, 0])
                        parts.append(jnp.where(up ^ flip_up, b[:, 1], b[:, 0]))
                    return jnp.concatenate(parts, axis=-1)

                self.of = of
                self.keep = of(True, False)
                return [(self, "came", of(True, True), n_seq)]

            def middle_z(self):
                total = (self.keep.astype(F32) + self.came.astype(F32)).astype(BF)
                return [(self, "near", total, 2 * n_seq)]

            def middle_y(self):
                self.keep = self.of(False, False)
                return [(self, "came", self.of(False, True), n_seq)]

            def middle(self):
                return self.middle_z() + self.middle_y()

            def last(self):
                total = (
                    self.keep.astype(F32) + self.came.astype(F32) + self.near.astype(F32)
                ).astype(BF)
                high = bit_of(dp, 4) == 1
                self.keep = jnp.where(high, total[1], total[0])
                return [(self, "came", jnp.where(high, total[0], total[1]), 4 * n_seq)]

            def rows(self):
                return self.keep.astype(F32) + self.came.astype(F32)

        def scatter_out(grad):
            if not special:
                placed = grad.reshape(pairs_here, 1, 2 * HEAD, dim)
                hot = (jnp.arange(n_seq) == seq)[None, :, None, None]
                placed = jnp.where(hot, placed, jnp.zeros_like(placed)).reshape(dim, dim)
                return lax.psum_scatter(placed, AXES, scatter_dimension=0, tiled=True)
            return None

        def unsplit(pieces, size):
            count = pieces[0].shape[1] // size
            return jnp.concatenate(
                [pieces[s][:, i * size : (i + 1) * size] for i in range(count) for s in range(n_seq)],
                axis=1,
            )

        class Grads:
            pass

        class Back:
            def __init__(self, blocks):
                pieces = by_origin(blocks)
                self.step_0, self.pieces = pieces[0], pieces

            def moves(self):
                return [(self, "step_%d" % i, self.pieces[i], i) for i in range(1, n_seq)]

            def got(self):
                return [getattr(self, "step_%d" % i) for i in range(n_seq)]

        class Table:
            def __init__(self, rows, more):
                self.keep, self.more = rows, more
                self.bits = [4 * n_seq, 2 * n_seq, n_seq]

            def take(self):
                if hasattr(self, "came"):
                    self.keep = self.keep + self.came

            def step(self):
                self.take()
                bit = self.bits.pop(0)
                middle = self.keep.shape[1] // 2
                low, up = self.keep[:, :middle], self.keep[:, middle:]
                chosen = bit_of(dp, bit // n_seq) == 1
                self.keep = jnp.where(chosen, up, low)
                return [(self, "came", jnp.where(chosen, low, up), bit)]

            def group_step(self):
                self.take()
                more = jnp.pad(self.more, ((0, 0), (0, self.keep.shape[1] - self.more.shape[1])))
                self.keep = jnp.concatenate([self.keep, more], axis=0)
                return [(self, "came_%d" % i, self.keep, i) for i in range(1, n_seq)]

            def whole(self):
                rest = [getattr(self, "came_%d" % i) for i in range(1, n_seq)]
                return sum(by_origin([self.keep] + rest))

        def rows_back(scattered):
            return exchange_steps([scattered[s * part : (s + 1) * part] for s in range(n_seq)])

        def columns_row(vector):
            hot = (jnp.arange(n_seq) == seq)[None, :, None]
            return jnp.where(hot, vector.reshape(pairs_here, 1, 2 * HEAD), 0.0).reshape(1, dim)

        def hidden_rows(vector):
            hot = (jnp.arange(n_seq) == seq)[:, None]
            return jnp.where(hot, vector[None, :], 0.0)

        def reduce_rows(rows, extra=None):
            unit = n_dp
            while unit > 1:
                unit //= 2
                middle = rows.shape[1] // 2
                keep, got = halve(
                    (rows[:, :middle], rows[:, middle:]), bit_of(dp, unit), unit * n_seq
                )
                rows = keep + got
            if extra is not None:
                extra = jnp.pad(extra, ((0, 0), (0, rows.shape[1] - extra.shape[1])))
                rows = jnp.concatenate([rows, extra], axis=0)
            for bit in seq_bits:
                rows = rows + swap(rows, bit)
            return rows

        def own_part(row):
            return lax.dynamic_slice_in_dim(row, seq * part, part)

        big = [None] * layers
        vectors, inner_vectors = [None] * layers, [None] * layers
        lex_row = jnp.zeros((1, n_dp, dim // n_dp), F32).at[0, :, :2].set(local_sums)
        lex_row = lex_row.reshape(1, dim)
        for layer in reversed(range(layers)):
            gain_one, gain_two = vector_of(layer, 3), vector_of(layer, 6)
            (group, qkv, attended, row_max, row_sum, rhat_one, inverse_one, normed_group,
             active, slope, rhat_two, inverse_two) = kept[layer]
            grad_second, fgain, fbias = norm_back(grad_now, gain_two, rhat_two, inverse_two)
            low_second = grad_second.astype(BF)

            def token_rows():
                return jnp.stack(
                    [column_sums(low_first), ngain, nbias, column_sums(low_second), fgain, fbias]
                )

            def layer_rows():
                vectors[0] = jnp.concatenate([token_rows()] + head_rows, axis=0)
                inner_vectors[0] = hidden_rows(inner_sums)
                return jnp.concatenate(vectors + [lex_row] + inner_vectors, axis=0)

            above = big[layer + 1] if special and layer + 1 < layers else None
            moves = above.expand.last() + above.qkv.first() if above else []
            halves = gather_seq(low_second, moves, grad_now)
            moving = launch(above.qkv.middle(), above.qkv.came) if above else []
            low_inner = [
                (dot(rows, shrink_all[layer], 1, 1) * slope[i]).astype(BF)
                for i, rows in enumerate(halves)
            ]
            low_inner[1] = settle(low_inner[1], moving)
            second_group = both(halves)
            inner_group = both(low_inner)
            shrink_grad = dot(active, second_group, 0, 0).astype(BF)
            moves, marks = [], []
            if special:
                big[layer] = mine = Grads()
                mine.shrink = Sums([shrink_grad])
                moves = (above.qkv.last() if above else []) + mine.shrink.first()
            summed = reduce_seq(low_inner, (expand_all[layer], (1, 1)), moves, None, marks)
            inner_group = after(inner_group, *marks)
            expand_grad = dot(normed_group, inner_group, 0, 0).astype(BF)
            if special:
                mine.expand = Sums([expand_grad])
            inner_sums = column_sums(inner_group)
            grad_normed = grad_second + summed
            grad_first, ngain, nbias = norm_back(grad_normed, gain_one, rhat_one, inverse_one)
            low_first = grad_first.astype(BF)
            if special:
                moves = mine.shrink.middle()
            first_group = both(gather_seq(low_first, moves, summed))
            if special:
                gate = mine.shrink.near
                moves = mine.shrink.last() + mine.expand.first()
                moving = launch(moves, gate)
            low_attn = dot(first_group, out_all[layer], 1, 1).astype(BF)
            out_grad = dot(attended, first_group, 0, 0).astype(BF)
            if special:
                quarter = dim // n_seq
                pieces = [out_grad[:, s * quarter : (s + 1) * quarter] for s in range(n_seq)]
                out_back = Back(pieces)
                moving += launch(out_back.moves(), first_group)
            grad_qkv = attend_back(qkv, starts, row_max, row_sum, low_attn)
            if special:
                grad_qkv = settle(grad_qkv, moving)

            def late_grads(grad_qkv):
                qkv_grad = dot(group, grad_qkv, 0, 0).astype(BF)
                if special:
                    pieces = out_back.got()
                    pieces = [p.reshape(pairs_here, 1, 2 * HEAD, quarter) for p in by_origin(pieces)]
                    out_columns = jnp.concatenate(pieces, axis=1).reshape(dim, quarter)
                    mine.qkv = Sums([qkv_grad, out_columns])
                return qkv_grad

            gate, moves, marks = grad_qkv, [], []
            if special and layer == 0:
                late_grads(grad_qkv)
                tail_moves = mine.qkv.first() + mine.expand.middle_z()
                tail_moving = launch(tail_moves, grad_qkv)
                grad_qkv = after(grad_qkv, tail_moves[0][2])
            elif special:
                moves = mine.expand.middle()
            left = (grad_qkv[:chip_rows], grad_qkv[chip_rows:])
            summed = reduce_seq(left, (qkv_all[layer], (1, 1)), moves, gate, marks)
            grad_qkv = after(grad_qkv, *marks)
            qkv_sums = column_sums(grad_qkv)
            if layer or not special:
                qkv_grad = late_grads(grad_qkv)
            head_rows = [columns_row(qkv_sums[:width]), columns_row(qkv_sums[2 * width :])]
            if special and layer == 0:
                table = Table(layer_rows(), scores)
                for home, name, array in launch(table.step(), marks[0]):
                    setattr(home, name, array)
            if not special:
                big[layer] = (
                    scatter_dp(shrink_grad),
                    scatter_dp(expand_grad),
                    scatter_out(out_grad),
                    scatter_dp(qkv_grad),
                )
            grad_now = grad_first + summed
            if layer or not special:
                vectors[layer] = jnp.concatenate([token_rows()] + head_rows, axis=0)
                inner_vectors[layer] = hidden_rows(inner_sums)

        tokens_grad = grad_now.astype(BF)

        counts = [v.shape[0] for v in vectors] + [1] + [n_seq] * layers

        def small_outs(table, inner_tables=None):
            cut = [0]
            for count in counts:
                cut.append(cut[-1] + count)
            tables = [table[cut[i] : cut[i + 1]] for i in range(len(counts))]
            inner_tables = inner_tables or tables[layers + 1 :]
            inner_out = jnp.stack(
                [lax.dynamic_index_in_dim(t, seq, 0, keepdims=False) for t in inner_tables]
            )
            scores = table[-1:, : queries.shape[1]]
            stats = tables[layers][0, :2] / (rows_here * n_dev)
            vector_outs = [
                jnp.stack([own_part(tables[i][row]) for i in range(layers)])
                for row in (6, 7, 0, 1, 2, 3, 4, 5)
            ]
            return [scores, stats, inner_out] + vector_outs

        def stacked(arrays):
            return jnp.stack([a.astype(F32) for a in arrays])

        def head_outs(gots):
            outs = [
                stacked(
                    [
                        unsplit([g[:, i * width : (i + 1) * width] for g in got], 2 * HEAD)
                        for got in gots
                    ]
                )
                for i in range(3)
            ]
            return outs + [
                stacked([jnp.concatenate([g[:, 3 * width :] for g in got], axis=1) for got in gots])
            ]

        if special:

            def back_of(grads):
                grads = [g.astype(BF) for g in grads]
                return Back(
                    [
                        jnp.concatenate([g[s * part : (s + 1) * part] for g in grads], axis=1)
                        for s in range(n_seq)
                    ]
                )

            low = big[0]
            gate = settle(marks[0], tail_moving)
            moves = low.qkv.middle()
            for home, name, array in launch(table.step(), gate):
                setattr(home, name, array)
            gate, tokens_grad = settle([gate, tokens_grad], launch(moves + table.step(), gate))
            moves = low.qkv.last() + low.expand.middle_y() + table.group_step()
            gate = settle(gate, launch(moves, gate))
            back = back_of([low.qkv.rows()] + [g.rows() for m in big[1:] for g in (m.expand, m.qkv)])
            moving = launch(low.expand.last(), gate)
            gate = settle(gate, launch(back.moves(), gate))
            got = by_origin(back.got())
            size = 3 * width + dim // n_seq
            gots, upper_expand = [[g[:, :size] for g in got]], []
            for layer in range(1, layers):
                at = size + (layer - 1) * (own_hidden + size)
                upper_expand.append(
                    unsplit([g[:, at : at + own_hidden] for g in got], hidden_part).astype(F32)
                )
                gots.append([g[:, at + own_hidden : at + own_hidden + size] for g in got])
            smalls = small_outs(table.whole())
            heads = head_outs(gots)
            shrink_out = stacked([m.shrink.rows() for m in big])
            ready = settle(smalls + heads + upper_expand + [shrink_out, gate], moving)
            smalls, heads = ready[:11], ready[11:15]
            upper_expand, shrink_out, gate = ready[15:-2], ready[-2], ready[-1]
            back = back_of([low.expand.rows()])
            settle(gate, launch(back.moves(), gate))
            expand_out = stacked([unsplit(by_origin(back.got()), hidden_part)] + upper_expand)
        else:
            table = reduce_rows(jnp.concatenate(vectors + [lex_row], axis=0), scores)
            inner = reduce_rows(jnp.concatenate(inner_vectors, axis=0))
            smalls = small_outs(table, [inner[i * n_seq : (i + 1) * n_seq] for i in range(layers)])
            gots = [by_origin(rows_back(b[3])) for b in big]
            gots = [[jnp.concatenate([g, g[:, :0]], axis=1) for g in got] for got in gots]
            heads = head_outs(gots)[:3] + [stacked([b[2] for b in big])]
            expand_out = stacked([unsplit(by_origin(rows_back(b[1])), hidden_part) for b in big])
            shrink_out = stacked([b[0] for b in big])
        scores, lexical_stats, inner_out = smalls[:3]
        vector_outs = smalls[3:]
        return (
            encoded, scores, lexical_stats, tokens_grad,
            heads[0], vector_outs[0], heads[1], heads[2], vector_outs[1],
            heads[3], vector_outs[2], vector_outs[3], vector_outs[4],
            expand_out, inner_out, shrink_out, vector_outs[5],
            vector_outs[6], vector_outs[7],
        )

    rows = P(AXES, None)
    weight = P(None, AXES, None)
    vector = P(None, AXES)
    placed = (
        rows, P("dp", None), P(AXES), P("dp", None, None), P("dp", None),
        weight, vector, weight, weight, vector, weight, vector, vector, vector,
        weight, vector, weight, vector, vector, vector, P(), P(), P("dp", None), rows,
    )
    results = (
        rows, P("dp", None), P(), rows,
        weight, vector, weight, weight, vector, weight, vector, vector, vector,
        weight, vector, weight, vector, vector, vector,
    )
    return jax.shard_map(local, mesh=mesh, in_specs=placed, out_specs=results, check_vma=False)
```
